32 devices in a mesh: depth: 4 (over y, x), freq: 8 (over z, core).
Axes of the slice: x: 2, y: 2, z: 4, core: 2. Of those that a mesh axis runs over, the one named last changes fastest.
Arguments:
- source: bfloat16 [8, 2, 1024, 256], P('freq'), may hold values from -6 to 6
- propagator: bfloat16 [4, 8, 2, 1024, 1024], P('depth', 'freq'), may hold values from -0.125 to 0.125
- transmission: float32 [4, 8, 1024], P('depth', 'freq'), may hold values from 0.5 to 1.5
- upgoing: bfloat16 [4, 8, 2, 1024, 256], P('depth', 'freq'), may hold values from -6 to 6
Outputs:
- gradient: float32 [4, 1024, 2, 1024], P('depth', 'freq')
The draws below stay inside these ranges and needn't reach their ends.
All inputs are finite; a program needn't handle non-finite values.
Results may differ from the reference program's by a relative error of at most 0.013.
Values may be sent and summed in bfloat16 or wider, within the bound.
No kernel may reach another device: no remote copies, remote signals or barrier semaphores. Data moves between devices by JAX's collectives and lax.ppermute only.
A program may use at most 64 MiB of HBM per device.

```python
import jax
import jax.numpy as jnp
from jax import lax

NX = 1024
SHOTS = 256
LEVELS = 4
FREQS = 8


def strengthened(values, rng, source, target, shards_of, factor):
    def block_of(axis_at):
        return (jnp.arange(values.shape[axis_at]) // (values.shape[axis_at] // shards_of)).reshape((-1,) + (1,) * (values.ndim - 1 - axis_at))

    first = jax.random.permutation(rng, shards_of)[block_of(target)]
    far = (block_of(target) + shards_of // 2) % shards_of
    return jnp.where((block_of(source) == first) | (block_of(source) == far), factor * values, values)


def level_of(own_key, shape, cuts, least, top_value):
    factor_of = 1.0
    for dim, parts in cuts:
        steps = jax.random.uniform(jax.random.fold_in(jax.random.fold_in(own_key, 6), dim), (parts,), jnp.float32, least / len(cuts), top_value / len(cuts))
        factor_of = factor_of * jnp.repeat(jnp.exp(steps), shape[dim] // parts).reshape((-1,) + (1,) * (len(shape) - 1 - dim))
    return factor_of


def gaussian(stream_key, extent, scale, bound, shards=(), kind=jnp.bfloat16):
    entries = jax.random.normal(stream_key, extent, jnp.float32) * scale
    if len(shards) > 0:
        entries = level_of(stream_key, extent, shards, -0.22, 0.18) * entries
    return jnp.clip(entries, min=-bound, max=bound).astype(kind)


def noise_with(stream_key, shape, scale, reach, shards, heavy, held_as=jnp.bfloat16):
    drawn = scale * jax.random.normal(stream_key, shape, jnp.float32)
    if shards:
        drawn = drawn * level_of(stream_key, shape, shards, -0.22, 0.18)
    return jnp.clip(strengthened(drawn, jax.random.fold_in(stream_key, 3), *heavy), -reach, reach).astype(held_as)


def setup_inputs(seed: int = 0) -> dict:
    splits = jax.random.split(jax.random.key(seed), 5)
    return {
        "source": gaussian(splits[0], (FREQS, 2, NX, SHOTS), 1.0, 6.0, ((0, 8),)),
        "propagator": gaussian(splits[1], (LEVELS, FREQS, 2, NX, NX), (2 * NX) ** -0.5, 0.125, ((0, 4), (1, 8))),
        "transmission": jnp.clip(1.0 + 0.1 * jax.random.normal(splits[2], (LEVELS, FREQS, NX), jnp.float32), 0.5, 1.5),
        "upgoing": noise_with(splits[3], (LEVELS, FREQS, 2, NX, SHOTS), 1.0, 6.0, ((0, 4), (1, 8)), (1, 3, 8, 2.0)),
    }


def advance(panel, weight, factor):
    shots = panel.shape[1] // 2
    real_part = jnp.dot(weight[0], panel, preferred_element_type=jnp.float32)
    imag_part = jnp.dot(weight[1], panel, preferred_element_type=jnp.float32)
    out_real = real_part[:, :shots] - imag_part[:, shots:]
    out_imag = real_part[:, shots:] + imag_part[:, :shots]
    joined = jnp.concatenate([out_real, out_imag], axis=1)
    return (joined * factor[:, None]).astype(jnp.bfloat16)


def correlate(upward, panel):
    up_pair = jnp.concatenate([upward[0], upward[1]], axis=1)
    up_turn = jnp.concatenate([upward[1], -upward[0]], axis=1)
    dims = (((1,), (1,)), ((), ()))
    real_part = lax.dot_general(up_pair, panel, dims, preferred_element_type=jnp.float32)
    imag_part = lax.dot_general(up_turn, panel, dims, preferred_element_type=jnp.float32)
    return jnp.stack([real_part, imag_part], axis=1)


def reference(source, propagator, transmission, upgoing):
    levels = propagator.shape[0]
    freqs = propagator.shape[1]
    width = propagator.shape[3]
    shots = source.shape[3]
    factor = (2.0 * shots * freqs) ** -0.5

    def one_freq(carry, index):
        panel = jnp.concatenate([source[index, 0], source[index, 1]], axis=1)
        outputs = []
        for level in range(levels):
            panel = advance(panel, propagator[level, index], transmission[level, index])
            outputs.append(carry[level] + correlate(upgoing[level, index], panel))
        return jnp.stack(outputs), None

    start = jnp.zeros((levels, width, 2, width), jnp.float32)
    total, _ = lax.scan(one_freq, start, jnp.arange(freqs, dtype=jnp.int32))
    return total * factor
```

```python
import jax
import jax.numpy as jnp
from jax import lax
from jax.sharding import PartitionSpec as P


def shifted(block, axis, distance):
    devices = range(lax.axis_size(axis))
    route = [(i - distance, i) for i in devices if i - distance in devices]
    return lax.ppermute(block, axis, route)


def advance(panel, weight, factor):
    shots = panel.shape[1] // 2
    real_part = jnp.dot(weight[0], panel, preferred_element_type=jnp.float32)
    imag_part = jnp.dot(weight[1], panel, preferred_element_type=jnp.float32)
    out_real = real_part[:, :shots] - imag_part[:, shots:]
    out_imag = real_part[:, shots:] + imag_part[:, :shots]
    joined = jnp.concatenate([out_real, out_imag], axis=1)
    return (joined * factor[:, None]).astype(jnp.bfloat16)


def shards(source, propagator, transmission, upgoing):
    weight = propagator[0, 0]
    factor = transmission[0, 0]
    upward = upgoing[0, 0]
    width = weight.shape[1]
    shots = source.shape[3]
    level = lax.axis_index("depth")
    levels = lax.axis_size("depth")
    freqs = lax.axis_size("freq")
    rows_own = width // freqs
    start_panel = jnp.concatenate([source[0, 0], source[0, 1]], axis=1)
    incoming = start_panel
    outgoing = advance(incoming, weight, factor)
    for tick in range(1, levels):
        arrived = shifted(outgoing, "depth", 1)
        incoming = jnp.where(level == 0, start_panel, arrived)
        outgoing = advance(incoming, weight, factor)
    up_pair = jnp.concatenate([upward[0], upward[1]], axis=1)
    dims = (((1,), (1,)), ((), ()))
    turned = jnp.concatenate([-outgoing[:, shots:], outgoing[:, :shots]], axis=1)
    both = jnp.concatenate([outgoing, turned], axis=0)
    term = lax.dot_general(up_pair, both, dims, preferred_element_type=jnp.float32)
    summed = lax.psum_scatter(
        term.astype(jnp.bfloat16), "freq", scatter_dimension=0, tiled=True
    )
    scale = (2.0 * shots * freqs) ** (-0.5)
    return (summed.astype(jnp.float32) * scale).reshape(1, rows_own, 2, width)


def solution(mesh):
    return jax.shard_map(
        shards,
        mesh=mesh,
        in_specs=(
            P("freq", None, None, None),
            P("depth", "freq", None, None, None),
            P("depth", "freq", None),
            P("depth", "freq", None, None, None),
        ),
        out_specs=P("depth", "freq", None, None),
        check_vma=False,
    )
```

```python
import jax
import jax.numpy as jnp
from jax import lax
from jax.sharding import PartitionSpec as P

CHUNKS = 4
DELAY = 2


def shifted(block, axis, distance):
    devices = range(lax.axis_size(axis))
    route = [(i - distance, i) for i in devices if i - distance in devices]
    return lax.ppermute(block, axis, route)


def advance(panel, weight, factor):
    shots = panel.shape[1] // 2
    turned = jnp.concatenate([-panel[:, shots:], panel[:, :shots]], axis=1)
    out = jnp.dot(weight[0], panel, preferred_element_type=jnp.float32) + jnp.dot(
        weight[1], turned, preferred_element_type=jnp.float32
    )
    return (out * factor[:, None]).astype(jnp.bfloat16)


def shards(source, propagator, transmission, upgoing):
    weight = propagator[0, 0]
    factor = transmission[0, 0]
    upward = upgoing[0, 0]
    width = weight.shape[1]
    shots = source.shape[3]
    level = lax.axis_index("depth")
    levels = lax.axis_size("depth")
    freqs = lax.axis_size("freq")
    rows_own = width // freqs
    part = shots // CHUNKS
    starts = [
        jnp.concatenate([source[0, 0, :, at : at + part], source[0, 1, :, at : at + part]], axis=1)
        for at in range(0, shots, part)
    ]
    first = lax.rem(DELAY * (levels - 1 - level), CHUNKS) * part
    rolled = lax.dynamic_slice_in_dim(jnp.concatenate([upward, upward], axis=2), first, shots, axis=2)
    up_pair = jnp.concatenate(
        [rolled[part_of, :, at : at + part] for at in range(0, shots, part) for part_of in range(2)], axis=1
    )
    ticks = CHUNKS + DELAY * (levels - 1)
    flying = []
    outs = []
    for tick in range(ticks):
        panel = starts[tick % CHUNKS]
        if tick >= DELAY:
            panel = jnp.where(level == 0, panel, flying[tick - DELAY])
        out = advance(panel, weight, factor)
        outs.append(out)
        if tick + DELAY < ticks:
            flying.append(shifted(out, "depth", 1))
    last = outs[-CHUNKS:]
    dims = (((1,), (1,)), ((), ()))
    panel = jnp.concatenate(last, axis=1)
    turned = jnp.concatenate([half for out in last for half in (-out[:, part:], out[:, :part])], axis=1)
    both = jnp.concatenate([panel, turned], axis=0)
    term = lax.dot_general(up_pair, both, dims, preferred_element_type=jnp.float32)
    summed = lax.psum_scatter(
        term.astype(jnp.bfloat16), "freq", scatter_dimension=0, tiled=True
    )
    scale = (2.0 * shots * freqs) ** (-0.5)
    return (summed.astype(jnp.float32) * scale).reshape(1, rows_own, 2, width)


def solution(mesh):
    return jax.shard_map(
        shards,
        mesh=mesh,
        in_specs=(
            P("freq", None, None, None),
            P("depth", "freq", None, None, None),
            P("depth", "freq", None),
            P("depth", "freq", None, None, None),
        ),
        out_specs=P("depth", "freq", None, None),
        check_vma=False,
    )
```

```python
import jax
import jax.numpy as jnp
from jax import lax
from jax.sharding import PartitionSpec as P

CHUNKS = 4
DELAY = 2


def shifted(block, axis, distance):
    size = lax.axis_size(axis)
    route = [(i, (i + distance) % size) for i in range(size)]
    return lax.ppermute(block, axis, route)


def advance(panel, weight, factor):
    shots = panel.shape[1] // 2
    turned = jnp.concatenate([-panel[:, shots:], panel[:, :shots]], axis=1)
    out = jnp.dot(weight[0], panel, preferred_element_type=jnp.float32) + jnp.dot(
        weight[1], turned, preferred_element_type=jnp.float32
    )
    return (out * factor[:, None]).astype(jnp.bfloat16)


def shards(source, propagator, transmission, upgoing):
    weight = propagator[0, 0]
    factor = transmission[0, 0]
    upward = upgoing[0, 0]
    width = weight.shape[1]
    shots = source.shape[3]
    level = lax.axis_index("depth")
    levels = lax.axis_size("depth")
    freqs = lax.axis_size("freq")
    rows_own = width // freqs
    part = shots // CHUNKS
    starts = [
        jnp.concatenate([source[0, 0, :, at : at + part], source[0, 1, :, at : at + part]], axis=1)
        for at in range(0, shots, part)
    ]
    first = lax.rem(DELAY * (levels - 1 - level), CHUNKS) * part
    rolled = lax.dynamic_slice_in_dim(jnp.concatenate([upward, upward], axis=2), first, shots, axis=2)
    up_pair = jnp.concatenate(
        [rolled[part_of, :, at : at + part] for at in range(0, shots, part) for part_of in range(2)], axis=1
    )
    ticks = CHUNKS + DELAY * (levels - 1)
    flying = []
    outs = []
    for tick in range(ticks):
        panel = starts[tick % CHUNKS]
        if tick >= DELAY:
            panel = jnp.where(level == 0, panel, flying[tick - DELAY])
        out = advance(panel, weight, factor)
        outs.append(out)
        if tick + DELAY < ticks:
            flying.append(shifted(out, "depth", 1))
    last = outs[-CHUNKS:]
    dims = (((1,), (1,)), ((), ()))
    panel = jnp.concatenate(last, axis=1)
    turned = jnp.concatenate([half for out in last for half in (-out[:, part:], out[:, :part])], axis=1)
    both = jnp.concatenate([panel, turned], axis=0)
    term = lax.dot_general(up_pair, both, dims, preferred_element_type=jnp.float32)
    summed = lax.psum_scatter(
        term.astype(jnp.bfloat16), "freq", scatter_dimension=0, tiled=True
    )
    scale = (2.0 * shots * freqs) ** (-0.5)
    return (summed.astype(jnp.float32) * scale).reshape(1, rows_own, 2, width)


def solution(mesh):
    return jax.shard_map(
        shards,
        mesh=mesh,
        in_specs=(
            P("freq", None, None, None),
            P("depth", "freq", None, None, None),
            P("depth", "freq", None),
            P("depth", "freq", None, None, None),
        ),
        out_specs=P("depth", "freq", None, None),
        check_vma=False,
    )
```

```python
import functools
import math

import jax
import jax.numpy as jnp
from jax import lax
from jax.experimental import pallas as pl
from jax.experimental.pallas import tpu as pltpu
from jax.sharding import PartitionSpec as P

CHUNKS = 4
DELAY = 2
LIMIT = 48 * 1024 * 1024


def ring(block, axis, distance):
    size = lax.axis_size(axis)
    return lax.ppermute(block, axis, [(i, (i + distance) % size) for i in range(size)])


def swapped(block, axis, bit):
    return lax.ppermute(block, axis, [(i, i ^ bit) for i in range(lax.axis_size(axis))])


def first_kernel(part, source_ref, weight_ref, factor_ref, out_ref):
    chunks = out_ref.shape[0]
    dims = (((0,), (1,)), ((), ()))
    dot = functools.partial(lax.dot_general, dimension_numbers=dims, preferred_element_type=jnp.float32)
    real, imag = source_ref[0, 0], source_ref[0, 1]
    out_real = dot(real, weight_ref[0, 0, 0]) - dot(imag, weight_ref[0, 0, 1])
    out_imag = dot(real, weight_ref[0, 0, 1]) + dot(imag, weight_ref[0, 0, 0])
    out_real = (out_real * factor_ref[0]).astype(jnp.bfloat16)
    out_imag = (out_imag * factor_ref[0]).astype(jnp.bfloat16)
    for chunk in range(chunks):
        out_ref[chunk, :part] = out_real[chunk * part : (chunk + 1) * part]
        out_ref[chunk, part:] = out_imag[chunk * part : (chunk + 1) * part]


def first_advance(source, propagator, transmission, part):
    width = propagator.shape[3]
    shots = source.shape[3]
    wide = width // 4
    return pl.pallas_call(
        functools.partial(first_kernel, part),
        grid=(width // wide,),
        in_specs=[
            pl.BlockSpec((1, 2, width, shots), lambda n: (0, 0, 0, 0)),
            pl.BlockSpec((1, 1, 2, wide, width), lambda n: (0, 0, 0, n, 0)),
            pl.BlockSpec((1, 1, wide), lambda n: (0, 0, n)),
        ],
        out_specs=pl.BlockSpec((shots // part, 2 * part, wide), lambda n: (0, 0, n)),
        out_shape=jax.ShapeDtypeStruct((shots // part, 2 * part, width), jnp.bfloat16),
        compiler_params=pltpu.CompilerParams(vmem_limit_bytes=LIMIT),
        cost_estimate=pl.CostEstimate(
            flops=8 * width * width * shots, bytes_accessed=4 * width * (width + 2 * shots), transcendentals=0
        ),
    )(source, propagator, transmission)


def advance(panel, weight, factor):
    part = panel.shape[0] // 2
    dims = (((1,), (1,)), ((), ()))
    turned = jnp.concatenate([-panel[part:], panel[:part]], axis=0)
    out = lax.dot_general(panel, weight[0], dims, preferred_element_type=jnp.float32) + lax.dot_general(
        turned, weight[1], dims, preferred_element_type=jnp.float32
    )
    return (out * factor[None, :]).astype(jnp.bfloat16)


def operand_kernel(part, step, spot_ref, own_ref, got_ref, out_ref):
    rows = own_ref.shape[1]
    shots = own_ref.shape[2]
    chunks = shots // part
    for first in range(0, chunks, step):

        @pl.when(spot_ref[0] == first)
        def _():
            for which, ref in enumerate((own_ref, got_ref)):
                real, imag = ref[0], ref[1]
                minus = -real
                for at in range(chunks):
                    lo = (first + at) % chunks * part
                    left = (which * chunks + at) * 2 * part
                    out_ref[:rows, left : left + 2 * part] = jnp.concatenate(
                        [real[:, lo : lo + part], imag[:, lo : lo + part]], axis=1
                    )
                    out_ref[rows:, left : left + 2 * part] = jnp.concatenate(
                        [imag[:, lo : lo + part], minus[:, lo : lo + part]], axis=1
                    )


def operand(spots, own, got, rows, part, step):
    shots = own.shape[2]
    blocks = got.shape[1] // rows
    return pl.pallas_call(
        functools.partial(operand_kernel, part, step),
        grid_spec=pltpu.PrefetchScalarGridSpec(
            num_scalar_prefetch=1,
            grid=(blocks,),
            in_specs=[
                pl.BlockSpec((2, rows, shots), lambda i, spot: (0, spot[1 + i], 0)),
                pl.BlockSpec((2, rows, shots), lambda i, spot: (0, spot[1 + blocks + i], 0)),
            ],
            out_specs=pl.BlockSpec((2 * rows, 4 * shots), lambda i, spot: (i, 0)),
        ),
        out_shape=jax.ShapeDtypeStruct((2 * rows * blocks, 4 * shots), jnp.bfloat16),
        compiler_params=pltpu.CompilerParams(vmem_limit_bytes=LIMIT),
        cost_estimate=pl.CostEstimate(flops=0, bytes_accessed=24 * rows * blocks * shots, transcendentals=0),
    )(spots, own, got)


def term_kernel(rows, *refs):
    left_ref, panels, (keep_ref, send_ref, joined) = refs[0], refs[1:-3], refs[-3:]
    at = 0
    for panel in panels:
        joined[at : at + panel.shape[0]] = panel[...]
        at += panel.shape[0]
    out = jnp.dot(left_ref[...], joined[...], preferred_element_type=jnp.float32)
    groups = keep_ref.shape[0]
    for k in range(groups):
        for part in range(2):
            lo = (2 * k + part) * rows
            keep_ref[k, part] = out[lo : lo + rows]
            lo += 2 * groups * rows
            send_ref[k, part] = out[lo : lo + rows].astype(jnp.bfloat16)


def terms(left, panels, rows):
    deep = left.shape[1]
    width = panels[0].shape[1]
    groups = left.shape[0] // (4 * rows)
    wide = width // 4
    return pl.pallas_call(
        functools.partial(term_kernel, rows),
        grid=(width // wide,),
        in_specs=[pl.BlockSpec(left.shape, lambda n: (0, 0))]
        + [pl.BlockSpec((panel.shape[0], wide), lambda n: (0, n)) for panel in panels],
        out_specs=[pl.BlockSpec((groups, 2, rows, wide), lambda n: (0, 0, 0, n))] * 2,
        out_shape=[
            jax.ShapeDtypeStruct((groups, 2, rows, width), jnp.float32),
            jax.ShapeDtypeStruct((groups, 2, rows, width), jnp.bfloat16),
        ],
        scratch_shapes=[pltpu.VMEM((deep, wide), jnp.bfloat16)],
        compiler_params=pltpu.CompilerParams(vmem_limit_bytes=LIMIT),
        cost_estimate=pl.CostEstimate(
            flops=2 * left.shape[0] * deep * width,
            bytes_accessed=2 * deep * (left.shape[0] + width) + 12 * groups * rows * width,
            transcendentals=0,
        ),
    )(left, *panels)


def last_kernel(scale, *refs):
    *parts, out_ref = refs
    for part in range(2):
        total = parts[0][0, part]
        for ref in parts[1:]:
            total += ref[0, part].astype(jnp.float32)
        out_ref[0, :, part] = total * scale


def last_sum(parts, scale):
    rows, width = parts[0].shape[2:]
    return pl.pallas_call(
        functools.partial(last_kernel, scale),
        grid=(2,),
        in_specs=[pl.BlockSpec((1, 2, rows // 2, width), lambda n: (0, 0, n, 0)) for _ in parts],
        out_specs=pl.BlockSpec((1, rows // 2, 2, width), lambda n: (0, n, 0, 0)),
        out_shape=jax.ShapeDtypeStruct((1, rows, 2, width), jnp.float32),
        compiler_params=pltpu.CompilerParams(vmem_limit_bytes=LIMIT),
        cost_estimate=pl.CostEstimate(
            flops=2 * len(parts) * rows * width, bytes_accessed=16 * rows * width, transcendentals=0
        ),
    )(*parts)


def shards(source, propagator, transmission, upgoing):
    weight = propagator[0, 0]
    factor = transmission[0, 0]
    upward = upgoing[0, 0]
    width = weight.shape[1]
    shots = source.shape[3]
    level = lax.axis_index("depth")
    levels = lax.axis_size("depth")
    freqs = lax.axis_size("freq")
    mine = lax.axis_index("freq")
    groups = freqs // 4
    group, place, core = mine // 4, (mine // 2) % 2, mine % 2
    rows = width // freqs
    part = shots // CHUNKS
    ready = first_advance(source, propagator, transmission, part)
    by_place = upward.reshape(2, groups, 2, 2 * rows, shots)
    asked = lax.dynamic_index_in_dim(by_place, 1 - place, 2, keepdims=False).reshape(2, 2 * groups * rows, shots)
    got = swapped(asked, "freq", 2)
    order = [(s, k) for s in range(2) for k in range(groups)]
    spots = (
        [lax.rem(DELAY * (levels - 1 - level), CHUNKS)]
        + [4 * lax.rem(group + k, groups) + 2 * place + (core ^ s) for s, k in order]
        + [2 * lax.rem(group + k, groups) + (core ^ s) for s, k in order]
    )
    left = operand(jnp.stack(spots).astype(jnp.int32), upward, got, rows, part, math.gcd(DELAY, CHUNKS))

    ticks = CHUNKS + DELAY * (levels - 1)
    flying = []
    own = []
    other = []
    for tick in range(ticks):
        out = ready[tick % CHUNKS]
        if tick >= DELAY:
            arrived = flying[tick - DELAY]
            if tick == ticks // 2:
                arrived, left = lax.optimization_barrier((arrived, left))
            out = jnp.where(level == 0, out, advance(arrived, weight, factor))
        if tick + DELAY < ticks:
            flying.append(ring(out, "depth", 1))
        if tick >= ticks - CHUNKS:
            own.append(out)
            other.append(swapped(out, "freq", 2))
    keep, send = terms(left, own + other, rows)
    near = swapped(send, "freq", 1)
    parts = [keep, near]
    for k in range(1, groups):
        total = (keep[k : k + 1] + near[k : k + 1].astype(jnp.float32)).astype(jnp.bfloat16)
        parts.append(ring(total, "freq", 4 * k))
    return last_sum(parts, (2.0 * shots * freqs) ** (-0.5))


def solution(mesh):
    return jax.shard_map(
        shards,
        mesh=mesh,
        in_specs=(
            P("freq", None, None, None),
            P("depth", "freq", None, None, None),
            P("depth", "freq", None),
            P("depth", "freq", None, None, None),
        ),
        out_specs=P("depth", "freq", None, None),
        check_vma=False,
    )
```

```python
import functools
import math

import jax
import jax.numpy as jnp
from jax import lax
from jax.experimental import pallas as pl
from jax.experimental.pallas import tpu as pltpu
from jax.sharding import PartitionSpec as P

CHUNKS = 4
DELAY = 2
LIMIT = 32 * 1024 * 1024


def ring(block, axis, distance):
    size = lax.axis_size(axis)
    return lax.ppermute(block, axis, [(i, (i + distance) % size) for i in range(size)])


def swapped(block, axis, bit):
    return lax.ppermute(block, axis, [(i, i ^ bit) for i in range(lax.axis_size(axis))])


def first_kernel(part, source_ref, weight_ref, factor_ref, *refs):
    *outs, joined_ref, source, factor, left, sem, sems = refs
    width = joined_ref.shape[0]
    blocks = sems.shape[0]
    wide = width // blocks

    def copies(n):
        rows = pl.ds(n * wide, wide)
        return [
            pltpu.make_async_copy(
                weight_ref.at[0, 0, half, rows], joined_ref.at[rows, pl.ds(half * width, width)], sems.at[n, half]
            )
            for half in range(2)
        ]

    begin = [
        pltpu.make_async_copy(source_ref.at[0], source, sem.at[0]),
        pltpu.make_async_copy(factor_ref.at[0], factor, sem.at[1]),
    ]
    for copy in begin:
        copy.start()
    for n in range(blocks):
        for copy in copies(n):
            copy.start()
    for copy in begin:
        copy.wait()
    real, imag = source[0].T, source[1].T
    for chunk in range(len(outs)):
        lo, at = chunk * part, 2 * chunk * part
        left[at : at + part, :width] = real[lo : lo + part]
        left[at : at + part, width:] = -imag[lo : lo + part]
        left[at + part : at + 2 * part, :width] = imag[lo : lo + part]
        left[at + part : at + 2 * part, width:] = real[lo : lo + part]
    for n in range(blocks):
        for copy in copies(n):
            copy.wait()
        columns = slice(n * wide, (n + 1) * wide)
        out = lax.dot_general(
            left[...], joined_ref[columns], (((1,), (1,)), ((), ())), preferred_element_type=jnp.float32
        )
        out = (out * factor[:, columns]).astype(jnp.bfloat16)
        for chunk in range(len(outs)):
            outs[chunk][:, columns] = out[2 * chunk * part : 2 * (chunk + 1) * part]


def first_advance(source, propagator, transmission, part):
    width = propagator.shape[3]
    shots = source.shape[3]
    chunks = shots // part
    whole = pl.BlockSpec(memory_space=pltpu.VMEM)
    return pl.pallas_call(
        functools.partial(first_kernel, part),
        in_specs=[pl.BlockSpec(memory_space=pltpu.HBM)] * 3,
        out_specs=[whole] * (chunks + 1),
        out_shape=[jax.ShapeDtypeStruct((2 * part, width), jnp.bfloat16)] * chunks
        + [jax.ShapeDtypeStruct((width, 2 * width), jnp.bfloat16)],
        scratch_shapes=[
            pltpu.VMEM((2, width, shots), jnp.bfloat16),
            pltpu.VMEM((1, width), jnp.float32),
            pltpu.VMEM((2 * shots, 2 * width), jnp.bfloat16),
            pltpu.SemaphoreType.DMA((2,)),
            pltpu.SemaphoreType.DMA((4, 2)),
        ],
        compiler_params=pltpu.CompilerParams(vmem_limit_bytes=LIMIT),
        cost_estimate=pl.CostEstimate(
            flops=8 * width * width * shots, bytes_accessed=4 * width * (width + 2 * shots), transcendentals=0
        ),
    )(*(pltpu.with_memory_space_constraint(x, pltpu.HBM) for x in (source, propagator, transmission)))


def advance(panel, joined, factor):
    part = panel.shape[0] // 2
    turned = jnp.concatenate([-panel[part:], panel[:part]], axis=0)
    both = jnp.concatenate([panel, turned], axis=1)
    out = lax.dot_general(both, joined, (((1,), (1,)), ((), ())), preferred_element_type=jnp.float32)
    return (out * factor[None, :]).astype(jnp.bfloat16)


def operand_kernel(part, step, spot_ref, own_ref, got_ref, out_ref):
    rows = own_ref.shape[1]
    shots = own_ref.shape[2]
    chunks = shots // part
    for first in range(0, chunks, step):

        @pl.when(spot_ref[0] == first)
        def _():
            for which, ref in enumerate((own_ref, got_ref)):
                real, imag = ref[0], ref[1]
                minus = -real
                for at in range(chunks):
                    lo = (first + at) % chunks * part
                    left = (which * chunks + at) * 2 * part
                    out_ref[:rows, left : left + 2 * part] = jnp.concatenate(
                        [real[:, lo : lo + part], imag[:, lo : lo + part]], axis=1
                    )
                    out_ref[rows:, left : left + 2 * part] = jnp.concatenate(
                        [imag[:, lo : lo + part], minus[:, lo : lo + part]], axis=1
                    )


def operand(spots, own, got, rows, part, step):
    shots = own.shape[2]
    blocks = got.shape[1] // rows
    return pl.pallas_call(
        functools.partial(operand_kernel, part, step),
        grid_spec=pltpu.PrefetchScalarGridSpec(
            num_scalar_prefetch=1,
            grid=(blocks,),
            in_specs=[
                pl.BlockSpec((2, rows, shots), lambda i, spot: (0, spot[1 + i], 0)),
                pl.BlockSpec((2, rows, shots), lambda i, spot: (0, spot[1 + blocks + i], 0)),
            ],
            out_specs=pl.BlockSpec((2 * rows, 4 * shots), lambda i, spot: (i, 0)),
        ),
        out_shape=jax.ShapeDtypeStruct((2 * rows * blocks, 4 * shots), jnp.bfloat16),
        compiler_params=pltpu.CompilerParams(vmem_limit_bytes=LIMIT),
        cost_estimate=pl.CostEstimate(flops=0, bytes_accessed=24 * rows * blocks * shots, transcendentals=0),
    )(spots, own, got)


def gathered(panels, columns):
    return jnp.concatenate([panel[:, columns] for panel in panels], axis=0)


def early_kernel(left_ref, *refs):
    *panels, out_ref = refs
    deep = sum(panel.shape[0] for panel in panels)
    wide = out_ref.shape[1] // 4
    for n in range(4):
        columns = slice(n * wide, (n + 1) * wide)
        out_ref[:, columns] = jnp.dot(
            left_ref[:, :deep], gathered(panels, columns), preferred_element_type=jnp.float32
        )


def late_kernel(left_ref, early_ref, *refs):
    *panels, keep_ref, send_ref = refs
    deep = sum(panel.shape[0] for panel in panels)
    start = left_ref.shape[1] - deep
    groups, _, rows, width = keep_ref.shape
    wide = width // 4
    for n in range(4):
        columns = slice(n * wide, (n + 1) * wide)
        out = early_ref[:, columns] + jnp.dot(
            left_ref[:, start:], gathered(panels, columns), preferred_element_type=jnp.float32
        )
        for k in range(groups):
            for part in range(2):
                lo = (2 * k + part) * rows
                keep_ref[k, part, :, columns] = out[lo : lo + rows]
                lo += 2 * groups * rows
                send_ref[k, part, :, columns] = out[lo : lo + rows].astype(jnp.bfloat16)


def whole_call(kernel, args, outs, flops):
    whole = pl.BlockSpec(memory_space=pltpu.VMEM)
    size = sum(math.prod(x.shape) * x.dtype.itemsize for x in (*args, *outs))
    return pl.pallas_call(
        kernel,
        in_specs=[whole] * len(args),
        out_specs=[whole] * len(outs),
        out_shape=outs,
        compiler_params=pltpu.CompilerParams(vmem_limit_bytes=LIMIT),
        cost_estimate=pl.CostEstimate(flops=flops, bytes_accessed=size, transcendentals=0),
    )(*args)


def early_terms(left, panels):
    out = jax.ShapeDtypeStruct((left.shape[0], panels[0].shape[1]), jnp.float32)
    deep = sum(panel.shape[0] for panel in panels)
    return whole_call(early_kernel, (left, *panels), [out], 2 * deep * out.shape[0] * out.shape[1])[0]


def late_terms(left, early, panels, rows):
    width = early.shape[1]
    deep = sum(panel.shape[0] for panel in panels)
    shape = (left.shape[0] // (4 * rows), 2, rows, width)
    outs = [jax.ShapeDtypeStruct(shape, jnp.float32), jax.ShapeDtypeStruct(shape, jnp.bfloat16)]
    return whole_call(late_kernel, (left, early, *panels), outs, 2 * deep * left.shape[0] * width)


def last_kernel(scale, *refs):
    *parts, out_ref = refs
    for part in range(2):
        total = parts[0][0, part]
        for ref in parts[1:]:
            total += ref[0, part].astype(jnp.float32)
        out_ref[0, :, part] = total * scale


def last_sum(parts, scale):
    rows, width = parts[0].shape[2:]
    return pl.pallas_call(
        functools.partial(last_kernel, scale),
        grid=(2,),
        in_specs=[pl.BlockSpec((1, 2, rows // 2, width), lambda n: (0, 0, n, 0)) for _ in parts],
        out_specs=pl.BlockSpec((1, rows // 2, 2, width), lambda n: (0, n, 0, 0)),
        out_shape=jax.ShapeDtypeStruct((1, rows, 2, width), jnp.float32),
        compiler_params=pltpu.CompilerParams(vmem_limit_bytes=LIMIT),
        cost_estimate=pl.CostEstimate(
            flops=2 * len(parts) * rows * width, bytes_accessed=16 * rows * width, transcendentals=0
        ),
    )(*parts)


def shards(source, propagator, transmission, upgoing):
    factor = transmission[0, 0]
    upward = upgoing[0, 0]
    width = propagator.shape[3]
    shots = source.shape[3]
    level = lax.axis_index("depth")
    levels = lax.axis_size("depth")
    freqs = lax.axis_size("freq")
    mine = lax.axis_index("freq")
    groups = freqs // 4
    group, place, core = mine // 4, (mine // 2) % 2, mine % 2
    rows = width // freqs
    part = shots // CHUNKS
    *ready, joined = first_advance(source, propagator, transmission, part)
    by_place = upward.reshape(2, groups, 2, 2 * rows, shots)
    asked = lax.dynamic_index_in_dim(by_place, 1 - place, 2, keepdims=False).reshape(2, 2 * groups * rows, shots)
    got = swapped(asked, "freq", 2)
    order = [(s, k) for s in range(2) for k in range(groups)]
    spots = (
        [lax.rem(DELAY * (levels - 1 - level), CHUNKS)]
        + [4 * lax.rem(group + k, groups) + 2 * place + (core ^ s) for s, k in order]
        + [2 * lax.rem(group + k, groups) + (core ^ s) for s, k in order]
    )
    left = operand(jnp.stack(spots).astype(jnp.int32), upward, got, rows, part, math.gcd(DELAY, CHUNKS))

    ticks = CHUNKS + DELAY * (levels - 1)
    flying = []
    own = []
    other = []
    for tick in range(ticks):
        out = ready[tick % CHUNKS]
        if tick >= DELAY:
            arrived = flying[tick - DELAY]
            if tick == ticks // 2:
                arrived, left = lax.optimization_barrier((arrived, left))
            out = jnp.where(level == 0, out, advance(arrived, joined, factor))
        if tick + DELAY < ticks:
            flying.append(ring(out, "depth", 1))
        if tick >= ticks - CHUNKS:
            own.append(out)
            other.append(swapped(out, "freq", 2))
    early = early_terms(left, own + other[:-2])
    keep, send = late_terms(left, early, other[-2:], rows)
    near = swapped(send, "freq", 1)
    parts = [keep, near]
    for k in range(1, groups):
        total = (keep[k : k + 1] + near[k : k + 1].astype(jnp.float32)).astype(jnp.bfloat16)
        parts.append(ring(total, "freq", 4 * k))
    return last_sum(parts, (2.0 * shots * freqs) ** (-0.5))


def solution(mesh):
    return jax.shard_map(
        shards,
        mesh=mesh,
        in_specs=(
            P("freq", None, None, None),
            P("depth", "freq", None, None, None),
            P("depth", "freq", None),
            P("depth", "freq", None, None, None),
        ),
        out_specs=P("depth", "freq", None, None),
        check_vma=False,
    )
```

```python
import functools
import math

import jax
import jax.numpy as jnp
from jax import lax
from jax.experimental import pallas as pl
from jax.experimental.pallas import tpu as pltpu
from jax.sharding import PartitionSpec as P

CHUNKS = 4
DELAY = 2
LIMIT = 16 * 1024 * 1024


def ring(block, axis, distance):
    size = lax.axis_size(axis)
    return lax.ppermute(block, axis, [(i, (i + distance) % size) for i in range(size)])


def swapped(block, axis, bit):
    return lax.ppermute(block, axis, [(i, i ^ bit) for i in range(lax.axis_size(axis))])


def first_kernel(part, source_ref, weight_ref, factor_ref, *refs):
    *outs, joined_ref, source, factor, right, sem, sems = refs
    width = joined_ref.shape[0]
    blocks = sems.shape[0]
    wide = width // blocks

    def copies(n):
        rows = pl.ds(n * wide, wide)
        return [
            pltpu.make_async_copy(
                weight_ref.at[0, 0, half, rows], joined_ref.at[rows, pl.ds(half * width, width)], sems.at[n, half]
            )
            for half in range(2)
        ]

    begin = [
        pltpu.make_async_copy(source_ref.at[0], source, sem.at[0]),
        pltpu.make_async_copy(factor_ref.at[0], factor, sem.at[1]),
    ]
    for copy in begin:
        copy.start()
    for n in range(blocks):
        for copy in copies(n):
            copy.start()
    for copy in begin:
        copy.wait()
    shots = source.shape[2]
    for half, (re, im) in enumerate(((source[0], source[1]), (-source[1], source[0]))):
        right[half * width : (half + 1) * width, :shots] = re
        right[half * width : (half + 1) * width, shots:] = im
    for n in range(blocks):
        for copy in copies(n):
            copy.wait()
        columns = slice(n * wide, (n + 1) * wide)
        out = jnp.dot(joined_ref[columns], right[...], preferred_element_type=jnp.float32)
        out = (out.T * factor[:, columns]).astype(jnp.bfloat16)
        for chunk in range(len(outs)):
            lo = chunk * part
            outs[chunk][:part, columns] = out[lo : lo + part]
            outs[chunk][part:, columns] = out[shots + lo : shots + lo + part]


def first_advance(source, propagator, transmission, part):
    width = propagator.shape[3]
    shots = source.shape[3]
    chunks = shots // part
    whole = pl.BlockSpec(memory_space=pltpu.VMEM)
    return pl.pallas_call(
        functools.partial(first_kernel, part),
        in_specs=[pl.BlockSpec(memory_space=pltpu.HBM)] * 3,
        out_specs=[whole] * (chunks + 1),
        out_shape=[jax.ShapeDtypeStruct((2 * part, width), jnp.bfloat16)] * chunks
        + [pltpu.VMEM((width, 2 * width), jnp.bfloat16)],
        scratch_shapes=[
            pltpu.VMEM((2, width, shots), jnp.bfloat16),
            pltpu.VMEM((1, width), jnp.float32),
            pltpu.VMEM((2 * width, 2 * shots), jnp.bfloat16),
            pltpu.SemaphoreType.DMA((2,)),
            pltpu.SemaphoreType.DMA((4, 2)),
        ],
        compiler_params=pltpu.CompilerParams(vmem_limit_bytes=LIMIT),
        cost_estimate=pl.CostEstimate(
            flops=8 * width * width * shots, bytes_accessed=4 * width * (width + 2 * shots), transcendentals=0
        ),
    )(*(pltpu.with_memory_space_constraint(x, pltpu.HBM) for x in (source, propagator, transmission)))


def advance_kernel(level_ref, arrived_ref, ready_ref, joined_ref, factor_ref, out_ref, both):
    part = arrived_ref.shape[0] // 2
    width = arrived_ref.shape[1]
    wide = width // 4

    @pl.when(level_ref[0] == 0)
    def _():
        out_ref[...] = ready_ref[...]

    @pl.when(level_ref[0] != 0)
    def _():
        both[:, :width] = arrived_ref[...]
        both[:part, width:] = -arrived_ref[part:]
        both[part:, width:] = arrived_ref[:part]
        for n in range(4):
            columns = slice(n * wide, (n + 1) * wide)
            out = lax.dot_general(
                joined_ref[columns], both[...], (((1,), (1,)), ((), ())), preferred_element_type=jnp.float32
            )
            out_ref[:, columns] = (out.T * factor_ref[:, columns]).astype(jnp.bfloat16)


def advance(level, arrived, ready, joined, factor):
    rows, width = arrived.shape
    whole = pl.BlockSpec(memory_space=pltpu.VMEM)
    return pl.pallas_call(
        advance_kernel,
        in_specs=[pl.BlockSpec(memory_space=pltpu.SMEM)] + [whole] * 4,
        out_specs=whole,
        out_shape=jax.ShapeDtypeStruct((rows, width), jnp.bfloat16),
        scratch_shapes=[pltpu.VMEM((rows, 2 * width), jnp.bfloat16)],
        compiler_params=pltpu.CompilerParams(vmem_limit_bytes=LIMIT),
        cost_estimate=pl.CostEstimate(
            flops=4 * rows * width * width, bytes_accessed=4 * width * width + 6 * rows * width, transcendentals=0
        ),
    )(level, arrived, ready, pltpu.with_memory_space_constraint(joined, pltpu.VMEM), factor)


def operand_kernel(part, step, spot_ref, own_ref, got_ref, out_ref):
    rows = own_ref.shape[1]
    shots = own_ref.shape[2]
    chunks = shots // part
    for first in range(0, chunks, step):

        @pl.when(spot_ref[0] == first)
        def _():
            for which, ref in enumerate((own_ref, got_ref)):
                real, imag = ref[0], ref[1]
                minus = -real
                for at in range(chunks):
                    lo = (first + at) % chunks * part
                    left = (which * chunks + at) * 2 * part
                    out_ref[:rows, left : left + 2 * part] = jnp.concatenate(
                        [real[:, lo : lo + part], imag[:, lo : lo + part]], axis=1
                    )
                    out_ref[rows:, left : left + 2 * part] = jnp.concatenate(
                        [imag[:, lo : lo + part], minus[:, lo : lo + part]], axis=1
                    )


def operand(spots, own, got, rows, part, step):
    shots = own.shape[2]
    blocks = got.shape[1] // rows
    return pl.pallas_call(
        functools.partial(operand_kernel, part, step),
        grid_spec=pltpu.PrefetchScalarGridSpec(
            num_scalar_prefetch=1,
            grid=(blocks,),
            in_specs=[
                pl.BlockSpec((2, rows, shots), lambda i, spot: (0, spot[1 + i], 0)),
                pl.BlockSpec((2, rows, shots), lambda i, spot: (0, spot[1 + blocks + i], 0)),
            ],
            out_specs=pl.BlockSpec((2 * rows, 4 * shots), lambda i, spot: (i, 0)),
        ),
        out_shape=jax.ShapeDtypeStruct((2 * rows * blocks, 4 * shots), jnp.bfloat16),
        compiler_params=pltpu.CompilerParams(vmem_limit_bytes=LIMIT),
        cost_estimate=pl.CostEstimate(flops=0, bytes_accessed=24 * rows * blocks * shots, transcendentals=0),
    )(spots, own, got)


def gathered(panels, columns):
    return jnp.concatenate([panel[:, columns] for panel in panels], axis=0)


def early_kernel(left_ref, *refs):
    *panels, out_ref = refs
    deep = sum(panel.shape[0] for panel in panels)
    wide = out_ref.shape[1] // 4
    for n in range(4):
        columns = slice(n * wide, (n + 1) * wide)
        out_ref[:, columns] = jnp.dot(
            left_ref[:, :deep], gathered(panels, columns), preferred_element_type=jnp.float32
        )


def late_kernel(left_ref, early_ref, *refs):
    *panels, keep_ref, send_ref = refs
    deep = sum(panel.shape[0] for panel in panels)
    start = left_ref.shape[1] - deep
    groups, _, rows, width = keep_ref.shape
    wide = width // 4
    for n in range(4):
        columns = slice(n * wide, (n + 1) * wide)
        out = early_ref[:, columns] + jnp.dot(
            left_ref[:, start:], gathered(panels, columns), preferred_element_type=jnp.float32
        )
        for k in range(groups):
            for part in range(2):
                lo = (2 * k + part) * rows
                keep_ref[k, part, :, columns] = out[lo : lo + rows]
                lo += 2 * groups * rows
                send_ref[k, part, :, columns] = out[lo : lo + rows].astype(jnp.bfloat16)


def whole_call(kernel, args, outs, flops):
    whole = pl.BlockSpec(memory_space=pltpu.VMEM)
    size = sum(math.prod(x.shape) * x.dtype.itemsize for x in (*args, *outs))
    return pl.pallas_call(
        kernel,
        in_specs=[whole] * len(args),
        out_specs=[whole] * len(outs),
        out_shape=outs,
        compiler_params=pltpu.CompilerParams(vmem_limit_bytes=LIMIT),
        cost_estimate=pl.CostEstimate(flops=flops, bytes_accessed=size, transcendentals=0),
    )(*args)


def early_terms(left, panels):
    out = jax.ShapeDtypeStruct((left.shape[0], panels[0].shape[1]), jnp.float32)
    deep = sum(panel.shape[0] for panel in panels)
    return whole_call(early_kernel, (left, *panels), [out], 2 * deep * out.shape[0] * out.shape[1])[0]


def late_terms(left, early, panels, rows):
    width = early.shape[1]
    deep = sum(panel.shape[0] for panel in panels)
    shape = (left.shape[0] // (4 * rows), 2, rows, width)
    outs = [jax.ShapeDtypeStruct(shape, jnp.float32), jax.ShapeDtypeStruct(shape, jnp.bfloat16)]
    return whole_call(late_kernel, (left, early, *panels), outs, 2 * deep * left.shape[0] * width)


def last_kernel(scale, *refs):
    *parts, out_ref = refs
    for part in range(2):
        total = parts[0][0, part]
        for ref in parts[1:]:
            total += ref[0, part].astype(jnp.float32)
        out_ref[0, :, part] = total * scale


def last_sum(parts, scale):
    rows, width = parts[0].shape[2:]
    return pl.pallas_call(
        functools.partial(last_kernel, scale),
        grid=(2,),
        in_specs=[pl.BlockSpec((1, 2, rows // 2, width), lambda n: (0, 0, n, 0)) for _ in parts],
        out_specs=pl.BlockSpec((1, rows // 2, 2, width), lambda n: (0, n, 0, 0)),
        out_shape=jax.ShapeDtypeStruct((1, rows, 2, width), jnp.float32),
        compiler_params=pltpu.CompilerParams(vmem_limit_bytes=LIMIT),
        cost_estimate=pl.CostEstimate(
            flops=2 * len(parts) * rows * width, bytes_accessed=16 * rows * width, transcendentals=0
        ),
    )(*parts)


def shards(source, propagator, transmission, upgoing):
    factor = transmission[0]
    upward = upgoing[0, 0]
    width = propagator.shape[3]
    shots = source.shape[3]
    level = lax.axis_index("depth")
    levels = lax.axis_size("depth")
    level_at = level.astype(jnp.int32).reshape(1)
    freqs = lax.axis_size("freq")
    mine = lax.axis_index("freq")
    groups = freqs // 4
    group, place, core = mine // 4, (mine // 2) % 2, mine % 2
    rows = width // freqs
    part = shots // CHUNKS
    *ready, joined = first_advance(source, propagator, transmission, part)
    by_place = upward.reshape(2, groups, 2, 2 * rows, shots)
    asked = lax.dynamic_index_in_dim(by_place, 1 - place, 2, keepdims=False).reshape(2, 2 * groups * rows, shots)
    got = swapped(asked, "freq", 2)
    order = [(s, k) for s in range(2) for k in range(groups)]
    spots = (
        [lax.rem(DELAY * (levels - 1 - level), CHUNKS)]
        + [4 * lax.rem(group + k, groups) + 2 * place + (core ^ s) for s, k in order]
        + [2 * lax.rem(group + k, groups) + (core ^ s) for s, k in order]
    )
    left = operand(jnp.stack(spots).astype(jnp.int32), upward, got, rows, part, math.gcd(DELAY, CHUNKS))

    ticks = CHUNKS + DELAY * (levels - 1)
    flying = []
    own = []
    other = []
    for tick in range(ticks):
        out = ready[tick % CHUNKS]
        if tick >= DELAY:
            arrived = flying[tick - DELAY]
            if tick == ticks // 2:
                arrived, left = lax.optimization_barrier((arrived, left))
            out = advance(level_at, arrived, out, joined, factor)
        if tick + DELAY < ticks:
            flying.append(ring(out, "depth", 1))
        if tick >= ticks - CHUNKS:
            own.append(out)
            other.append(swapped(out, "freq", 2))
    early = early_terms(left, own + other[:-2])
    keep, send = late_terms(left, early, other[-2:], rows)
    near = swapped(send, "freq", 1)
    parts = [keep, near]
    for k in range(1, groups):
        total = (keep[k : k + 1] + near[k : k + 1].astype(jnp.float32)).astype(jnp.bfloat16)
        parts.append(ring(total, "freq", 4 * k))
    return last_sum(parts, (2.0 * shots * freqs) ** (-0.5))


def solution(mesh):
    return jax.shard_map(
        shards,
        mesh=mesh,
        in_specs=(
            P("freq", None, None, None),
            P("depth", "freq", None, None, None),
            P("depth", "freq", None),
            P("depth", "freq", None, None, None),
        ),
        out_specs=P("depth", "freq", None, None),
        check_vma=False,
    )
```

```python
import functools
import math

import jax
import jax.numpy as jnp
from jax import lax
from jax.experimental import pallas as pl
from jax.experimental.pallas import tpu as pltpu
from jax.sharding import PartitionSpec as P

CHUNKS = 4
DELAY = 2
LIMIT = 16 * 1024 * 1024


def ring(block, axis, distance):
    size = lax.axis_size(axis)
    return lax.ppermute(block, axis, [(i, (i + distance) % size) for i in range(size)])


def swapped(block, axis, bit):
    return lax.ppermute(block, axis, [(i, i ^ bit) for i in range(lax.axis_size(axis))])


def places(ids_ref):
    mine = ids_ref[1]
    return lax.div(mine, 4), lax.rem(lax.div(mine, 2), 2), lax.rem(mine, 2)


def first_kernel(part, ids_ref, source_ref, weight_ref, factor_ref, upward_ref, *refs):
    *outs, joined_ref, asked_ref, source, factor, sem, sems, asked_sems = refs
    width = joined_ref.shape[0]
    shots = source.shape[2]
    blocks = sems.shape[0]
    wide = width // blocks
    groups = asked_sems.shape[0]
    tall = asked_ref.shape[1] // groups
    _, place, _ = places(ids_ref)

    def copies(n):
        rows = pl.ds(n * wide, wide)
        return [
            pltpu.make_async_copy(
                weight_ref.at[0, 0, half, rows], joined_ref.at[rows, pl.ds(half * width, width)], sems.at[n, half]
            )
            for half in range(2)
        ]

    begin = [
        pltpu.make_async_copy(source_ref.at[0], source, sem.at[0]),
        pltpu.make_async_copy(factor_ref.at[0], factor, sem.at[1]),
    ]
    asked = []
    for k in range(groups):
        row = pl.multiple_of((2 * k + 1 - place) * tall, tall)
        asked.append(
            pltpu.make_async_copy(
                upward_ref.at[0, 0, :, pl.ds(row, tall)], asked_ref.at[:, pl.ds(k * tall, tall)], asked_sems.at[k]
            )
        )
    for copy in begin + copies(0):
        copy.start()
    for copy in begin:
        copy.wait()
    for n in range(1, blocks):
        for copy in copies(n):
            copy.start()
    for copy in asked:
        copy.start()
    dot = functools.partial(jnp.dot, preferred_element_type=jnp.float32)
    for n in range(blocks):
        for copy in copies(n):
            copy.wait()
        columns = slice(n * wide, (n + 1) * wide)
        real, imag = joined_ref[columns, :width], joined_ref[columns, width:]
        out_real = dot(real, source[0]) - dot(imag, source[1])
        out_imag = dot(real, source[1]) + dot(imag, source[0])
        out_real = (out_real.T * factor[:, columns]).astype(jnp.bfloat16)
        out_imag = (out_imag.T * factor[:, columns]).astype(jnp.bfloat16)
        for chunk in range(len(outs)):
            lo = chunk * part
            outs[chunk][:part, columns] = out_real[lo : lo + part]
            outs[chunk][part:, columns] = out_imag[lo : lo + part]
    for copy in asked:
        copy.wait()


def first_advance(ids, source, propagator, transmission, upgoing, part, groups):
    width = propagator.shape[3]
    shots = source.shape[3]
    chunks = shots // part
    whole = pl.BlockSpec(memory_space=pltpu.VMEM)
    pinned = [pltpu.with_memory_space_constraint(x, pltpu.HBM) for x in (source, propagator, transmission, upgoing)]
    return pl.pallas_call(
        functools.partial(first_kernel, part),
        in_specs=[pl.BlockSpec(memory_space=pltpu.SMEM)] + [pl.BlockSpec(memory_space=pltpu.HBM)] * 4,
        out_specs=[whole] * (chunks + 2),
        out_shape=[jax.ShapeDtypeStruct((2 * part, width), jnp.bfloat16)] * chunks
        + [
            pltpu.VMEM((width, 2 * width), jnp.bfloat16),
            jax.ShapeDtypeStruct((2, width // 2, shots), jnp.bfloat16),
        ],
        scratch_shapes=[
            pltpu.VMEM((2, width, shots), jnp.bfloat16),
            pltpu.VMEM((1, width), jnp.float32),
            pltpu.SemaphoreType.DMA((2,)),
            pltpu.SemaphoreType.DMA((4, 2)),
            pltpu.SemaphoreType.DMA((groups,)),
        ],
        compiler_params=pltpu.CompilerParams(vmem_limit_bytes=LIMIT),
        cost_estimate=pl.CostEstimate(
            flops=8 * width * width * shots, bytes_accessed=4 * width * (width + 2 * shots), transcendentals=0
        ),
    )(ids, *pinned)


def advance_kernel(ids_ref, arrived_ref, ready_ref, joined_ref, factor_ref, out_ref, both):
    part = arrived_ref.shape[0] // 2
    width = arrived_ref.shape[1]
    wide = width // 4

    @pl.when(ids_ref[0] == 0)
    def _():
        out_ref[...] = ready_ref[...]

    @pl.when(ids_ref[0] != 0)
    def _():
        both[:, :width] = arrived_ref[...]
        both[:part, width:] = -arrived_ref[part:]
        both[part:, width:] = arrived_ref[:part]
        for n in range(4):
            columns = slice(n * wide, (n + 1) * wide)
            out = lax.dot_general(
                joined_ref[columns], both[...], (((1,), (1,)), ((), ())), preferred_element_type=jnp.float32
            )
            out_ref[:, columns] = (out.T * factor_ref[:, columns]).astype(jnp.bfloat16)


def advance(ids, arrived, ready, joined, factor):
    rows, width = arrived.shape
    whole = pl.BlockSpec(memory_space=pltpu.VMEM)
    return pl.pallas_call(
        advance_kernel,
        in_specs=[pl.BlockSpec(memory_space=pltpu.SMEM)] + [whole] * 4,
        out_specs=whole,
        out_shape=jax.ShapeDtypeStruct((rows, width), jnp.bfloat16),
        scratch_shapes=[pltpu.VMEM((rows, 2 * width), jnp.bfloat16)],
        compiler_params=pltpu.CompilerParams(vmem_limit_bytes=LIMIT),
        cost_estimate=pl.CostEstimate(
            flops=4 * rows * width * width, bytes_accessed=4 * width * width + 6 * rows * width, transcendentals=0
        ),
    )(ids, arrived, ready, pltpu.with_memory_space_constraint(joined, pltpu.VMEM), factor)


def operand_kernel(part, levels, ids_ref, own_ref, got_ref, out_ref):
    rows = own_ref.shape[1]
    shots = own_ref.shape[2]
    chunks = shots // part
    turn = lax.rem(DELAY * (levels - 1 - ids_ref[0]), chunks)
    for first in range(0, chunks, math.gcd(DELAY, chunks)):

        @pl.when(turn == first)
        def _():
            for which, ref in enumerate((own_ref, got_ref)):
                real, imag = ref[0], ref[1]
                minus = -real
                for at in range(chunks):
                    lo = (first + at) % chunks * part
                    left = (which * chunks + at) * 2 * part
                    out_ref[:rows, left : left + 2 * part] = jnp.concatenate(
                        [real[:, lo : lo + part], imag[:, lo : lo + part]], axis=1
                    )
                    out_ref[rows:, left : left + 2 * part] = jnp.concatenate(
                        [imag[:, lo : lo + part], minus[:, lo : lo + part]], axis=1
                    )


def operand(ids, own, got, rows, part, levels):
    shots = own.shape[2]
    blocks = got.shape[1] // rows
    groups = blocks // 2

    def spot(i, ids_ref, stride):
        group, place, core = places(ids_ref)
        other = lax.rem(lax.div(i, groups) + core, 2)
        block = stride * lax.rem(group + lax.rem(i, groups), groups) + other
        return block + 2 * place if stride == 4 else block

    return pl.pallas_call(
        functools.partial(operand_kernel, part, levels),
        grid_spec=pltpu.PrefetchScalarGridSpec(
            num_scalar_prefetch=1,
            grid=(blocks,),
            in_specs=[
                pl.BlockSpec((2, rows, shots), lambda i, ids_ref: (0, spot(i, ids_ref, 4), 0)),
                pl.BlockSpec((2, rows, shots), lambda i, ids_ref: (0, spot(i, ids_ref, 2), 0)),
            ],
            out_specs=pl.BlockSpec((2 * rows, 4 * shots), lambda i, ids_ref: (i, 0)),
        ),
        out_shape=jax.ShapeDtypeStruct((2 * rows * blocks, 4 * shots), jnp.bfloat16),
        compiler_params=pltpu.CompilerParams(vmem_limit_bytes=LIMIT),
        cost_estimate=pl.CostEstimate(flops=0, bytes_accessed=24 * rows * blocks * shots, transcendentals=0),
    )(ids, own, got)


def gathered(panels, columns):
    return jnp.concatenate([panel[:, columns] for panel in panels], axis=0)


def early_kernel(left_ref, *refs):
    *panels, out_ref = refs
    deep = sum(panel.shape[0] for panel in panels)
    wide = out_ref.shape[1] // 4
    for n in range(4):
        columns = slice(n * wide, (n + 1) * wide)
        out_ref[:, columns] = jnp.dot(
            left_ref[:, :deep], gathered(panels, columns), preferred_element_type=jnp.float32
        )


def late_kernel(left_ref, early_ref, *refs):
    *panels, keep_ref, send_ref = refs
    deep = sum(panel.shape[0] for panel in panels)
    start = left_ref.shape[1] - deep
    groups, _, rows, width = keep_ref.shape
    wide = width // 4
    for n in range(4):
        columns = slice(n * wide, (n + 1) * wide)
        out = early_ref[:, columns] + jnp.dot(
            left_ref[:, start:], gathered(panels, columns), preferred_element_type=jnp.float32
        )
        for k in range(groups):
            for part in range(2):
                lo = (2 * k + part) * rows
                keep_ref[k, part, :, columns] = out[lo : lo + rows]
                lo += 2 * groups * rows
                send_ref[k, part, :, columns] = out[lo : lo + rows].astype(jnp.bfloat16)


def whole_call(kernel, args, outs, flops):
    whole = pl.BlockSpec(memory_space=pltpu.VMEM)
    size = sum(math.prod(x.shape) * x.dtype.itemsize for x in (*args, *outs))
    return pl.pallas_call(
        kernel,
        in_specs=[whole] * len(args),
        out_specs=[whole] * len(outs),
        out_shape=outs,
        compiler_params=pltpu.CompilerParams(vmem_limit_bytes=LIMIT),
        cost_estimate=pl.CostEstimate(flops=flops, bytes_accessed=size, transcendentals=0),
    )(*args)


def early_terms(left, panels):
    out = jax.ShapeDtypeStruct((left.shape[0], panels[0].shape[1]), jnp.float32)
    deep = sum(panel.shape[0] for panel in panels)
    return whole_call(early_kernel, (left, *panels), [out], 2 * deep * out.shape[0] * out.shape[1])[0]


def late_terms(left, early, panels, rows):
    width = early.shape[1]
    deep = sum(panel.shape[0] for panel in panels)
    shape = (left.shape[0] // (4 * rows), 2, rows, width)
    outs = [jax.ShapeDtypeStruct(shape, jnp.float32), jax.ShapeDtypeStruct(shape, jnp.bfloat16)]
    return whole_call(late_kernel, (left, early, *panels), outs, 2 * deep * left.shape[0] * width)


def last_kernel(scale, *refs):
    *parts, out_ref = refs
    for part in range(2):
        total = parts[0][0, part]
        for ref in parts[1:]:
            total += ref[0, part].astype(jnp.float32)
        out_ref[0, :, part] = total * scale


def last_sum(parts, scale):
    rows, width = parts[0].shape[2:]
    return pl.pallas_call(
        functools.partial(last_kernel, scale),
        grid=(2,),
        in_specs=[pl.BlockSpec((1, 2, rows // 2, width), lambda n: (0, 0, n, 0)) for _ in parts],
        out_specs=pl.BlockSpec((1, rows // 2, 2, width), lambda n: (0, n, 0, 0)),
        out_shape=jax.ShapeDtypeStruct((1, rows, 2, width), jnp.float32),
        compiler_params=pltpu.CompilerParams(vmem_limit_bytes=LIMIT),
        cost_estimate=pl.CostEstimate(
            flops=2 * len(parts) * rows * width, bytes_accessed=16 * rows * width, transcendentals=0
        ),
    )(*parts)


def shards(source, propagator, transmission, upgoing):
    factor = transmission[0]
    upward = upgoing[0, 0]
    width = propagator.shape[3]
    shots = source.shape[3]
    levels = lax.axis_size("depth")
    freqs = lax.axis_size("freq")
    groups = freqs // 4
    rows = width // freqs
    part = shots // CHUNKS
    ids = jnp.stack([lax.axis_index("depth"), lax.axis_index("freq")]).astype(jnp.int32)
    *ready, joined, asked = first_advance(ids, source, propagator, transmission, upgoing, part, groups)
    got = swapped(asked, "freq", 2)
    left = operand(ids, upward, got, rows, part, levels)

    ticks = CHUNKS + DELAY * (levels - 1)
    flying = []
    own = []
    other = []
    for tick in range(ticks):
        out = ready[tick % CHUNKS]
        if tick >= DELAY:
            arrived = flying[tick - DELAY]
            if tick == ticks // 2:
                arrived, left = lax.optimization_barrier((arrived, left))
            out = advance(ids, arrived, out, joined, factor)
        if tick + DELAY < ticks:
            flying.append(ring(out, "depth", 1))
        if tick >= ticks - CHUNKS:
            own.append(out)
            other.append(swapped(out, "freq", 2))
    early = early_terms(left, own + other[:-2])
    keep, send = late_terms(left, early, other[-2:], rows)
    near = swapped(send, "freq", 1)
    parts = [keep, near]
    for k in range(1, groups):
        total = (keep[k : k + 1] + near[k : k + 1].astype(jnp.float32)).astype(jnp.bfloat16)
        parts.append(ring(total, "freq", 4 * k))
    return last_sum(parts, (2.0 * shots * freqs) ** (-0.5))


def solution(mesh):
    return jax.shard_map(
        shards,
        mesh=mesh,
        in_specs=(
            P("freq", None, None, None),
            P("depth", "freq", None, None, None),
            P("depth", "freq", None),
            P("depth", "freq", None, None, None),
        ),
        out_specs=P("depth", "freq", None, None),
        check_vma=False,
    )
```

```python
import functools
import math

import jax
import jax.numpy as jnp
from jax import lax
from jax.experimental import pallas as pl
from jax.experimental.pallas import tpu as pltpu
from jax.sharding import PartitionSpec as P

CHUNKS = 4
DELAY = 2
LIMIT = 16 * 1024 * 1024


def ring(block, axis, distance):
    size = lax.axis_size(axis)
    return lax.ppermute(block, axis, [(i, (i + distance) % size) for i in range(size)])


def swapped(block, axis, bit):
    return lax.ppermute(block, axis, [(i, i ^ bit) for i in range(lax.axis_size(axis))])


def places(mine_ref):
    mine = mine_ref[0]
    return lax.div(mine, 4), lax.rem(lax.div(mine, 2), 2), lax.rem(mine, 2)


def first_kernel(part, level_ref, mine_ref, source_ref, weight_ref, factor_ref, upward_ref, *refs):
    *outs, joined_ref, asked_ref, source, factor, sem, sems, asked_sems = refs
    width = joined_ref.shape[0]
    shots = source.shape[2]
    blocks = sems.shape[0]
    wide = width // blocks
    groups = asked_sems.shape[0]
    tall = asked_ref.shape[1] // groups
    _, place, _ = places(mine_ref)

    def copies(n):
        rows = pl.ds(n * wide, wide)
        return [
            pltpu.make_async_copy(
                weight_ref.at[0, 0, half, rows], joined_ref.at[rows, pl.ds(half * width, width)], sems.at[n, half]
            )
            for half in range(2)
        ]

    begin = [
        pltpu.make_async_copy(source_ref.at[0], source, sem.at[0]),
        pltpu.make_async_copy(factor_ref.at[0], factor, sem.at[1]),
    ]
    asked = []
    for k in range(groups):
        row = pl.multiple_of((2 * k + 1 - place) * tall, tall)
        asked.append(
            pltpu.make_async_copy(
                upward_ref.at[0, 0, :, pl.ds(row, tall)], asked_ref.at[:, pl.ds(k * tall, tall)], asked_sems.at[k]
            )
        )
    for copy in begin + copies(0):
        copy.start()
    for copy in begin:
        copy.wait()
    for n in range(1, blocks):
        for copy in copies(n):
            copy.start()
    for copy in asked:
        copy.start()
    dot = functools.partial(jnp.dot, preferred_element_type=jnp.float32)
    for n in range(blocks):
        for copy in copies(n):
            copy.wait()
        columns = slice(n * wide, (n + 1) * wide)
        real, imag = joined_ref[columns, :width], joined_ref[columns, width:]
        out_real = dot(real, source[0]) - dot(imag, source[1])
        out_imag = dot(real, source[1]) + dot(imag, source[0])
        out_real = (out_real.T * factor[:, columns]).astype(jnp.bfloat16)
        out_imag = (out_imag.T * factor[:, columns]).astype(jnp.bfloat16)
        for chunk in range(len(outs)):
            lo = chunk * part
            outs[chunk][:part, columns] = out_real[lo : lo + part]
            outs[chunk][part:, columns] = out_imag[lo : lo + part]
    for copy in asked:
        copy.wait()


def first_advance(level, mine, source, propagator, transmission, upgoing, part, groups):
    width = propagator.shape[3]
    shots = source.shape[3]
    chunks = shots // part
    whole = pl.BlockSpec(memory_space=pltpu.VMEM)
    pinned = [pltpu.with_memory_space_constraint(x, pltpu.HBM) for x in (source, propagator, transmission, upgoing)]
    return pl.pallas_call(
        functools.partial(first_kernel, part),
        in_specs=[pl.BlockSpec(memory_space=pltpu.SMEM)] * 2 + [pl.BlockSpec(memory_space=pltpu.HBM)] * 4,
        out_specs=[whole] * (chunks + 2),
        out_shape=[jax.ShapeDtypeStruct((2 * part, width), jnp.bfloat16)] * chunks
        + [
            pltpu.VMEM((width, 2 * width), jnp.bfloat16),
            jax.ShapeDtypeStruct((2, width // 2, shots), jnp.bfloat16),
        ],
        scratch_shapes=[
            pltpu.VMEM((2, width, shots), jnp.bfloat16),
            pltpu.VMEM((1, width), jnp.float32),
            pltpu.SemaphoreType.DMA((2,)),
            pltpu.SemaphoreType.DMA((4, 2)),
            pltpu.SemaphoreType.DMA((groups,)),
        ],
        compiler_params=pltpu.CompilerParams(vmem_limit_bytes=LIMIT),
        cost_estimate=pl.CostEstimate(
            flops=8 * width * width * shots, bytes_accessed=4 * width * (width + 2 * shots), transcendentals=0
        ),
    )(level, mine, *pinned)


def advance_kernel(level_ref, arrived_ref, ready_ref, joined_ref, factor_ref, out_ref, both):
    part = arrived_ref.shape[0] // 2
    width = arrived_ref.shape[1]
    wide = width // 4

    @pl.when(level_ref[0] == 0)
    def _():
        out_ref[...] = ready_ref[...]

    @pl.when(level_ref[0] != 0)
    def _():
        both[:, :width] = arrived_ref[...]
        both[:part, width:] = -arrived_ref[part:]
        both[part:, width:] = arrived_ref[:part]
        for n in range(4):
            columns = slice(n * wide, (n + 1) * wide)
            out = lax.dot_general(
                joined_ref[columns], both[...], (((1,), (1,)), ((), ())), preferred_element_type=jnp.float32
            )
            out_ref[:, columns] = (out.T * factor_ref[:, columns]).astype(jnp.bfloat16)


def advance(level, arrived, ready, joined, factor):
    rows, width = arrived.shape
    whole = pl.BlockSpec(memory_space=pltpu.VMEM)
    return pl.pallas_call(
        advance_kernel,
        in_specs=[pl.BlockSpec(memory_space=pltpu.SMEM)] + [whole] * 4,
        out_specs=whole,
        out_shape=jax.ShapeDtypeStruct((rows, width), jnp.bfloat16),
        scratch_shapes=[pltpu.VMEM((rows, 2 * width), jnp.bfloat16)],
        compiler_params=pltpu.CompilerParams(vmem_limit_bytes=LIMIT),
        cost_estimate=pl.CostEstimate(
            flops=4 * rows * width * width, bytes_accessed=4 * width * width + 6 * rows * width, transcendentals=0
        ),
    )(level, arrived, ready, pltpu.with_memory_space_constraint(joined, pltpu.VMEM), factor)


def operand_kernel(part, levels, level_ref, mine_ref, own_ref, got_ref, out_ref):
    rows = own_ref.shape[1]
    shots = own_ref.shape[2]
    chunks = shots // part
    turn = lax.rem(DELAY * (levels - 1 - level_ref[0]), chunks)
    for first in range(0, chunks, math.gcd(DELAY, chunks)):

        @pl.when(turn == first)
        def _():
            for which, ref in enumerate((own_ref, got_ref)):
                real, imag = ref[0], ref[1]
                minus = -real
                for at in range(chunks):
                    lo = (first + at) % chunks * part
                    left = (which * chunks + at) * 2 * part
                    out_ref[:rows, left : left + 2 * part] = jnp.concatenate(
                        [real[:, lo : lo + part], imag[:, lo : lo + part]], axis=1
                    )
                    out_ref[rows:, left : left + 2 * part] = jnp.concatenate(
                        [imag[:, lo : lo + part], minus[:, lo : lo + part]], axis=1
                    )


def operand(level, mine, own, got, rows, part, levels):
    shots = own.shape[2]
    blocks = got.shape[1] // rows
    groups = blocks // 2

    def spot(i, mine_ref, stride):
        group, place, core = places(mine_ref)
        other = lax.rem(lax.div(i, groups) + core, 2)
        block = stride * lax.rem(group + lax.rem(i, groups), groups) + other
        return block + 2 * place if stride == 4 else block

    return pl.pallas_call(
        functools.partial(operand_kernel, part, levels),
        grid_spec=pltpu.PrefetchScalarGridSpec(
            num_scalar_prefetch=2,
            grid=(blocks,),
            in_specs=[
                pl.BlockSpec((2, rows, shots), lambda i, _, mine_ref: (0, spot(i, mine_ref, 4), 0)),
                pl.BlockSpec((2, rows, shots), lambda i, _, mine_ref: (0, spot(i, mine_ref, 2), 0)),
            ],
            out_specs=pl.BlockSpec((2 * rows, 4 * shots), lambda i, *_: (i, 0)),
        ),
        out_shape=jax.ShapeDtypeStruct((2 * rows * blocks, 4 * shots), jnp.bfloat16),
        compiler_params=pltpu.CompilerParams(vmem_limit_bytes=LIMIT),
        cost_estimate=pl.CostEstimate(flops=0, bytes_accessed=24 * rows * blocks * shots, transcendentals=0),
    )(level, mine, own, got)


def gathered(panels, columns):
    return jnp.concatenate([panel[:, columns] for panel in panels], axis=0)


def early_kernel(left_ref, *refs):
    *panels, out_ref = refs
    deep = sum(panel.shape[0] for panel in panels)
    wide = out_ref.shape[1] // 4
    for n in range(4):
        columns = slice(n * wide, (n + 1) * wide)
        out_ref[:, columns] = jnp.dot(
            left_ref[:, :deep], gathered(panels, columns), preferred_element_type=jnp.float32
        )


def late_kernel(left_ref, early_ref, *refs):
    *panels, keep_ref, send_ref = refs
    deep = sum(panel.shape[0] for panel in panels)
    start = left_ref.shape[1] - deep
    groups, _, rows, width = keep_ref.shape
    wide = width // 4
    for n in range(4):
        columns = slice(n * wide, (n + 1) * wide)
        out = early_ref[:, columns] + jnp.dot(
            left_ref[:, start:], gathered(panels, columns), preferred_element_type=jnp.float32
        )
        for k in range(groups):
            for part in range(2):
                lo = (2 * k + part) * rows
                keep_ref[k, part, :, columns] = out[lo : lo + rows]
                lo += 2 * groups * rows
                send_ref[k, part, :, columns] = out[lo : lo + rows].astype(jnp.bfloat16)


def whole_call(kernel, args, outs, flops):
    whole = pl.BlockSpec(memory_space=pltpu.VMEM)
    size = sum(math.prod(x.shape) * x.dtype.itemsize for x in (*args, *outs))
    return pl.pallas_call(
        kernel,
        in_specs=[whole] * len(args),
        out_specs=[whole] * len(outs),
        out_shape=outs,
        compiler_params=pltpu.CompilerParams(vmem_limit_bytes=LIMIT),
        cost_estimate=pl.CostEstimate(flops=flops, bytes_accessed=size, transcendentals=0),
    )(*args)


def early_terms(left, panels):
    out = jax.ShapeDtypeStruct((left.shape[0], panels[0].shape[1]), jnp.float32)
    deep = sum(panel.shape[0] for panel in panels)
    return whole_call(early_kernel, (left, *panels), [out], 2 * deep * out.shape[0] * out.shape[1])[0]


def late_terms(left, early, panels, rows):
    width = early.shape[1]
    deep = sum(panel.shape[0] for panel in panels)
    shape = (left.shape[0] // (4 * rows), 2, rows, width)
    outs = [jax.ShapeDtypeStruct(shape, jnp.float32), jax.ShapeDtypeStruct(shape, jnp.bfloat16)]
    return whole_call(late_kernel, (left, early, *panels), outs, 2 * deep * left.shape[0] * width)


def last_kernel(scale, *refs):
    *parts, out_ref = refs
    for part in range(2):
        total = parts[0][0, part]
        for ref in parts[1:]:
            total += ref[0, part].astype(jnp.float32)
        out_ref[0, :, part] = total * scale


def last_sum(parts, scale):
    rows, width = parts[0].shape[2:]
    return pl.pallas_call(
        functools.partial(last_kernel, scale),
        grid=(2,),
        in_specs=[pl.BlockSpec((1, 2, rows // 2, width), lambda n: (0, 0, n, 0)) for _ in parts],
        out_specs=pl.BlockSpec((1, rows // 2, 2, width), lambda n: (0, n, 0, 0)),
        out_shape=jax.ShapeDtypeStruct((1, rows, 2, width), jnp.float32),
        compiler_params=pltpu.CompilerParams(vmem_limit_bytes=LIMIT),
        cost_estimate=pl.CostEstimate(
            flops=2 * len(parts) * rows * width, bytes_accessed=16 * rows * width, transcendentals=0
        ),
    )(*parts)


def shards(source, propagator, transmission, upgoing):
    factor = transmission[0]
    upward = upgoing[0, 0]
    width = propagator.shape[3]
    shots = source.shape[3]
    levels = lax.axis_size("depth")
    freqs = lax.axis_size("freq")
    groups = freqs // 4
    rows = width // freqs
    part = shots // CHUNKS
    level, mine = (lax.axis_index(axis).astype(jnp.int32).reshape(1) for axis in ("depth", "freq"))
    *ready, joined, asked = first_advance(level, mine, source, propagator, transmission, upgoing, part, groups)
    got = swapped(asked, "freq", 2)
    left = operand(level, mine, upward, got, rows, part, levels)

    ticks = CHUNKS + DELAY * (levels - 1)
    flying = []
    own = []
    other = []
    for tick in range(ticks):
        out = ready[tick % CHUNKS]
        if tick >= DELAY:
            arrived = flying[tick - DELAY]
            if tick == ticks // 2:
                arrived, left = lax.optimization_barrier((arrived, left))
            if len(other) >= DELAY:
                arrived, other[-DELAY] = lax.optimization_barrier((arrived, other[-DELAY]))
            out = advance(level, arrived, out, joined, factor)
        if tick + DELAY < ticks:
            flying.append(ring(out, "depth", 1))
        if tick >= ticks - CHUNKS:
            own.append(out)
            other.append(swapped(out, "freq", 2))
    early = early_terms(left, own + other[:-2])
    keep, send = late_terms(left, early, other[-2:], rows)
    near = swapped(send, "freq", 1)
    parts = [keep, near]
    for k in range(1, groups):
        total = (keep[k : k + 1] + near[k : k + 1].astype(jnp.float32)).astype(jnp.bfloat16)
        parts.append(ring(total, "freq", 4 * k))
    return last_sum(parts, (2.0 * shots * freqs) ** (-0.5))


def solution(mesh):
    return jax.shard_map(
        shards,
        mesh=mesh,
        in_specs=(
            P("freq", None, None, None),
            P("depth", "freq", None, None, None),
            P("depth", "freq", None),
            P("depth", "freq", None, None, None),
        ),
        out_specs=P("depth", "freq", None, None),
        check_vma=False,
    )
```

```python
import functools
import math

import jax
import jax.numpy as jnp
from jax import lax
from jax.experimental import pallas as pl
from jax.experimental.pallas import tpu as pltpu
from jax.sharding import PartitionSpec as P

CHUNKS = 8
DELAY = 2
LIMIT = 16 * 1024 * 1024


def ring(block, axis, distance):
    size = lax.axis_size(axis)
    return lax.ppermute(block, axis, [(i, (i + distance) % size) for i in range(size)])


def swapped(block, axis, bit):
    return lax.ppermute(block, axis, [(i, i ^ bit) for i in range(lax.axis_size(axis))])


def places(mine_ref):
    mine = mine_ref[0]
    return lax.div(mine, 4), lax.rem(lax.div(mine, 2), 2), lax.rem(mine, 2)


def first_kernel(part, level_ref, mine_ref, source_ref, weight_ref, factor_ref, upward_ref, *refs):
    *outs, joined_ref, asked_ref, source, factor, sem, sems, asked_sems = refs
    width = joined_ref.shape[0]
    shots = source.shape[2]
    blocks = sems.shape[0]
    wide = width // blocks
    groups = asked_sems.shape[0]
    tall = asked_ref.shape[1] // groups
    _, place, _ = places(mine_ref)

    def copies(n):
        rows = pl.ds(n * wide, wide)
        return [
            pltpu.make_async_copy(
                weight_ref.at[0, 0, half, rows], joined_ref.at[rows, pl.ds(half * width, width)], sems.at[n, half]
            )
            for half in range(2)
        ]

    begin = [
        pltpu.make_async_copy(source_ref.at[0], source, sem.at[0]),
        pltpu.make_async_copy(factor_ref.at[0], factor, sem.at[1]),
    ]
    asked = []
    for k in range(groups):
        row = pl.multiple_of((2 * k + 1 - place) * tall, tall)
        asked.append(
            pltpu.make_async_copy(
                upward_ref.at[0, 0, :, pl.ds(row, tall)], asked_ref.at[:, pl.ds(k * tall, tall)], asked_sems.at[k]
            )
        )
    for copy in begin + copies(0):
        copy.start()
    for copy in begin:
        copy.wait()
    for n in range(1, blocks):
        for copy in copies(n):
            copy.start()
    for copy in asked:
        copy.start()
    dot = functools.partial(jnp.dot, preferred_element_type=jnp.float32)
    for n in range(blocks):
        for copy in copies(n):
            copy.wait()
        columns = slice(n * wide, (n + 1) * wide)
        real, imag = joined_ref[columns, :width], joined_ref[columns, width:]
        out_real = dot(real, source[0]) - dot(imag, source[1])
        out_imag = dot(real, source[1]) + dot(imag, source[0])
        out_real = (out_real.T * factor[:, columns]).astype(jnp.bfloat16)
        out_imag = (out_imag.T * factor[:, columns]).astype(jnp.bfloat16)
        for chunk in range(len(outs)):
            lo = chunk * part
            outs[chunk][:part, columns] = out_real[lo : lo + part]
            outs[chunk][part:, columns] = out_imag[lo : lo + part]
    for copy in asked:
        copy.wait()


def first_advance(level, mine, source, propagator, transmission, upgoing, part, groups):
    width = propagator.shape[3]
    shots = source.shape[3]
    chunks = shots // part
    whole = pl.BlockSpec(memory_space=pltpu.VMEM)
    pinned = [pltpu.with_memory_space_constraint(x, pltpu.HBM) for x in (source, propagator, transmission, upgoing)]
    return pl.pallas_call(
        functools.partial(first_kernel, part),
        in_specs=[pl.BlockSpec(memory_space=pltpu.SMEM)] * 2 + [pl.BlockSpec(memory_space=pltpu.HBM)] * 4,
        out_specs=[whole] * (chunks + 2),
        out_shape=[jax.ShapeDtypeStruct((2 * part, width), jnp.bfloat16)] * chunks
        + [
            pltpu.VMEM((width, 2 * width), jnp.bfloat16),
            jax.ShapeDtypeStruct((2, width // 2, shots), jnp.bfloat16),
        ],
        scratch_shapes=[
            pltpu.VMEM((2, width, shots), jnp.bfloat16),
            pltpu.VMEM((1, width), jnp.float32),
            pltpu.SemaphoreType.DMA((2,)),
            pltpu.SemaphoreType.DMA((4, 2)),
            pltpu.SemaphoreType.DMA((groups,)),
        ],
        compiler_params=pltpu.CompilerParams(vmem_limit_bytes=LIMIT),
        cost_estimate=pl.CostEstimate(
            flops=8 * width * width * shots, bytes_accessed=4 * width * (width + 2 * shots), transcendentals=0
        ),
    )(level, mine, *pinned)


def advance_kernel(level_ref, arrived_ref, ready_ref, joined_ref, factor_ref, out_ref, both):
    part = arrived_ref.shape[0] // 2
    width = arrived_ref.shape[1]
    wide = width // 4

    @pl.when(level_ref[0] == 0)
    def _():
        out_ref[...] = ready_ref[...]

    @pl.when(level_ref[0] != 0)
    def _():
        both[:, :width] = arrived_ref[...]
        both[:part, width:] = -arrived_ref[part:]
        both[part:, width:] = arrived_ref[:part]
        for n in range(4):
            columns = slice(n * wide, (n + 1) * wide)
            out = lax.dot_general(
                joined_ref[columns], both[...], (((1,), (1,)), ((), ())), preferred_element_type=jnp.float32
            )
            out_ref[:, columns] = (out.T * factor_ref[:, columns]).astype(jnp.bfloat16)


def advance(level, arrived, ready, joined, factor):
    rows, width = arrived.shape
    whole = pl.BlockSpec(memory_space=pltpu.VMEM)
    return pl.pallas_call(
        advance_kernel,
        in_specs=[pl.BlockSpec(memory_space=pltpu.SMEM)] + [whole] * 4,
        out_specs=whole,
        out_shape=jax.ShapeDtypeStruct((rows, width), jnp.bfloat16),
        scratch_shapes=[pltpu.VMEM((rows, 2 * width), jnp.bfloat16)],
        compiler_params=pltpu.CompilerParams(vmem_limit_bytes=LIMIT),
        cost_estimate=pl.CostEstimate(
            flops=4 * rows * width * width, bytes_accessed=4 * width * width + 6 * rows * width, transcendentals=0
        ),
    )(level, arrived, ready, pltpu.with_memory_space_constraint(joined, pltpu.VMEM), factor)


def operand_kernel(part, levels, level_ref, mine_ref, own_ref, got_ref, out_ref):
    rows = own_ref.shape[1]
    shots = own_ref.shape[2]
    chunks = shots // part
    turn = lax.rem(DELAY * (levels - 1 - level_ref[0]), chunks)
    for first in range(0, chunks, math.gcd(DELAY, chunks)):

        @pl.when(turn == first)
        def _():
            for which, ref in enumerate((own_ref, got_ref)):
                real, imag = ref[0], ref[1]
                minus = -real
                for at in range(chunks):
                    lo = (first + at) % chunks * part
                    left = (which * chunks + at) * 2 * part
                    out_ref[:rows, left : left + 2 * part] = jnp.concatenate(
                        [real[:, lo : lo + part], imag[:, lo : lo + part]], axis=1
                    )
                    out_ref[rows:, left : left + 2 * part] = jnp.concatenate(
                        [imag[:, lo : lo + part], minus[:, lo : lo + part]], axis=1
                    )


def operand(level, mine, own, got, rows, part, levels):
    shots = own.shape[2]
    blocks = got.shape[1] // rows
    groups = blocks // 2

    def spot(i, mine_ref, stride):
        group, place, core = places(mine_ref)
        other = lax.rem(lax.div(i, groups) + core, 2)
        block = stride * lax.rem(group + lax.rem(i, groups), groups) + other
        return block + 2 * place if stride == 4 else block

    return pl.pallas_call(
        functools.partial(operand_kernel, part, levels),
        grid_spec=pltpu.PrefetchScalarGridSpec(
            num_scalar_prefetch=2,
            grid=(blocks,),
            in_specs=[
                pl.BlockSpec((2, rows, shots), lambda i, _, mine_ref: (0, spot(i, mine_ref, 4), 0)),
                pl.BlockSpec((2, rows, shots), lambda i, _, mine_ref: (0, spot(i, mine_ref, 2), 0)),
            ],
            out_specs=pl.BlockSpec((2 * rows, 4 * shots), lambda i, *_: (i, 0)),
        ),
        out_shape=jax.ShapeDtypeStruct((2 * rows * blocks, 4 * shots), jnp.bfloat16),
        compiler_params=pltpu.CompilerParams(vmem_limit_bytes=LIMIT),
        cost_estimate=pl.CostEstimate(flops=0, bytes_accessed=24 * rows * blocks * shots, transcendentals=0),
    )(level, mine, own, got)


def gathered(panels, columns):
    return jnp.concatenate([panel[:, columns] for panel in panels], axis=0)


def early_kernel(left_ref, *refs):
    *panels, out_ref = refs
    deep = sum(panel.shape[0] for panel in panels)
    wide = out_ref.shape[1] // 4
    for n in range(4):
        columns = slice(n * wide, (n + 1) * wide)
        out_ref[:, columns] = jnp.dot(
            left_ref[:, :deep], gathered(panels, columns), preferred_element_type=jnp.float32
        )


def late_kernel(left_ref, early_ref, *refs):
    *panels, keep_ref, send_ref = refs
    deep = sum(panel.shape[0] for panel in panels)
    start = left_ref.shape[1] - deep
    groups, _, rows, width = keep_ref.shape
    wide = width // 4
    for n in range(4):
        columns = slice(n * wide, (n + 1) * wide)
        out = early_ref[:, columns] + jnp.dot(
            left_ref[:, start:], gathered(panels, columns), preferred_element_type=jnp.float32
        )
        for k in range(groups):
            for part in range(2):
                lo = (2 * k + part) * rows
                keep_ref[k, part, :, columns] = out[lo : lo + rows]
                lo += 2 * groups * rows
                send_ref[k, part, :, columns] = out[lo : lo + rows].astype(jnp.bfloat16)


def whole_call(kernel, args, outs, flops):
    whole = pl.BlockSpec(memory_space=pltpu.VMEM)
    size = sum(math.prod(x.shape) * x.dtype.itemsize for x in (*args, *outs))
    return pl.pallas_call(
        kernel,
        in_specs=[whole] * len(args),
        out_specs=[whole] * len(outs),
        out_shape=outs,
        compiler_params=pltpu.CompilerParams(vmem_limit_bytes=LIMIT),
        cost_estimate=pl.CostEstimate(flops=flops, bytes_accessed=size, transcendentals=0),
    )(*args)


def early_terms(left, panels):
    out = jax.ShapeDtypeStruct((left.shape[0], panels[0].shape[1]), jnp.float32)
    deep = sum(panel.shape[0] for panel in panels)
    return whole_call(early_kernel, (left, *panels), [out], 2 * deep * out.shape[0] * out.shape[1])[0]


def late_terms(left, early, panels, rows):
    width = early.shape[1]
    deep = sum(panel.shape[0] for panel in panels)
    shape = (left.shape[0] // (4 * rows), 2, rows, width)
    outs = [jax.ShapeDtypeStruct(shape, jnp.float32), jax.ShapeDtypeStruct(shape, jnp.bfloat16)]
    return whole_call(late_kernel, (left, early, *panels), outs, 2 * deep * left.shape[0] * width)


def last_kernel(scale, *refs):
    *parts, out_ref = refs
    for part in range(2):
        total = parts[0][0, part]
        for ref in parts[1:]:
            total += ref[0, part].astype(jnp.float32)
        out_ref[0, :, part] = total * scale


def last_sum(parts, scale):
    rows, width = parts[0].shape[2:]
    return pl.pallas_call(
        functools.partial(last_kernel, scale),
        grid=(2,),
        in_specs=[pl.BlockSpec((1, 2, rows // 2, width), lambda n: (0, 0, n, 0)) for _ in parts],
        out_specs=pl.BlockSpec((1, rows // 2, 2, width), lambda n: (0, n, 0, 0)),
        out_shape=jax.ShapeDtypeStruct((1, rows, 2, width), jnp.float32),
        compiler_params=pltpu.CompilerParams(vmem_limit_bytes=LIMIT),
        cost_estimate=pl.CostEstimate(
            flops=2 * len(parts) * rows * width, bytes_accessed=16 * rows * width, transcendentals=0
        ),
    )(*parts)


def shards(source, propagator, transmission, upgoing):
    factor = transmission[0]
    upward = upgoing[0, 0]
    width = propagator.shape[3]
    shots = source.shape[3]
    levels = lax.axis_size("depth")
    freqs = lax.axis_size("freq")
    groups = freqs // 4
    rows = width // freqs
    part = shots // CHUNKS
    level, mine = (lax.axis_index(axis).astype(jnp.int32).reshape(1) for axis in ("depth", "freq"))
    *ready, joined, asked = first_advance(level, mine, source, propagator, transmission, upgoing, part, groups)
    got = swapped(asked, "freq", 2)
    left = operand(level, mine, upward, got, rows, part, levels)

    ticks = CHUNKS + DELAY * (levels - 1)
    flying = []
    own = []
    other = []
    for tick in range(ticks):
        out = ready[tick % CHUNKS]
        if tick >= DELAY:
            arrived = flying[tick - DELAY]
            if tick == ticks // 2:
                arrived, left = lax.optimization_barrier((arrived, left))
            if len(other) >= DELAY:
                arrived, other[-DELAY] = lax.optimization_barrier((arrived, other[-DELAY]))
            out = advance(level, arrived, out, joined, factor)
        if tick + DELAY < ticks:
            flying.append(ring(out, "depth", 1))
        if tick >= ticks - CHUNKS:
            own.append(out)
            other.append(swapped(out, "freq", 2))
    early = early_terms(left, own + other[:-2])
    keep, send = late_terms(left, early, other[-2:], rows)
    near = swapped(send, "freq", 1)
    parts = [keep, near]
    for k in range(1, groups):
        total = (keep[k : k + 1] + near[k : k + 1].astype(jnp.float32)).astype(jnp.bfloat16)
        parts.append(ring(total, "freq", 4 * k))
    return last_sum(parts, (2.0 * shots * freqs) ** (-0.5))


def solution(mesh):
    return jax.shard_map(
        shards,
        mesh=mesh,
        in_specs=(
            P("freq", None, None, None),
            P("depth", "freq", None, None, None),
            P("depth", "freq", None),
            P("depth", "freq", None, None, None),
        ),
        out_specs=P("depth", "freq", None, None),
        check_vma=False,
    )
```

```python
import functools
import math

import jax
import jax.numpy as jnp
from jax import lax
from jax.experimental import pallas as pl
from jax.experimental.pallas import tpu as pltpu
from jax.sharding import PartitionSpec as P

CHUNKS = 4
DELAY = 2
LIMIT = 16 * 1024 * 1024


def ring(block, axis, distance):
    size = lax.axis_size(axis)
    return lax.ppermute(block, axis, [(i, (i + distance) % size) for i in range(size)])


def swapped(block, axis, bit):
    return lax.ppermute(block, axis, [(i, i ^ bit) for i in range(lax.axis_size(axis))])


def places(mine_ref):
    mine = mine_ref[0]
    return lax.div(mine, 4), lax.rem(lax.div(mine, 2), 2), lax.rem(mine, 2)


def start_panels(part, real, imag, right, factor, outs, columns):
    dot = functools.partial(jnp.dot, preferred_element_type=jnp.float32)
    shots = right.shape[1] // 2
    first, second = dot(real, right), dot(imag, right)
    out_real = ((first[:, :shots] - second[:, shots:]).T * factor).astype(jnp.bfloat16)
    out_imag = ((first[:, shots:] + second[:, :shots]).T * factor).astype(jnp.bfloat16)
    for chunk, out in enumerate(outs):
        lo = chunk * part
        out[:part, columns] = out_real[lo : lo + part]
        out[part:, columns] = out_imag[lo : lo + part]


def first_kernel(part, level_ref, mine_ref, source_ref, weight_ref, factor_ref, upward_ref, *refs):
    *outs, joined_ref, later_ref, asked_ref, right, factor, sem, sems, asked_sems = refs
    width = joined_ref.shape[0]
    shots = later_ref.shape[1] // 2
    blocks = sems.shape[0]
    wide = width // blocks
    groups = asked_sems.shape[0]
    tall = asked_ref.shape[1] // groups
    _, place, _ = places(mine_ref)

    def copies(n):
        rows = pl.ds(n * wide, wide)
        return [
            pltpu.make_async_copy(
                weight_ref.at[0, 0, half, rows], joined_ref.at[rows, pl.ds(half * width, width)], sems.at[n, half]
            )
            for half in range(2)
        ]

    def columns_of(start, to_ref, first_sem):
        return [
            pltpu.make_async_copy(
                source_ref.at[0, half, :, pl.ds(start, shots)],
                to_ref.at[:, pl.ds(half * shots, shots)],
                sem.at[first_sem + half],
            )
            for half in range(2)
        ]

    begin = columns_of(0, right, 0) + [pltpu.make_async_copy(factor_ref.at[0], factor, sem.at[4])]
    rest = columns_of(shots, later_ref, 2)
    for k in range(groups):
        row = pl.multiple_of((2 * k + 1 - place) * tall, tall)
        rest.append(
            pltpu.make_async_copy(
                upward_ref.at[0, 0, :, pl.ds(row, tall)], asked_ref.at[:, pl.ds(k * tall, tall)], asked_sems.at[k]
            )
        )
    for copy in begin:
        copy.start()
    for n in range(blocks):
        for copy in copies(n):
            copy.start()
    for copy in rest:
        copy.start()
    for copy in begin:
        copy.wait()
    for n in range(blocks):
        for copy in copies(n):
            copy.wait()
        columns = slice(n * wide, (n + 1) * wide)
        real, imag = joined_ref[columns, :width], joined_ref[columns, width:]
        start_panels(part, real, imag, right[...], factor[:, columns], outs, columns)
    for copy in rest:
        copy.wait()


def first_advance(level, mine, source, propagator, transmission, upgoing, part, groups):
    width = propagator.shape[3]
    shots = source.shape[3]
    chunks = shots // 2 // part
    whole = pl.BlockSpec(memory_space=pltpu.VMEM)
    pinned = [pltpu.with_memory_space_constraint(x, pltpu.HBM) for x in (source, propagator, transmission, upgoing)]
    return pl.pallas_call(
        functools.partial(first_kernel, part),
        in_specs=[pl.BlockSpec(memory_space=pltpu.SMEM)] * 2 + [pl.BlockSpec(memory_space=pltpu.HBM)] * 4,
        out_specs=[whole] * (chunks + 3),
        out_shape=[jax.ShapeDtypeStruct((2 * part, width), jnp.bfloat16)] * chunks
        + [
            pltpu.VMEM((width, 2 * width), jnp.bfloat16),
            jax.ShapeDtypeStruct((width, shots), jnp.bfloat16),
            jax.ShapeDtypeStruct((2, width // 2, shots), jnp.bfloat16),
        ],
        scratch_shapes=[
            pltpu.VMEM((width, shots), jnp.bfloat16),
            pltpu.VMEM((1, width), jnp.float32),
            pltpu.SemaphoreType.DMA((5,)),
            pltpu.SemaphoreType.DMA((4, 2)),
            pltpu.SemaphoreType.DMA((groups,)),
        ],
        compiler_params=pltpu.CompilerParams(vmem_limit_bytes=LIMIT),
        cost_estimate=pl.CostEstimate(
            flops=4 * width * width * shots, bytes_accessed=4 * width * (width + 2 * shots), transcendentals=0
        ),
    )(level, mine, *pinned)


def second_kernel(part, joined_ref, right_ref, factor_ref, *outs):
    width = joined_ref.shape[0]
    wide = width // 4
    for n in range(4):
        columns = slice(n * wide, (n + 1) * wide)
        real, imag = joined_ref[columns, :width], joined_ref[columns, width:]
        start_panels(part, real, imag, right_ref[...], factor_ref[:, columns], outs, columns)


def second_advance(joined, right, factor, part):
    width, shots = right.shape
    outs = [jax.ShapeDtypeStruct((2 * part, width), jnp.bfloat16)] * (shots // 2 // part)
    joined = pltpu.with_memory_space_constraint(joined, pltpu.VMEM)
    return whole_call(functools.partial(second_kernel, part), (joined, right, factor), outs, 4 * width * width * shots)


def advance_kernel(level_ref, arrived_ref, ready_ref, joined_ref, factor_ref, out_ref, both):
    part = arrived_ref.shape[0] // 2
    width = arrived_ref.shape[1]
    wide = width // 4

    @pl.when(level_ref[0] == 0)
    def _():
        out_ref[...] = ready_ref[...]

    @pl.when(level_ref[0] != 0)
    def _():
        both[:, :width] = arrived_ref[...]
        both[:part, width:] = -arrived_ref[part:]
        both[part:, width:] = arrived_ref[:part]
        for n in range(4):
            columns = slice(n * wide, (n + 1) * wide)
            out = lax.dot_general(
                joined_ref[columns], both[...], (((1,), (1,)), ((), ())), preferred_element_type=jnp.float32
            )
            out_ref[:, columns] = (out.T * factor_ref[:, columns]).astype(jnp.bfloat16)


def advance(level, arrived, ready, joined, factor):
    rows, width = arrived.shape
    whole = pl.BlockSpec(memory_space=pltpu.VMEM)
    return pl.pallas_call(
        advance_kernel,
        in_specs=[pl.BlockSpec(memory_space=pltpu.SMEM)] + [whole] * 4,
        out_specs=whole,
        out_shape=jax.ShapeDtypeStruct((rows, width), jnp.bfloat16),
        scratch_shapes=[pltpu.VMEM((rows, 2 * width), jnp.bfloat16)],
        compiler_params=pltpu.CompilerParams(vmem_limit_bytes=LIMIT),
        cost_estimate=pl.CostEstimate(
            flops=4 * rows * width * width, bytes_accessed=4 * width * width + 6 * rows * width, transcendentals=0
        ),
    )(level, arrived, ready, pltpu.with_memory_space_constraint(joined, pltpu.VMEM), factor)


def operand_kernel(part, levels, level_ref, mine_ref, own_ref, got_ref, out_ref):
    rows = own_ref.shape[1]
    shots = own_ref.shape[2]
    chunks = shots // part
    turn = lax.rem(DELAY * (levels - 1 - level_ref[0]), chunks)
    for first in range(0, chunks, math.gcd(DELAY, chunks)):

        @pl.when(turn == first)
        def _():
            for which, ref in enumerate((own_ref, got_ref)):
                real, imag = ref[0], ref[1]
                minus = -real
                for at in range(chunks):
                    lo = (first + at) % chunks * part
                    left = (which * chunks + at) * 2 * part
                    out_ref[:rows, left : left + 2 * part] = jnp.concatenate(
                        [real[:, lo : lo + part], imag[:, lo : lo + part]], axis=1
                    )
                    out_ref[rows:, left : left + 2 * part] = jnp.concatenate(
                        [imag[:, lo : lo + part], minus[:, lo : lo + part]], axis=1
                    )


def operand(level, mine, own, got, rows, part, levels):
    shots = own.shape[2]
    blocks = got.shape[1] // rows
    groups = blocks // 2

    def spot(i, mine_ref, stride):
        group, place, core = places(mine_ref)
        other = lax.rem(lax.div(i, groups) + core, 2)
        block = stride * lax.rem(group + lax.rem(i, groups), groups) + other
        return block + 2 * place if stride == 4 else block

    return pl.pallas_call(
        functools.partial(operand_kernel, part, levels),
        grid_spec=pltpu.PrefetchScalarGridSpec(
            num_scalar_prefetch=2,
            grid=(blocks,),
            in_specs=[
                pl.BlockSpec((2, rows, shots), lambda i, _, mine_ref: (0, spot(i, mine_ref, 4), 0)),
                pl.BlockSpec((2, rows, shots), lambda i, _, mine_ref: (0, spot(i, mine_ref, 2), 0)),
            ],
            out_specs=pl.BlockSpec((2 * rows, 4 * shots), lambda i, *_: (i, 0)),
        ),
        out_shape=jax.ShapeDtypeStruct((2 * rows * blocks, 4 * shots), jnp.bfloat16),
        compiler_params=pltpu.CompilerParams(vmem_limit_bytes=LIMIT),
        cost_estimate=pl.CostEstimate(flops=0, bytes_accessed=24 * rows * blocks * shots, transcendentals=0),
    )(level, mine, own, got)


def gathered(panels, columns):
    return jnp.concatenate([panel[:, columns] for panel in panels], axis=0)


def early_kernel(left_ref, *refs):
    *panels, out_ref = refs
    deep = sum(panel.shape[0] for panel in panels)
    wide = out_ref.shape[1] // 4
    for n in range(4):
        columns = slice(n * wide, (n + 1) * wide)
        out_ref[:, columns] = jnp.dot(
            left_ref[:, :deep], gathered(panels, columns), preferred_element_type=jnp.float32
        )


def late_kernel(left_ref, early_ref, *refs):
    *panels, keep_ref, send_ref = refs
    deep = sum(panel.shape[0] for panel in panels)
    start = left_ref.shape[1] - deep
    groups, _, rows, width = keep_ref.shape
    wide = width // 4
    for n in range(4):
        columns = slice(n * wide, (n + 1) * wide)
        out = early_ref[:, columns] + jnp.dot(
            left_ref[:, start:], gathered(panels, columns), preferred_element_type=jnp.float32
        )
        for k in range(groups):
            for part in range(2):
                lo = (2 * k + part) * rows
                keep_ref[k, part, :, columns] = out[lo : lo + rows]
                lo += 2 * groups * rows
                send_ref[k, part, :, columns] = out[lo : lo + rows].astype(jnp.bfloat16)


def whole_call(kernel, args, outs, flops):
    whole = pl.BlockSpec(memory_space=pltpu.VMEM)
    size = sum(math.prod(x.shape) * x.dtype.itemsize for x in (*args, *outs))
    return pl.pallas_call(
        kernel,
        in_specs=[whole] * len(args),
        out_specs=[whole] * len(outs),
        out_shape=outs,
        compiler_params=pltpu.CompilerParams(vmem_limit_bytes=LIMIT),
        cost_estimate=pl.CostEstimate(flops=flops, bytes_accessed=size, transcendentals=0),
    )(*args)


def early_terms(left, panels):
    out = jax.ShapeDtypeStruct((left.shape[0], panels[0].shape[1]), jnp.float32)
    deep = sum(panel.shape[0] for panel in panels)
    return whole_call(early_kernel, (left, *panels), [out], 2 * deep * out.shape[0] * out.shape[1])[0]


def late_terms(left, early, panels, rows):
    width = early.shape[1]
    deep = sum(panel.shape[0] for panel in panels)
    shape = (left.shape[0] // (4 * rows), 2, rows, width)
    outs = [jax.ShapeDtypeStruct(shape, jnp.float32), jax.ShapeDtypeStruct(shape, jnp.bfloat16)]
    return whole_call(late_kernel, (left, early, *panels), outs, 2 * deep * left.shape[0] * width)


def last_kernel(scale, *refs):
    *parts, out_ref = refs
    for part in range(2):
        total = parts[0][0, part]
        for ref in parts[1:]:
            total += ref[0, part].astype(jnp.float32)
        out_ref[0, :, part] = total * scale


def last_sum(parts, scale):
    rows, width = parts[0].shape[2:]
    out = jax.ShapeDtypeStruct((1, rows, 2, width), jnp.float32)
    return whole_call(functools.partial(last_kernel, scale), parts, [out], 2 * len(parts) * rows * width)[0]


def shards(source, propagator, transmission, upgoing):
    factor = transmission[0]
    upward = upgoing[0, 0]
    width = propagator.shape[3]
    shots = source.shape[3]
    levels = lax.axis_size("depth")
    freqs = lax.axis_size("freq")
    groups = freqs // 4
    rows = width // freqs
    part = shots // CHUNKS
    level, mine = (lax.axis_index(axis).astype(jnp.int32).reshape(1) for axis in ("depth", "freq"))
    *ready, joined, later, asked = first_advance(level, mine, source, propagator, transmission, upgoing, part, groups)
    ready += second_advance(joined, later, factor, part)
    got = swapped(asked, "freq", 2)
    left = operand(level, mine, upward, got, rows, part, levels)

    ticks = CHUNKS + DELAY * (levels - 1)
    flying = []
    own = []
    other = []
    for tick in range(ticks):
        out = ready[tick % CHUNKS]
        if tick >= DELAY:
            arrived = flying[tick - DELAY]
            if tick == ticks // 2:
                arrived, left = lax.optimization_barrier((arrived, left))
            if len(other) >= DELAY:
                arrived, other[-DELAY] = lax.optimization_barrier((arrived, other[-DELAY]))
            out = advance(level, arrived, out, joined, factor)
        if tick + DELAY < ticks:
            flying.append(ring(out, "depth", 1))
        if tick >= ticks - CHUNKS:
            own.append(out)
            other.append(swapped(out, "freq", 2))
    early = early_terms(left, own + other[:-2])
    keep, send = late_terms(left, early, other[-2:], rows)
    near = swapped(send, "freq", 1)
    parts = [keep, near]
    for k in range(1, groups):
        total = (keep[k : k + 1] + near[k : k + 1].astype(jnp.float32)).astype(jnp.bfloat16)
        parts.append(ring(total, "freq", 4 * k))
    return last_sum(parts, (2.0 * shots * freqs) ** (-0.5))


def solution(mesh):
    return jax.shard_map(
        shards,
        mesh=mesh,
        in_specs=(
            P("freq", None, None, None),
            P("depth", "freq", None, None, None),
            P("depth", "freq", None),
            P("depth", "freq", None, None, None),
        ),
        out_specs=P("depth", "freq", None, None),
        check_vma=False,
    )
```

```python
import functools
import math

import jax
import jax.numpy as jnp
from jax import lax
from jax.experimental import pallas as pl
from jax.experimental.pallas import tpu as pltpu
from jax.sharding import PartitionSpec as P

STEPS = 4
STREAMS = 2
BEHIND = 2
LIMIT = 16 * 1024 * 1024


def ring(block, axis, distance):
    size = lax.axis_size(axis)
    return lax.ppermute(block, axis, [(i, (i + distance) % size) for i in range(size)])


def swapped(block, axis, bit):
    return lax.ppermute(block, axis, [(i, i ^ bit) for i in range(lax.axis_size(axis))])


def places(mine_ref):
    mine = mine_ref[0]
    return lax.div(mine, 4), lax.rem(lax.div(mine, 2), 2), lax.rem(mine, 2)


def start_panels(part, real, imag, right, factor, outs, columns):
    dot = functools.partial(jnp.dot, preferred_element_type=jnp.float32)
    shots = right.shape[1] // 2
    first, second = dot(real, right), dot(imag, right)
    out_real = ((first[:, :shots] - second[:, shots:]).T * factor).astype(jnp.bfloat16)
    out_imag = ((first[:, shots:] + second[:, :shots]).T * factor).astype(jnp.bfloat16)
    for chunk, out in enumerate(outs):
        lo = chunk * part
        out[:part, columns] = out_real[lo : lo + part]
        out[part:, columns] = out_imag[lo : lo + part]


def first_kernel(part, level_ref, mine_ref, source_ref, weight_ref, factor_ref, upward_ref, *refs):
    *outs, joined_ref, later_ref, asked_ref, right, factor, sem, sems, asked_sems = refs
    width = joined_ref.shape[0]
    shots = later_ref.shape[1] // 2
    blocks = sems.shape[0]
    wide = width // blocks
    groups = asked_sems.shape[0]
    tall = asked_ref.shape[1] // groups
    _, place, _ = places(mine_ref)

    def copies(n):
        rows = pl.ds(n * wide, wide)
        return [
            pltpu.make_async_copy(
                weight_ref.at[0, 0, half, rows], joined_ref.at[rows, pl.ds(half * width, width)], sems.at[n, half]
            )
            for half in range(2)
        ]

    def columns_of(start, to_ref, first_sem):
        return [
            pltpu.make_async_copy(
                source_ref.at[0, half, :, pl.ds(start, shots)],
                to_ref.at[:, pl.ds(half * shots, shots)],
                sem.at[first_sem + half],
            )
            for half in range(2)
        ]

    begin = columns_of(0, right, 0) + [pltpu.make_async_copy(factor_ref.at[0], factor, sem.at[4])]
    rest = columns_of(shots, later_ref, 2)
    for k in range(groups):
        row = pl.multiple_of((2 * k + 1 - place) * tall, tall)
        rest.append(
            pltpu.make_async_copy(
                upward_ref.at[0, 0, :, pl.ds(row, tall)], asked_ref.at[:, pl.ds(k * tall, tall)], asked_sems.at[k]
            )
        )
    for copy in begin:
        copy.start()
    for n in range(blocks):
        for copy in copies(n):
            copy.start()
    for copy in rest:
        copy.start()
    for copy in begin:
        copy.wait()
    for n in range(blocks):
        for copy in copies(n):
            copy.wait()
        columns = slice(n * wide, (n + 1) * wide)
        real, imag = joined_ref[columns, :width], joined_ref[columns, width:]
        start_panels(part, real, imag, right[...], factor[:, columns], outs, columns)
    for copy in rest:
        copy.wait()


def first_advance(level, mine, source, propagator, transmission, upgoing, part, groups):
    width = propagator.shape[3]
    shots = source.shape[3]
    chunks = shots // 2 // part
    whole = pl.BlockSpec(memory_space=pltpu.VMEM)
    pinned = [pltpu.with_memory_space_constraint(x, pltpu.HBM) for x in (source, propagator, transmission, upgoing)]
    return pl.pallas_call(
        functools.partial(first_kernel, part),
        in_specs=[pl.BlockSpec(memory_space=pltpu.SMEM)] * 2 + [pl.BlockSpec(memory_space=pltpu.HBM)] * 4,
        out_specs=[whole] * (chunks + 3),
        out_shape=[jax.ShapeDtypeStruct((2 * part, width), jnp.bfloat16)] * chunks
        + [
            pltpu.VMEM((width, 2 * width), jnp.bfloat16),
            jax.ShapeDtypeStruct((width, shots), jnp.bfloat16),
            jax.ShapeDtypeStruct((2, width // 2, shots), jnp.bfloat16),
        ],
        scratch_shapes=[
            pltpu.VMEM((width, shots), jnp.bfloat16),
            pltpu.VMEM((1, width), jnp.float32),
            pltpu.SemaphoreType.DMA((5,)),
            pltpu.SemaphoreType.DMA((4, 2)),
            pltpu.SemaphoreType.DMA((groups,)),
        ],
        compiler_params=pltpu.CompilerParams(vmem_limit_bytes=LIMIT),
        cost_estimate=pl.CostEstimate(
            flops=4 * width * width * shots, bytes_accessed=4 * width * (width + 2 * shots), transcendentals=0
        ),
    )(level, mine, *pinned)


def second_kernel(part, joined_ref, right_ref, factor_ref, *outs):
    width = joined_ref.shape[0]
    wide = width // 4
    for n in range(4):
        columns = slice(n * wide, (n + 1) * wide)
        real, imag = joined_ref[columns, :width], joined_ref[columns, width:]
        start_panels(part, real, imag, right_ref[...], factor_ref[:, columns], outs, columns)


def second_advance(joined, right, factor, part):
    width, shots = right.shape
    outs = [jax.ShapeDtypeStruct((2 * part, width), jnp.bfloat16)] * (shots // 2 // part)
    joined = pltpu.with_memory_space_constraint(joined, pltpu.VMEM)
    return whole_call(functools.partial(second_kernel, part), (joined, right, factor), outs, 4 * width * width * shots)


def advance_kernel(level_ref, arrived_ref, ready_ref, joined_ref, factor_ref, out_ref, both):
    part = arrived_ref.shape[0] // 2
    width = arrived_ref.shape[1]
    wide = width // 4

    @pl.when(level_ref[0] == 0)
    def _():
        out_ref[...] = ready_ref[...]

    @pl.when(level_ref[0] != 0)
    def _():
        both[:, :width] = arrived_ref[...]
        both[:part, width:] = -arrived_ref[part:]
        both[part:, width:] = arrived_ref[:part]
        for n in range(4):
            columns = slice(n * wide, (n + 1) * wide)
            out = lax.dot_general(
                joined_ref[columns], both[...], (((1,), (1,)), ((), ())), preferred_element_type=jnp.float32
            )
            out_ref[:, columns] = (out.T * factor_ref[:, columns]).astype(jnp.bfloat16)


def advance(level, arrived, ready, joined, factor):
    rows, width = arrived.shape
    whole = pl.BlockSpec(memory_space=pltpu.VMEM)
    return pl.pallas_call(
        advance_kernel,
        in_specs=[pl.BlockSpec(memory_space=pltpu.SMEM)] + [whole] * 4,
        out_specs=whole,
        out_shape=jax.ShapeDtypeStruct((rows, width), jnp.bfloat16),
        scratch_shapes=[pltpu.VMEM((rows, 2 * width), jnp.bfloat16)],
        compiler_params=pltpu.CompilerParams(vmem_limit_bytes=LIMIT),
        cost_estimate=pl.CostEstimate(
            flops=4 * rows * width * width, bytes_accessed=4 * width * width + 6 * rows * width, transcendentals=0
        ),
    )(level, arrived, ready, pltpu.with_memory_space_constraint(joined, pltpu.VMEM), factor)


def operand_kernel(own_ref, got_ref, out_ref):
    rows, shots = own_ref.shape[1:]
    half = shots // STREAMS
    for which, ref in enumerate((own_ref, got_ref)):
        real, imag = ref[0], ref[1]
        minus = -real
        for stream in range(STREAMS):
            lanes = slice(stream * half, (stream + 1) * half)
            left = 2 * (which * shots + stream * half)
            out_ref[:rows, left : left + half] = real[:, lanes]
            out_ref[:rows, left + half : left + 2 * half] = imag[:, lanes]
            out_ref[rows:, left : left + half] = imag[:, lanes]
            out_ref[rows:, left + half : left + 2 * half] = minus[:, lanes]


def operand(mine, own, got, rows):
    shots = own.shape[2]
    blocks = got.shape[1] // rows
    groups = blocks // 2

    def spot(i, mine_ref, stride):
        group, place, core = places(mine_ref)
        other = lax.rem(lax.div(i, groups) + core, 2)
        block = stride * lax.rem(group + lax.rem(i, groups), groups) + other
        return block + 2 * place if stride == 4 else block

    return pl.pallas_call(
        lambda _, *refs: operand_kernel(*refs),
        grid_spec=pltpu.PrefetchScalarGridSpec(
            num_scalar_prefetch=1,
            grid=(blocks,),
            in_specs=[
                pl.BlockSpec((2, rows, shots), lambda i, mine_ref: (0, spot(i, mine_ref, 4), 0)),
                pl.BlockSpec((2, rows, shots), lambda i, mine_ref: (0, spot(i, mine_ref, 2), 0)),
            ],
            out_specs=pl.BlockSpec((2 * rows, 4 * shots), lambda i, mine_ref: (i, 0)),
        ),
        out_shape=jax.ShapeDtypeStruct((2 * rows * blocks, 4 * shots), jnp.bfloat16),
        compiler_params=pltpu.CompilerParams(vmem_limit_bytes=LIMIT),
        cost_estimate=pl.CostEstimate(flops=0, bytes_accessed=24 * rows * blocks * shots, transcendentals=0),
    )(mine, own, got)


def gather(levels, level_ref, panels, joined):
    part = panels[0].shape[0] // 2
    half = STEPS * part
    first = lax.rem(levels - 1 - level_ref[0], STEPS)
    for at, panel in enumerate(panels):
        base = at // STEPS * 2 * half
        row = pl.multiple_of(lax.rem(first + at, STEPS) * part, part)
        joined[pl.ds(base + row, part)] = panel[:part]
        joined[pl.ds(base + half + row, part)] = panel[part:]


def early_kernel(levels, level_ref, left_ref, *refs):
    *panels, out_ref, joined = refs
    gather(levels, level_ref, panels, joined)
    deep = joined.shape[0]
    wide = out_ref.shape[1] // 4
    for n in range(4):
        columns = slice(n * wide, (n + 1) * wide)
        out_ref[:, columns] = jnp.dot(left_ref[:, :deep], joined[:, columns], preferred_element_type=jnp.float32)


def late_kernel(levels, level_ref, left_ref, early_ref, *refs):
    *panels, keep_ref, send_ref, joined = refs
    gather(levels, level_ref, panels, joined)
    start = left_ref.shape[1] - joined.shape[0]
    groups, _, rows, width = keep_ref.shape
    wide = width // 4
    for n in range(4):
        columns = slice(n * wide, (n + 1) * wide)
        out = early_ref[:, columns] + jnp.dot(
            left_ref[:, start:], joined[:, columns], preferred_element_type=jnp.float32
        )
        for k in range(groups):
            for part in range(2):
                lo = (2 * k + part) * rows
                keep_ref[k, part, :, columns] = out[lo : lo + rows]
                lo += 2 * groups * rows
                send_ref[k, part, :, columns] = out[lo : lo + rows].astype(jnp.bfloat16)


def whole_call(kernel, args, outs, flops, scalars=(), scratch=()):
    whole = pl.BlockSpec(memory_space=pltpu.VMEM)
    size = sum(math.prod(x.shape) * x.dtype.itemsize for x in (*args, *outs))
    return pl.pallas_call(
        kernel,
        in_specs=[pl.BlockSpec(memory_space=pltpu.SMEM)] * len(scalars) + [whole] * len(args),
        out_specs=[whole] * len(outs),
        out_shape=outs,
        scratch_shapes=scratch,
        compiler_params=pltpu.CompilerParams(vmem_limit_bytes=LIMIT),
        cost_estimate=pl.CostEstimate(flops=flops, bytes_accessed=size, transcendentals=0),
    )(*scalars, *args)


def early_terms(level, left, panels, levels):
    width = panels[0].shape[1]
    deep = sum(panel.shape[0] for panel in panels)
    out = jax.ShapeDtypeStruct((left.shape[0], width), jnp.float32)
    kernel = functools.partial(early_kernel, levels)
    scratch = [pltpu.VMEM((deep, width), jnp.bfloat16)]
    return whole_call(kernel, (left, *panels), [out], 2 * deep * left.shape[0] * width, (level,), scratch)[0]


def late_terms(level, left, early, panels, rows, levels):
    width = early.shape[1]
    deep = sum(panel.shape[0] for panel in panels)
    shape = (left.shape[0] // (4 * rows), 2, rows, width)
    outs = [jax.ShapeDtypeStruct(shape, jnp.float32), jax.ShapeDtypeStruct(shape, jnp.bfloat16)]
    kernel = functools.partial(late_kernel, levels)
    scratch = [pltpu.VMEM((deep, width), jnp.bfloat16)]
    return whole_call(kernel, (left, early, *panels), outs, 2 * deep * left.shape[0] * width, (level,), scratch)


def last_kernel(scale, *refs):
    *parts, out_ref = refs
    for part in range(2):
        total = parts[0][0, part]
        for ref in parts[1:]:
            total += ref[0, part].astype(jnp.float32)
        out_ref[0, :, part] = total * scale


def last_sum(parts, scale):
    rows, width = parts[0].shape[2:]
    out = jax.ShapeDtypeStruct((1, rows, 2, width), jnp.float32)
    return whole_call(functools.partial(last_kernel, scale), parts, [out], 2 * len(parts) * rows * width)[0]


def shards(source, propagator, transmission, upgoing):
    factor = transmission[0]
    upward = upgoing[0, 0]
    width = propagator.shape[3]
    shots = source.shape[3]
    levels = lax.axis_size("depth")
    freqs = lax.axis_size("freq")
    groups = freqs // 4
    rows = width // freqs
    part = shots // STREAMS // STEPS
    level, mine = (lax.axis_index(axis).astype(jnp.int32).reshape(1) for axis in ("depth", "freq"))
    *ready, joined, later, asked = first_advance(level, mine, source, propagator, transmission, upgoing, part, groups)
    ready = [ready, second_advance(joined, later, factor, part)]
    got = swapped(asked, "freq", 2)
    left = operand(mine, upward, got, rows)

    steps = STEPS + levels - 1
    flying = [None] * STREAMS
    own = [[] for _ in range(STREAMS)]
    other = [[] for _ in range(STREAMS)]
    waiting = []
    crossing = []
    for event in range(STREAMS * steps):
        step, stream = divmod(event, STREAMS)
        out = ready[stream][step % STEPS]
        if step >= 1:
            arrived = flying[stream]
            if event == steps:
                arrived, left = lax.optimization_barrier((arrived, left))
            if waiting:
                which, panel = waiting.pop()
                panel, arrived = lax.optimization_barrier((panel, arrived))
                crossing.append((which, len(other[which])))
                other[which].append(swapped(panel, "freq", 2))
            if len(crossing) > BEHIND:
                which, at = crossing.pop(0)
                arrived, other[which][at] = lax.optimization_barrier((arrived, other[which][at]))
            out = advance(level, arrived, out, joined, factor)
        if step + 1 < steps:
            flying[stream] = ring(out, "depth", 1)
        if step >= levels - 1:
            own[stream].append(out)
            waiting.append((stream, out))
    which, panel = waiting.pop()
    other[which].append(swapped(panel, "freq", 2))
    early = early_terms(level, left, own[0] + own[1] + other[0], levels)
    keep, send = late_terms(level, left, early, other[1], rows, levels)
    near = swapped(send, "freq", 1)
    parts = [keep, near]
    for k in range(1, groups):
        total = (keep[k : k + 1] + near[k : k + 1].astype(jnp.float32)).astype(jnp.bfloat16)
        parts.append(ring(total, "freq", 4 * k))
    return last_sum(parts, (2.0 * shots * freqs) ** (-0.5))


def solution(mesh):
    return jax.shard_map(
        shards,
        mesh=mesh,
        in_specs=(
            P("freq", None, None, None),
            P("depth", "freq", None, None, None),
            P("depth", "freq", None),
            P("depth", "freq", None, None, None),
        ),
        out_specs=P("depth", "freq", None, None),
        check_vma=False,
    )
```

```python
import functools
import math

import jax
import jax.numpy as jnp
from jax import lax
from jax.experimental import pallas as pl
from jax.experimental.pallas import tpu as pltpu
from jax.sharding import PartitionSpec as P

STEPS = 4
STREAMS = 2
BEHIND = 3
LIMIT = 16 * 1024 * 1024


def ring(block, axis, distance):
    size = lax.axis_size(axis)
    return lax.ppermute(block, axis, [(i, (i + distance) % size) for i in range(size)])


def swapped(block, axis, bit):
    return lax.ppermute(block, axis, [(i, i ^ bit) for i in range(lax.axis_size(axis))])


def places(mine_ref):
    mine = mine_ref[0]
    return lax.div(mine, 4), lax.rem(lax.div(mine, 2), 2), lax.rem(mine, 2)


def start_panels(part, real, imag, right, factor, outs, columns):
    dot = functools.partial(jnp.dot, preferred_element_type=jnp.float32)
    shots = right.shape[1] // 2
    first, second = dot(real, right), dot(imag, right)
    out_real = ((first[:, :shots] - second[:, shots:]).T * factor).astype(jnp.bfloat16)
    out_imag = ((first[:, shots:] + second[:, :shots]).T * factor).astype(jnp.bfloat16)
    for chunk, out in enumerate(outs):
        lo = chunk * part
        out[:part, columns] = out_real[lo : lo + part]
        out[part:, columns] = out_imag[lo : lo + part]


def first_kernel(part, level_ref, mine_ref, source_ref, weight_ref, factor_ref, upward_ref, *refs):
    *outs, joined_ref, later_ref, asked_ref, right, factor, sem, sems, asked_sems = refs
    width = joined_ref.shape[0]
    shots = later_ref.shape[1] // 2
    blocks = sems.shape[0]
    wide = width // blocks
    groups = asked_sems.shape[0]
    tall = asked_ref.shape[1] // groups
    _, place, _ = places(mine_ref)

    def copies(n):
        rows = pl.ds(n * wide, wide)
        return [
            pltpu.make_async_copy(
                weight_ref.at[0, 0, half, rows], joined_ref.at[rows, pl.ds(half * width, width)], sems.at[n, half]
            )
            for half in range(2)
        ]

    def columns_of(start, to_ref, first_sem):
        return [
            pltpu.make_async_copy(
                source_ref.at[0, half, :, pl.ds(start, shots)],
                to_ref.at[:, pl.ds(half * shots, shots)],
                sem.at[first_sem + half],
            )
            for half in range(2)
        ]

    begin = columns_of(0, right, 0) + [pltpu.make_async_copy(factor_ref.at[0], factor, sem.at[4])]
    rest = columns_of(shots, later_ref, 2)
    for k in range(groups):
        row = pl.multiple_of((2 * k + 1 - place) * tall, tall)
        rest.append(
            pltpu.make_async_copy(
                upward_ref.at[0, 0, :, pl.ds(row, tall)], asked_ref.at[:, pl.ds(k * tall, tall)], asked_sems.at[k]
            )
        )
    for copy in begin:
        copy.start()
    for n in range(blocks):
        for copy in copies(n):
            copy.start()
    for copy in rest:
        copy.start()
    for copy in begin:
        copy.wait()
    for n in range(blocks):
        for copy in copies(n):
            copy.wait()
        columns = slice(n * wide, (n + 1) * wide)
        real, imag = joined_ref[columns, :width], joined_ref[columns, width:]
        start_panels(part, real, imag, right[...], factor[:, columns], outs, columns)
    for copy in rest:
        copy.wait()


def first_advance(level, mine, source, propagator, transmission, upgoing, part, groups):
    width = propagator.shape[3]
    shots = source.shape[3]
    chunks = shots // 2 // part
    whole = pl.BlockSpec(memory_space=pltpu.VMEM)
    pinned = [pltpu.with_memory_space_constraint(x, pltpu.HBM) for x in (source, propagator, transmission, upgoing)]
    return pl.pallas_call(
        functools.partial(first_kernel, part),
        in_specs=[pl.BlockSpec(memory_space=pltpu.SMEM)] * 2 + [pl.BlockSpec(memory_space=pltpu.HBM)] * 4,
        out_specs=[whole] * (chunks + 3),
        out_shape=[jax.ShapeDtypeStruct((2 * part, width), jnp.bfloat16)] * chunks
        + [
            pltpu.VMEM((width, 2 * width), jnp.bfloat16),
            jax.ShapeDtypeStruct((width, shots), jnp.bfloat16),
            jax.ShapeDtypeStruct((2, width // 2, shots), jnp.bfloat16),
        ],
        scratch_shapes=[
            pltpu.VMEM((width, shots), jnp.bfloat16),
            pltpu.VMEM((1, width), jnp.float32),
            pltpu.SemaphoreType.DMA((5,)),
            pltpu.SemaphoreType.DMA((4, 2)),
            pltpu.SemaphoreType.DMA((groups,)),
        ],
        compiler_params=pltpu.CompilerParams(vmem_limit_bytes=LIMIT),
        cost_estimate=pl.CostEstimate(
            flops=4 * width * width * shots, bytes_accessed=4 * width * (width + 2 * shots), transcendentals=0
        ),
    )(level, mine, *pinned)


def second_kernel(part, joined_ref, right_ref, factor_ref, *outs):
    width = joined_ref.shape[0]
    wide = width // 4
    for n in range(4):
        columns = slice(n * wide, (n + 1) * wide)
        real, imag = joined_ref[columns, :width], joined_ref[columns, width:]
        start_panels(part, real, imag, right_ref[...], factor_ref[:, columns], outs, columns)


def second_advance(joined, right, factor, part):
    width, shots = right.shape
    outs = [jax.ShapeDtypeStruct((2 * part, width), jnp.bfloat16)] * (shots // 2 // part)
    joined = pltpu.with_memory_space_constraint(joined, pltpu.VMEM)
    return whole_call(functools.partial(second_kernel, part), (joined, right, factor), outs, 4 * width * width * shots)


def advance_kernel(level_ref, arrived_ref, ready_ref, joined_ref, factor_ref, *refs):
    *mates, both = refs
    out_ref = mates[0] if len(mates) == 1 else mates[1]
    part = arrived_ref.shape[0] // 2
    width = arrived_ref.shape[1]
    wide = width // 4

    @pl.when(level_ref[0] == 0)
    def _():
        out_ref[...] = ready_ref[...]

    @pl.when(level_ref[0] != 0)
    def _():
        both[:, :width] = arrived_ref[...]
        both[:part, width:] = -arrived_ref[part:]
        both[part:, width:] = arrived_ref[:part]
        for n in range(4):
            columns = slice(n * wide, (n + 1) * wide)
            out = lax.dot_general(
                joined_ref[columns], both[...], (((1,), (1,)), ((), ())), preferred_element_type=jnp.float32
            )
            out_ref[:, columns] = (out.T * factor_ref[:, columns]).astype(jnp.bfloat16)

    if len(mates) > 1:
        mates[2][: 2 * part] = mates[0][...]
        mates[2][2 * part :] = out_ref[...]


def advance(level, arrived, ready, joined, factor, mate=None):
    rows, width = arrived.shape
    joined = pltpu.with_memory_space_constraint(joined, pltpu.VMEM)
    outs = [jax.ShapeDtypeStruct((rows, width), jnp.bfloat16)]
    args = [arrived, ready, joined, factor]
    if mate is not None:
        outs.append(jax.ShapeDtypeStruct((2 * rows, width), jnp.bfloat16))
        args.append(mate)
    scratch = [pltpu.VMEM((rows, 2 * width), jnp.bfloat16)]
    return whole_call(advance_kernel, args, outs, 4 * rows * width * width, (level,), scratch)


def operand_kernel(own_ref, got_ref, out_ref):
    rows, shots = own_ref.shape[1:]
    half = shots // STREAMS
    for which, ref in enumerate((own_ref, got_ref)):
        real, imag = ref[0], ref[1]
        minus = -real
        for stream in range(STREAMS):
            lanes = slice(stream * half, (stream + 1) * half)
            left = 2 * (which * shots + stream * half)
            out_ref[:rows, left : left + half] = real[:, lanes]
            out_ref[:rows, left + half : left + 2 * half] = imag[:, lanes]
            out_ref[rows:, left : left + half] = imag[:, lanes]
            out_ref[rows:, left + half : left + 2 * half] = minus[:, lanes]


def operand(mine, own, got, rows):
    shots = own.shape[2]
    blocks = got.shape[1] // rows
    groups = blocks // 2

    def spot(i, mine_ref, stride):
        group, place, core = places(mine_ref)
        other = lax.rem(lax.div(i, groups) + core, 2)
        block = stride * lax.rem(group + lax.rem(i, groups), groups) + other
        return block + 2 * place if stride == 4 else block

    return pl.pallas_call(
        lambda _, *refs: operand_kernel(*refs),
        grid_spec=pltpu.PrefetchScalarGridSpec(
            num_scalar_prefetch=1,
            grid=(blocks,),
            in_specs=[
                pl.BlockSpec((2, rows, shots), lambda i, mine_ref: (0, spot(i, mine_ref, 4), 0)),
                pl.BlockSpec((2, rows, shots), lambda i, mine_ref: (0, spot(i, mine_ref, 2), 0)),
            ],
            out_specs=pl.BlockSpec((2 * rows, 4 * shots), lambda i, mine_ref: (i, 0)),
        ),
        out_shape=jax.ShapeDtypeStruct((2 * rows * blocks, 4 * shots), jnp.bfloat16),
        compiler_params=pltpu.CompilerParams(vmem_limit_bytes=LIMIT),
        cost_estimate=pl.CostEstimate(flops=0, bytes_accessed=24 * rows * blocks * shots, transcendentals=0),
    )(mine, own, got)


def gather(levels, level_ref, panels, joined):
    part = joined.shape[0] // len(panels) // 2
    half = STEPS * part
    first = lax.rem(levels - 1 - level_ref[0], STEPS)
    for at, (ref, top) in enumerate(panels):
        base = at // STEPS * 2 * half
        row = pl.multiple_of(lax.rem(first + at, STEPS) * part, part)
        joined[pl.ds(base + row, part)] = ref[top : top + part]
        joined[pl.ds(base + half + row, part)] = ref[top + part : top + 2 * part]


def crossed(refs, stream):
    *pairs, last = refs
    rows = last.shape[0]
    return [(pair, stream * rows) for pair in pairs] + [(last, 0)]


def early_kernel(levels, level_ref, left_ref, *refs):
    *panels, out_ref, joined = refs
    own, other = panels[: STREAMS * STEPS], panels[STREAMS * STEPS :]
    gather(levels, level_ref, [(ref, 0) for ref in own] + crossed(other, 0), joined)
    deep = joined.shape[0]
    wide = out_ref.shape[1] // 4
    for n in range(4):
        columns = slice(n * wide, (n + 1) * wide)
        out_ref[:, columns] = jnp.dot(left_ref[:, :deep], joined[:, columns], preferred_element_type=jnp.float32)


def late_kernel(levels, level_ref, left_ref, early_ref, *refs):
    *panels, keep_ref, send_ref, joined = refs
    gather(levels, level_ref, crossed(panels, 1), joined)
    start = left_ref.shape[1] - joined.shape[0]
    groups, _, rows, width = keep_ref.shape
    wide = width // 4
    for n in range(4):
        columns = slice(n * wide, (n + 1) * wide)
        out = early_ref[:, columns] + jnp.dot(
            left_ref[:, start:], joined[:, columns], preferred_element_type=jnp.float32
        )
        for k in range(groups):
            for part in range(2):
                lo = (2 * k + part) * rows
                keep_ref[k, part, :, columns] = out[lo : lo + rows]
                lo += 2 * groups * rows
                send_ref[k, part, :, columns] = out[lo : lo + rows].astype(jnp.bfloat16)


def whole_call(kernel, args, outs, flops, scalars=(), scratch=()):
    whole = pl.BlockSpec(memory_space=pltpu.VMEM)
    size = sum(math.prod(x.shape) * x.dtype.itemsize for x in (*args, *outs))
    return pl.pallas_call(
        kernel,
        in_specs=[pl.BlockSpec(memory_space=pltpu.SMEM)] * len(scalars) + [whole] * len(args),
        out_specs=[whole] * len(outs),
        out_shape=outs,
        scratch_shapes=scratch,
        compiler_params=pltpu.CompilerParams(vmem_limit_bytes=LIMIT),
        cost_estimate=pl.CostEstimate(flops=flops, bytes_accessed=size, transcendentals=0),
    )(*scalars, *args)


def early_terms(level, left, panels, levels):
    width = panels[0].shape[1]
    deep = left.shape[1] - panels[-1].shape[0] * STEPS
    out = jax.ShapeDtypeStruct((left.shape[0], width), jnp.float32)
    kernel = functools.partial(early_kernel, levels)
    scratch = [pltpu.VMEM((deep, width), jnp.bfloat16)]
    return whole_call(kernel, (left, *panels), [out], 2 * deep * left.shape[0] * width, (level,), scratch)[0]


def late_terms(level, left, early, panels, rows, levels):
    width = early.shape[1]
    deep = panels[-1].shape[0] * STEPS
    shape = (left.shape[0] // (4 * rows), 2, rows, width)
    outs = [jax.ShapeDtypeStruct(shape, jnp.float32), jax.ShapeDtypeStruct(shape, jnp.bfloat16)]
    kernel = functools.partial(late_kernel, levels)
    scratch = [pltpu.VMEM((deep, width), jnp.bfloat16)]
    return whole_call(kernel, (left, early, *panels), outs, 2 * deep * left.shape[0] * width, (level,), scratch)


def last_kernel(scale, *refs):
    *parts, out_ref = refs
    for part in range(2):
        total = parts[0][0, part]
        for ref in parts[1:]:
            total += ref[0, part].astype(jnp.float32)
        out_ref[0, :, part] = total * scale


def last_sum(parts, scale):
    rows, width = parts[0].shape[2:]
    out = jax.ShapeDtypeStruct((1, rows, 2, width), jnp.float32)
    return whole_call(functools.partial(last_kernel, scale), parts, [out], 2 * len(parts) * rows * width)[0]


def shards(source, propagator, transmission, upgoing):
    factor = transmission[0]
    upward = upgoing[0, 0]
    width = propagator.shape[3]
    shots = source.shape[3]
    levels = lax.axis_size("depth")
    freqs = lax.axis_size("freq")
    groups = freqs // 4
    rows = width // freqs
    part = shots // STREAMS // STEPS
    level, mine = (lax.axis_index(axis).astype(jnp.int32).reshape(1) for axis in ("depth", "freq"))
    *ready, joined, later, asked = first_advance(level, mine, source, propagator, transmission, upgoing, part, groups)
    ready = [ready, second_advance(joined, later, factor, part)]
    got = swapped(asked, "freq", 2)
    left = operand(mine, upward, got, rows)

    steps = STEPS + levels - 1
    flying = [None] * STREAMS
    own = [[] for _ in range(STREAMS)]
    waiting = []
    crossing = []
    for event in range(STREAMS * steps):
        step, stream = divmod(event, STREAMS)
        out = ready[stream][step % STEPS]
        if step >= 1:
            arrived = flying[stream]
            if event == steps:
                arrived, left = lax.optimization_barrier((arrived, left))
            if waiting:
                panel, arrived = lax.optimization_barrier((waiting.pop(), arrived))
                crossing.append((event, swapped(panel, "freq", 2)))
            for at, (sent, panel) in enumerate(crossing):
                if event == sent + BEHIND:
                    arrived, panel = lax.optimization_barrier((arrived, panel))
                    crossing[at] = (sent, panel)
            pair = stream > 0 and levels - 1 <= step < steps - 1
            out, *both = advance(level, arrived, out, joined, factor, own[0][-1] if pair else None)
            if step >= levels - 1 and (pair or step == steps - 1):
                waiting.append(both[0] if pair else out)
        if step + 1 < steps:
            flying[stream] = ring(out, "depth", 1)
        if step >= levels - 1:
            own[stream].append(out)
    other = [panel for _, panel in crossing] + [swapped(waiting.pop(), "freq", 2)]
    early = early_terms(level, left, own[0] + own[1] + other[:-1], levels)
    keep, send = late_terms(level, left, early, other[:-2] + other[-1:], rows, levels)
    near = swapped(send, "freq", 1)
    parts = [keep, near]
    for k in range(1, groups):
        total = (keep[k : k + 1] + near[k : k + 1].astype(jnp.float32)).astype(jnp.bfloat16)
        parts.append(ring(total, "freq", 4 * k))
    return last_sum(parts, (2.0 * shots * freqs) ** (-0.5))


def solution(mesh):
    return jax.shard_map(
        shards,
        mesh=mesh,
        in_specs=(
            P("freq", None, None, None),
            P("depth", "freq", None, None, None),
            P("depth", "freq", None),
            P("depth", "freq", None, None, None),
        ),
        out_specs=P("depth", "freq", None, None),
        check_vma=False,
    )
```

```python
import functools
import math

import jax
import jax.numpy as jnp
from jax import lax
from jax.experimental import pallas as pl
from jax.experimental.pallas import tpu as pltpu
from jax.sharding import PartitionSpec as P

STEPS = 4
STREAMS = 2
BEHIND = 3
LIMIT = 16 * 1024 * 1024


def ring(block, axis, distance):
    size = lax.axis_size(axis)
    return lax.ppermute(block, axis, [(i, (i + distance) % size) for i in range(size)])


def swapped(block, axis, bit):
    return lax.ppermute(block, axis, [(i, i ^ bit) for i in range(lax.axis_size(axis))])


def places(mine_ref):
    mine = mine_ref[0]
    return lax.div(mine, 4), lax.rem(lax.div(mine, 2), 2), lax.rem(mine, 2)


def start_panels(part, real, imag, right, factor, outs, columns):
    dot = functools.partial(jnp.dot, preferred_element_type=jnp.float32)
    shots = right.shape[1] // 2
    first, second = dot(real, right), dot(imag, right)
    out_real = ((first[:, :shots] - second[:, shots:]).T * factor).astype(jnp.bfloat16)
    out_imag = ((first[:, shots:] + second[:, :shots]).T * factor).astype(jnp.bfloat16)
    for chunk, out in enumerate(outs):
        lo = chunk * part
        out[:part, columns] = out_real[lo : lo + part]
        out[part:, columns] = out_imag[lo : lo + part]


def first_kernel(part, level_ref, mine_ref, source_ref, weight_ref, factor_ref, upward_ref, *refs):
    *outs, joined_ref, later_ref, asked_ref, right, factor, sem, sems, asked_sems = refs
    width = joined_ref.shape[0]
    shots = later_ref.shape[1] // 2
    blocks = sems.shape[0]
    wide = width // blocks
    groups = asked_sems.shape[0]
    tall = asked_ref.shape[1] // groups
    _, place, _ = places(mine_ref)

    def copies(n):
        rows = pl.ds(n * wide, wide)
        return [
            pltpu.make_async_copy(
                weight_ref.at[0, 0, half, rows], joined_ref.at[rows, pl.ds(half * width, width)], sems.at[n, half]
            )
            for half in range(2)
        ]

    def columns_of(start, to_ref, first_sem):
        return [
            pltpu.make_async_copy(
                source_ref.at[0, half, :, pl.ds(start, shots)],
                to_ref.at[:, pl.ds(half * shots, shots)],
                sem.at[first_sem + half],
            )
            for half in range(2)
        ]

    begin = columns_of(0, right, 0) + [pltpu.make_async_copy(factor_ref.at[0], factor, sem.at[4])]
    rest = columns_of(shots, later_ref, 2)
    for k in range(groups):
        row = pl.multiple_of((2 * k + 1 - place) * tall, tall)
        rest.append(
            pltpu.make_async_copy(
                upward_ref.at[0, 0, :, pl.ds(row, tall)], asked_ref.at[:, pl.ds(k * tall, tall)], asked_sems.at[k]
            )
        )
    for copy in begin:
        copy.start()
    for n in range(blocks):
        for copy in copies(n):
            copy.start()
    for copy in rest:
        copy.start()
    for copy in begin:
        copy.wait()
    for n in range(blocks):
        for copy in copies(n):
            copy.wait()
        columns = slice(n * wide, (n + 1) * wide)
        real, imag = joined_ref[columns, :width], joined_ref[columns, width:]
        start_panels(part, real, imag, right[...], factor[:, columns], outs, columns)
    for copy in rest:
        copy.wait()


def first_advance(level, mine, source, propagator, transmission, upgoing, part, groups):
    width = propagator.shape[3]
    shots = source.shape[3]
    chunks = shots // 2 // part
    whole = pl.BlockSpec(memory_space=pltpu.VMEM)
    pinned = [pltpu.with_memory_space_constraint(x, pltpu.HBM) for x in (source, propagator, transmission, upgoing)]
    return pl.pallas_call(
        functools.partial(first_kernel, part),
        in_specs=[pl.BlockSpec(memory_space=pltpu.SMEM)] * 2 + [pl.BlockSpec(memory_space=pltpu.HBM)] * 4,
        out_specs=[whole] * (chunks + 3),
        out_shape=[jax.ShapeDtypeStruct((2 * part, width), jnp.bfloat16)] * chunks
        + [
            pltpu.VMEM((width, 2 * width), jnp.bfloat16),
            jax.ShapeDtypeStruct((width, shots), jnp.bfloat16),
            jax.ShapeDtypeStruct((2, width // 2, shots), jnp.bfloat16),
        ],
        scratch_shapes=[
            pltpu.VMEM((width, shots), jnp.bfloat16),
            pltpu.VMEM((1, width), jnp.float32),
            pltpu.SemaphoreType.DMA((5,)),
            pltpu.SemaphoreType.DMA((4, 2)),
            pltpu.SemaphoreType.DMA((groups,)),
        ],
        compiler_params=pltpu.CompilerParams(vmem_limit_bytes=LIMIT),
        cost_estimate=pl.CostEstimate(
            flops=4 * width * width * shots, bytes_accessed=4 * width * (width + 2 * shots), transcendentals=0
        ),
    )(level, mine, *pinned)


def second_kernel(part, joined_ref, right_ref, factor_ref, *outs):
    width = joined_ref.shape[0]
    wide = width // 4
    for n in range(4):
        columns = slice(n * wide, (n + 1) * wide)
        real, imag = joined_ref[columns, :width], joined_ref[columns, width:]
        start_panels(part, real, imag, right_ref[...], factor_ref[:, columns], outs, columns)


def second_advance(joined, right, factor, part):
    width, shots = right.shape
    outs = [jax.ShapeDtypeStruct((2 * part, width), jnp.bfloat16)] * (shots // 2 // part)
    joined = pltpu.with_memory_space_constraint(joined, pltpu.VMEM)
    return whole_call(functools.partial(second_kernel, part), (joined, right, factor), outs, 4 * width * width * shots)


def advance_kernel(level_ref, arrived_ref, ready_ref, joined_ref, factor_ref, *refs):
    *mates, both = refs
    out_ref = mates[0] if len(mates) == 1 else mates[1]
    part = arrived_ref.shape[0] // 2
    width = arrived_ref.shape[1]
    wide = width // 4

    @pl.when(level_ref[0] == 0)
    def _():
        out_ref[...] = ready_ref[...]

    @pl.when(level_ref[0] != 0)
    def _():
        both[:, :width] = arrived_ref[...]
        both[:part, width:] = -arrived_ref[part:]
        both[part:, width:] = arrived_ref[:part]
        for n in range(4):
            columns = slice(n * wide, (n + 1) * wide)
            out = lax.dot_general(
                joined_ref[columns], both[...], (((1,), (1,)), ((), ())), preferred_element_type=jnp.float32
            )
            out_ref[:, columns] = (out.T * factor_ref[:, columns]).astype(jnp.bfloat16)

    if len(mates) > 1:
        mates[2][: 2 * part] = mates[0][...]
        mates[2][2 * part :] = out_ref[...]


def advance(level, arrived, ready, joined, factor, mate=None):
    rows, width = arrived.shape
    joined = pltpu.with_memory_space_constraint(joined, pltpu.VMEM)
    outs = [jax.ShapeDtypeStruct((rows, width), jnp.bfloat16)]
    args = [arrived, ready, joined, factor]
    if mate is not None:
        outs.append(jax.ShapeDtypeStruct((2 * rows, width), jnp.bfloat16))
        args.append(mate)
    scratch = [pltpu.VMEM((rows, 2 * width), jnp.bfloat16)]
    return whole_call(advance_kernel, args, outs, 4 * rows * width * width, (level,), scratch)


def operand_kernel(own_ref, got_ref, out_ref):
    rows, shots = own_ref.shape[1:]
    half = shots // STREAMS
    for which, ref in enumerate((own_ref, got_ref)):
        real, imag = ref[0], ref[1]
        minus = -real
        for stream in range(STREAMS):
            lanes = slice(stream * half, (stream + 1) * half)
            left = 2 * (which * shots + stream * half)
            out_ref[:rows, left : left + half] = real[:, lanes]
            out_ref[:rows, left + half : left + 2 * half] = imag[:, lanes]
            out_ref[rows:, left : left + half] = imag[:, lanes]
            out_ref[rows:, left + half : left + 2 * half] = minus[:, lanes]


def operand(mine, own, got, rows):
    shots = own.shape[2]
    blocks = got.shape[1] // rows
    groups = blocks // 2

    def spot(i, mine_ref, stride):
        group, place, core = places(mine_ref)
        other = lax.rem(lax.div(i, groups) + core, 2)
        block = stride * lax.rem(group + lax.rem(i, groups), groups) + other
        return block + 2 * place if stride == 4 else block

    return pl.pallas_call(
        lambda _, *refs: operand_kernel(*refs),
        grid_spec=pltpu.PrefetchScalarGridSpec(
            num_scalar_prefetch=1,
            grid=(blocks,),
            in_specs=[
                pl.BlockSpec((2, rows, shots), lambda i, mine_ref: (0, spot(i, mine_ref, 4), 0)),
                pl.BlockSpec((2, rows, shots), lambda i, mine_ref: (0, spot(i, mine_ref, 2), 0)),
            ],
            out_specs=pl.BlockSpec((2 * rows, 4 * shots), lambda i, mine_ref: (i, 0)),
        ),
        out_shape=jax.ShapeDtypeStruct((2 * rows * blocks, 4 * shots), jnp.bfloat16),
        compiler_params=pltpu.CompilerParams(vmem_limit_bytes=LIMIT),
        cost_estimate=pl.CostEstimate(flops=0, bytes_accessed=24 * rows * blocks * shots, transcendentals=0),
    )(mine, own, got)


def gather(levels, level_ref, panels, joined):
    part = joined.shape[0] // len(panels) // 2
    half = STEPS * part
    first = lax.rem(levels - 1 - level_ref[0], STEPS)
    for at, (ref, top) in enumerate(panels):
        base = at // STEPS * 2 * half
        row = pl.multiple_of(lax.rem(first + at, STEPS) * part, part)
        joined[pl.ds(base + row, part)] = ref[top : top + part]
        joined[pl.ds(base + half + row, part)] = ref[top + part : top + 2 * part]


def crossed(refs, stream):
    *pairs, last = refs
    rows = last.shape[0]
    return [(pair, stream * rows) for pair in pairs] + [(last, 0)]


def early_kernel(levels, level_ref, left_ref, *refs):
    *panels, out_ref, joined = refs
    own, other = panels[: STREAMS * STEPS], panels[STREAMS * STEPS :]
    gather(levels, level_ref, [(ref, 0) for ref in own] + crossed(other, 0), joined)
    deep = joined.shape[0]
    wide = out_ref.shape[1] // 4
    for n in range(4):
        columns = slice(n * wide, (n + 1) * wide)
        out_ref[:, columns] = jnp.dot(left_ref[:, :deep], joined[:, columns], preferred_element_type=jnp.float32)


def late_kernel(levels, level_ref, left_ref, early_ref, *refs):
    *panels, keep_ref, send_ref, joined = refs
    gather(levels, level_ref, crossed(panels, 1), joined)
    start = left_ref.shape[1] - joined.shape[0]
    groups, _, rows, width = keep_ref.shape
    wide = width // 4
    for n in range(4):
        columns = slice(n * wide, (n + 1) * wide)
        out = early_ref[:, columns] + jnp.dot(
            left_ref[:, start:], joined[:, columns], preferred_element_type=jnp.float32
        )
        for k in range(groups):
            for part in range(2):
                lo = (2 * k + part) * rows
                keep_ref[k, part, :, columns] = out[lo : lo + rows]
                lo += 2 * groups * rows
                send_ref[k, part, :, columns] = out[lo : lo + rows].astype(jnp.bfloat16)


def whole_call(kernel, args, outs, flops, scalars=(), scratch=()):
    whole = pl.BlockSpec(memory_space=pltpu.VMEM)
    size = sum(math.prod(x.shape) * x.dtype.itemsize for x in (*args, *outs))
    return pl.pallas_call(
        kernel,
        in_specs=[pl.BlockSpec(memory_space=pltpu.SMEM)] * len(scalars) + [whole] * len(args),
        out_specs=[whole] * len(outs),
        out_shape=outs,
        scratch_shapes=scratch,
        compiler_params=pltpu.CompilerParams(vmem_limit_bytes=LIMIT),
        cost_estimate=pl.CostEstimate(flops=flops, bytes_accessed=size, transcendentals=0),
    )(*scalars, *args)


def early_terms(level, left, panels, levels):
    width = panels[0].shape[1]
    deep = left.shape[1] - panels[-1].shape[0] * STEPS
    out = jax.ShapeDtypeStruct((left.shape[0], width), jnp.float32)
    kernel = functools.partial(early_kernel, levels)
    scratch = [pltpu.VMEM((deep, width), jnp.bfloat16)]
    return whole_call(kernel, (left, *panels), [out], 2 * deep * left.shape[0] * width, (level,), scratch)[0]


def late_terms(level, left, early, panels, rows, levels):
    width = early.shape[1]
    deep = panels[-1].shape[0] * STEPS
    shape = (left.shape[0] // (4 * rows), 2, rows, width)
    outs = [jax.ShapeDtypeStruct(shape, jnp.float32), jax.ShapeDtypeStruct(shape, jnp.bfloat16)]
    kernel = functools.partial(late_kernel, levels)
    scratch = [pltpu.VMEM((deep, width), jnp.bfloat16)]
    return whole_call(kernel, (left, early, *panels), outs, 2 * deep * left.shape[0] * width, (level,), scratch)


def last_kernel(scale, *refs):
    *parts, out_ref = refs
    for part in range(2):
        total = parts[0][0, part]
        for ref in parts[1:]:
            total += ref[0, part].astype(jnp.float32)
        out_ref[0, :, part] = total * scale


def last_sum(parts, scale):
    rows, width = parts[0].shape[2:]
    out = jax.ShapeDtypeStruct((1, rows, 2, width), jnp.float32)
    return whole_call(functools.partial(last_kernel, scale), parts, [out], 2 * len(parts) * rows * width)[0]


def shards(source, propagator, transmission, upgoing):
    factor = transmission[0]
    upward = upgoing[0, 0]
    width = propagator.shape[3]
    shots = source.shape[3]
    levels = lax.axis_size("depth")
    freqs = lax.axis_size("freq")
    groups = freqs // 4
    rows = width // freqs
    part = shots // STREAMS // STEPS
    level, mine = (lax.axis_index(axis).astype(jnp.int32).reshape(1) for axis in ("depth", "freq"))
    *ready, joined, later, asked = first_advance(level, mine, source, propagator, transmission, upgoing, part, groups)
    ready = [ready, second_advance(joined, later, factor, part)]
    got = swapped(asked, "freq", 2)
    left = operand(mine, upward, got, rows)

    steps = STEPS + levels - 1
    flying = [None] * STREAMS
    own = [[] for _ in range(STREAMS)]
    crossing = []
    for event in range(STREAMS * steps):
        step, stream = divmod(event, STREAMS)
        out = ready[stream][step % STEPS]
        if step >= 1:
            arrived = flying[stream]
            if event == steps:
                arrived, left = lax.optimization_barrier((arrived, left))
            for at, (sent, panel) in enumerate(crossing):
                if event == sent + BEHIND:
                    arrived, panel = lax.optimization_barrier((arrived, panel))
                    crossing[at] = (sent, panel)
            pair = stream > 0 and levels - 1 <= step < steps - 1
            out, *both = advance(level, arrived, out, joined, factor, own[0][-1] if pair else None)
            if step >= levels - 1 and (pair or step == steps - 1):
                crossing.append((event, swapped(both[0] if pair else out, "freq", 2)))
        if step + 1 < steps:
            flying[stream] = ring(out, "depth", 1)
        if step >= levels - 1:
            own[stream].append(out)
    other = [panel for _, panel in crossing]
    early = early_terms(level, left, own[0] + own[1] + other[:-1], levels)
    keep, send = late_terms(level, left, early, other[:-2] + other[-1:], rows, levels)
    near = swapped(send, "freq", 1)
    parts = [keep, near]
    for k in range(1, groups):
        total = (keep[k : k + 1] + near[k : k + 1].astype(jnp.float32)).astype(jnp.bfloat16)
        parts.append(ring(total, "freq", 4 * k))
    return last_sum(parts, (2.0 * shots * freqs) ** (-0.5))


def solution(mesh):
    return jax.shard_map(
        shards,
        mesh=mesh,
        in_specs=(
            P("freq", None, None, None),
            P("depth", "freq", None, None, None),
            P("depth", "freq", None),
            P("depth", "freq", None, None, None),
        ),
        out_specs=P("depth", "freq", None, None),
        check_vma=False,
    )
```

```python
import functools
import math

import jax
import jax.numpy as jnp
from jax import lax
from jax.experimental import pallas as pl
from jax.experimental.pallas import tpu as pltpu
from jax.sharding import PartitionSpec as P

STEPS = 4
STREAMS = 2
BEHIND = 3
LIMIT = 16 * 1024 * 1024


def ring(block, axis, distance):
    size = lax.axis_size(axis)
    return lax.ppermute(block, axis, [(i, (i + distance) % size) for i in range(size)])


def swapped(block, axis, bit):
    return lax.ppermute(block, axis, [(i, i ^ bit) for i in range(lax.axis_size(axis))])


def places(mine_ref):
    mine = mine_ref[0]
    return lax.div(mine, 4), lax.rem(lax.div(mine, 2), 2), lax.rem(mine, 2)


def start_panels(part, real, imag, right, factor, outs, columns):
    dot = functools.partial(jnp.dot, preferred_element_type=jnp.float32)
    shots = right.shape[1] // 2
    first, second = dot(real, right), dot(imag, right)
    out_real = ((first[:, :shots] - second[:, shots:]).T * factor).astype(jnp.bfloat16)
    out_imag = ((first[:, shots:] + second[:, :shots]).T * factor).astype(jnp.bfloat16)
    for chunk, out in enumerate(outs):
        lo = chunk * part
        out[:part, columns] = out_real[lo : lo + part]
        out[part:, columns] = out_imag[lo : lo + part]


def first_kernel(part, level_ref, mine_ref, source_ref, weight_ref, factor_ref, upward_ref, *refs):
    *outs, joined_ref, later_ref, asked_ref, right, factor, sem, sems, asked_sems = refs
    width = joined_ref.shape[0]
    shots = later_ref.shape[1] // 2
    blocks = sems.shape[0]
    wide = width // blocks
    groups = asked_sems.shape[0]
    tall = asked_ref.shape[1] // groups
    _, place, _ = places(mine_ref)

    def copies(n):
        rows = pl.ds(n * wide, wide)
        return [
            pltpu.make_async_copy(
                weight_ref.at[0, 0, half, rows], joined_ref.at[rows, pl.ds(half * width, width)], sems.at[n, half]
            )
            for half in range(2)
        ]

    def columns_of(start, to_ref, first_sem):
        return [
            pltpu.make_async_copy(
                source_ref.at[0, half, :, pl.ds(start, shots)],
                to_ref.at[:, pl.ds(half * shots, shots)],
                sem.at[first_sem + half],
            )
            for half in range(2)
        ]

    begin = columns_of(0, right, 0) + [pltpu.make_async_copy(factor_ref.at[0], factor, sem.at[4])]
    rest = columns_of(shots, later_ref, 2)
    for k in range(groups):
        row = pl.multiple_of((2 * k + 1 - place) * tall, tall)
        rest.append(
            pltpu.make_async_copy(
                upward_ref.at[0, 0, :, pl.ds(row, tall)], asked_ref.at[:, pl.ds(k * tall, tall)], asked_sems.at[k]
            )
        )
    for copy in begin:
        copy.start()
    for n in range(blocks):
        for copy in copies(n):
            copy.start()
    for copy in rest:
        copy.start()
    for copy in begin:
        copy.wait()
    for n in range(blocks):
        for copy in copies(n):
            copy.wait()
        columns = slice(n * wide, (n + 1) * wide)
        real, imag = joined_ref[columns, :width], joined_ref[columns, width:]
        start_panels(part, real, imag, right[...], factor[:, columns], outs, columns)
    for copy in rest:
        copy.wait()


def first_advance(level, mine, source, propagator, transmission, upgoing, part, groups):
    width = propagator.shape[3]
    shots = source.shape[3]
    chunks = shots // 2 // part
    whole = pl.BlockSpec(memory_space=pltpu.VMEM)
    pinned = [pltpu.with_memory_space_constraint(x, pltpu.HBM) for x in (source, propagator, transmission, upgoing)]
    return pl.pallas_call(
        functools.partial(first_kernel, part),
        in_specs=[pl.BlockSpec(memory_space=pltpu.SMEM)] * 2 + [pl.BlockSpec(memory_space=pltpu.HBM)] * 4,
        out_specs=[whole] * (chunks + 3),
        out_shape=[jax.ShapeDtypeStruct((2 * part, width), jnp.bfloat16)] * chunks
        + [
            pltpu.VMEM((width, 2 * width), jnp.bfloat16),
            jax.ShapeDtypeStruct((width, shots), jnp.bfloat16),
            jax.ShapeDtypeStruct((2, width // 2, shots), jnp.bfloat16),
        ],
        scratch_shapes=[
            pltpu.VMEM((width, shots), jnp.bfloat16),
            pltpu.VMEM((1, width), jnp.float32),
            pltpu.SemaphoreType.DMA((5,)),
            pltpu.SemaphoreType.DMA((4, 2)),
            pltpu.SemaphoreType.DMA((groups,)),
        ],
        compiler_params=pltpu.CompilerParams(vmem_limit_bytes=LIMIT),
        cost_estimate=pl.CostEstimate(
            flops=4 * width * width * shots, bytes_accessed=4 * width * (width + 2 * shots), transcendentals=0
        ),
    )(level, mine, *pinned)


def second_kernel(part, joined_ref, right_ref, factor_ref, *outs):
    width = joined_ref.shape[0]
    wide = width // 4
    for n in range(4):
        columns = slice(n * wide, (n + 1) * wide)
        real, imag = joined_ref[columns, :width], joined_ref[columns, width:]
        start_panels(part, real, imag, right_ref[...], factor_ref[:, columns], outs, columns)


def second_advance(joined, right, factor, part):
    width, shots = right.shape
    outs = [jax.ShapeDtypeStruct((2 * part, width), jnp.bfloat16)] * (shots // 2 // part)
    joined = pltpu.with_memory_space_constraint(joined, pltpu.VMEM)
    return whole_call(functools.partial(second_kernel, part), (joined, right, factor), outs, 4 * width * width * shots)


def advance_kernel(level_ref, arrived_ref, ready_ref, joined_ref, factor_ref, out_ref, both):
    part = arrived_ref.shape[0] // 2
    width = arrived_ref.shape[1]
    wide = width // 4

    @pl.when(level_ref[0] == 0)
    def _():
        out_ref[...] = ready_ref[...]

    @pl.when(level_ref[0] != 0)
    def _():
        both[:, :width] = arrived_ref[...]
        both[:part, width:] = -arrived_ref[part:]
        both[part:, width:] = arrived_ref[:part]
        for n in range(4):
            columns = slice(n * wide, (n + 1) * wide)
            out = lax.dot_general(
                joined_ref[columns], both[...], (((1,), (1,)), ((), ())), preferred_element_type=jnp.float32
            )
            out_ref[:, columns] = (out.T * factor_ref[:, columns]).astype(jnp.bfloat16)


def advance(level, arrived, ready, joined, factor):
    rows, width = arrived.shape
    joined = pltpu.with_memory_space_constraint(joined, pltpu.VMEM)
    out = jax.ShapeDtypeStruct((rows, width), jnp.bfloat16)
    args = (arrived, ready, joined, factor)
    scratch = [pltpu.VMEM((rows, 2 * width), jnp.bfloat16)]
    return whole_call(advance_kernel, args, [out], 4 * rows * width * width, (level,), scratch)[0]


def pair_kernel(first_ref, second_ref, out_ref):
    rows = first_ref.shape[0]
    out_ref[:rows] = first_ref[...]
    out_ref[rows:] = second_ref[...]


def paired(first, second):
    out = jax.ShapeDtypeStruct((2 * first.shape[0], first.shape[1]), first.dtype)
    return whole_call(pair_kernel, (first, second), [out], 0)[0]


def operand_kernel(own_ref, got_ref, out_ref):
    rows, shots = own_ref.shape[1:]
    half = shots // STREAMS
    for which, ref in enumerate((own_ref, got_ref)):
        real, imag = ref[0], ref[1]
        minus = -real
        for stream in range(STREAMS):
            lanes = slice(stream * half, (stream + 1) * half)
            left = 2 * (which * shots + stream * half)
            out_ref[:rows, left : left + half] = real[:, lanes]
            out_ref[:rows, left + half : left + 2 * half] = imag[:, lanes]
            out_ref[rows:, left : left + half] = imag[:, lanes]
            out_ref[rows:, left + half : left + 2 * half] = minus[:, lanes]


def operand(mine, own, got, rows):
    shots = own.shape[2]
    blocks = got.shape[1] // rows
    groups = blocks // 2

    def spot(i, mine_ref, stride):
        group, place, core = places(mine_ref)
        other = lax.rem(lax.div(i, groups) + core, 2)
        block = stride * lax.rem(group + lax.rem(i, groups), groups) + other
        return block + 2 * place if stride == 4 else block

    return pl.pallas_call(
        lambda _, *refs: operand_kernel(*refs),
        grid_spec=pltpu.PrefetchScalarGridSpec(
            num_scalar_prefetch=1,
            grid=(blocks,),
            in_specs=[
                pl.BlockSpec((2, rows, shots), lambda i, mine_ref: (0, spot(i, mine_ref, 4), 0)),
                pl.BlockSpec((2, rows, shots), lambda i, mine_ref: (0, spot(i, mine_ref, 2), 0)),
            ],
            out_specs=pl.BlockSpec((2 * rows, 4 * shots), lambda i, mine_ref: (i, 0)),
        ),
        out_shape=jax.ShapeDtypeStruct((2 * rows * blocks, 4 * shots), jnp.bfloat16),
        compiler_params=pltpu.CompilerParams(vmem_limit_bytes=LIMIT),
        cost_estimate=pl.CostEstimate(flops=0, bytes_accessed=24 * rows * blocks * shots, transcendentals=0),
    )(mine, own, got)


def gather(levels, level_ref, panels, joined):
    part = joined.shape[0] // len(panels) // 2
    half = STEPS * part
    first = lax.rem(levels - 1 - level_ref[0], STEPS)
    for at, (ref, top) in enumerate(panels):
        base = at // STEPS * 2 * half
        row = pl.multiple_of(lax.rem(first + at, STEPS) * part, part)
        joined[pl.ds(base + row, part)] = ref[top : top + part]
        joined[pl.ds(base + half + row, part)] = ref[top + part : top + 2 * part]


def crossed(refs, stream):
    *pairs, last = refs
    rows = last.shape[0]
    return [(pair, stream * rows) for pair in pairs] + [(last, 0)]


def early_kernel(levels, level_ref, left_ref, *refs):
    *panels, out_ref, joined = refs
    own, other = panels[: STREAMS * STEPS], panels[STREAMS * STEPS :]
    gather(levels, level_ref, [(ref, 0) for ref in own] + crossed(other, 0), joined)
    deep = joined.shape[0]
    wide = out_ref.shape[1] // 4
    for n in range(4):
        columns = slice(n * wide, (n + 1) * wide)
        out_ref[:, columns] = jnp.dot(left_ref[:, :deep], joined[:, columns], preferred_element_type=jnp.float32)


def late_kernel(levels, level_ref, left_ref, early_ref, *refs):
    *panels, keep_ref, send_ref, joined = refs
    gather(levels, level_ref, crossed(panels, 1), joined)
    start = left_ref.shape[1] - joined.shape[0]
    groups, _, rows, width = keep_ref.shape
    wide = width // 4
    for n in range(4):
        columns = slice(n * wide, (n + 1) * wide)
        out = early_ref[:, columns] + jnp.dot(
            left_ref[:, start:], joined[:, columns], preferred_element_type=jnp.float32
        )
        for k in range(groups):
            for part in range(2):
                lo = (2 * k + part) * rows
                keep_ref[k, part, :, columns] = out[lo : lo + rows]
                lo += 2 * groups * rows
                send_ref[k, part, :, columns] = out[lo : lo + rows].astype(jnp.bfloat16)


def whole_call(kernel, args, outs, flops, scalars=(), scratch=()):
    whole = pl.BlockSpec(memory_space=pltpu.VMEM)
    size = sum(math.prod(x.shape) * x.dtype.itemsize for x in (*args, *outs))
    return pl.pallas_call(
        kernel,
        in_specs=[pl.BlockSpec(memory_space=pltpu.SMEM)] * len(scalars) + [whole] * len(args),
        out_specs=[whole] * len(outs),
        out_shape=outs,
        scratch_shapes=scratch,
        compiler_params=pltpu.CompilerParams(vmem_limit_bytes=LIMIT),
        cost_estimate=pl.CostEstimate(flops=flops, bytes_accessed=size, transcendentals=0),
    )(*scalars, *args)


def early_terms(level, left, panels, levels):
    width = panels[0].shape[1]
    deep = left.shape[1] - panels[-1].shape[0] * STEPS
    out = jax.ShapeDtypeStruct((left.shape[0], width), jnp.float32)
    kernel = functools.partial(early_kernel, levels)
    scratch = [pltpu.VMEM((deep, width), jnp.bfloat16)]
    return whole_call(kernel, (left, *panels), [out], 2 * deep * left.shape[0] * width, (level,), scratch)[0]


def late_terms(level, left, early, panels, rows, levels):
    width = early.shape[1]
    deep = panels[-1].shape[0] * STEPS
    shape = (left.shape[0] // (4 * rows), 2, rows, width)
    outs = [jax.ShapeDtypeStruct(shape, jnp.float32), jax.ShapeDtypeStruct(shape, jnp.bfloat16)]
    kernel = functools.partial(late_kernel, levels)
    scratch = [pltpu.VMEM((deep, width), jnp.bfloat16)]
    return whole_call(kernel, (left, early, *panels), outs, 2 * deep * left.shape[0] * width, (level,), scratch)


def last_kernel(scale, *refs):
    *parts, out_ref = refs
    for part in range(2):
        total = parts[0][0, part]
        for ref in parts[1:]:
            total += ref[0, part].astype(jnp.float32)
        out_ref[0, :, part] = total * scale


def last_sum(parts, scale):
    rows, width = parts[0].shape[2:]
    out = jax.ShapeDtypeStruct((1, rows, 2, width), jnp.float32)
    return whole_call(functools.partial(last_kernel, scale), parts, [out], 2 * len(parts) * rows * width)[0]


def shards(source, propagator, transmission, upgoing):
    factor = transmission[0]
    upward = upgoing[0, 0]
    width = propagator.shape[3]
    shots = source.shape[3]
    levels = lax.axis_size("depth")
    freqs = lax.axis_size("freq")
    groups = freqs // 4
    rows = width // freqs
    part = shots // STREAMS // STEPS
    level, mine = (lax.axis_index(axis).astype(jnp.int32).reshape(1) for axis in ("depth", "freq"))
    *ready, joined, later, asked = first_advance(level, mine, source, propagator, transmission, upgoing, part, groups)
    ready = [ready, second_advance(joined, later, factor, part)]
    got = swapped(asked, "freq", 2)
    left = operand(mine, upward, got, rows)

    steps = STEPS + levels - 1
    flying = [None] * STREAMS
    own = [[] for _ in range(STREAMS)]
    crossing = []
    for event in range(STREAMS * steps):
        step, stream = divmod(event, STREAMS)
        out = ready[stream][step % STEPS]
        if step >= 1:
            arrived = flying[stream]
            if event == steps:
                arrived, left = lax.optimization_barrier((arrived, left))
            for at, (sent, panel) in enumerate(crossing):
                if event == sent + BEHIND + (at == 0):
                    arrived, panel = lax.optimization_barrier((arrived, panel))
                    crossing[at] = (sent, panel)
            out = advance(level, arrived, out, joined, factor)
        if step + 1 < steps:
            flying[stream] = ring(out, "depth", 1)
        if step >= levels - 1:
            own[stream].append(out)
            if step == steps - 1:
                crossing.append((event, swapped(out, "freq", 2)))
            elif stream > 0:
                crossing.append((event, swapped(paired(own[0][-1], out), "freq", 2)))
    other = [panel for _, panel in crossing]
    early = early_terms(level, left, own[0] + own[1] + other[:-1], levels)
    keep, send = late_terms(level, left, early, other[:-2] + other[-1:], rows, levels)
    near = swapped(send, "freq", 1)
    parts = [keep, near]
    for k in range(1, groups):
        total = (keep[k : k + 1] + near[k : k + 1].astype(jnp.float32)).astype(jnp.bfloat16)
        parts.append(ring(total, "freq", 4 * k))
    return last_sum(parts, (2.0 * shots * freqs) ** (-0.5))


def solution(mesh):
    return jax.shard_map(
        shards,
        mesh=mesh,
        in_specs=(
            P("freq", None, None, None),
            P("depth", "freq", None, None, None),
            P("depth", "freq", None),
            P("depth", "freq", None, None, None),
        ),
        out_specs=P("depth", "freq", None, None),
        check_vma=False,
    )
```

```python
import functools
import math

import jax
import jax.numpy as jnp
from jax import lax
from jax.experimental import pallas as pl
from jax.experimental.pallas import tpu as pltpu
from jax.sharding import PartitionSpec as P

STEPS = 4
STREAMS = 2
BEHIND = 3
TOGETHER = 2
LIMIT = 16 * 1024 * 1024


def ring(block, axis, distance):
    size = lax.axis_size(axis)
    return lax.ppermute(block, axis, [(i, (i + distance) % size) for i in range(size)])


def swapped(block, axis, bit):
    return lax.ppermute(block, axis, [(i, i ^ bit) for i in range(lax.axis_size(axis))])


def places(mine_ref):
    mine = mine_ref[0]
    return lax.div(mine, 4), lax.rem(lax.div(mine, 2), 2), lax.rem(mine, 2)


def start_panels(part, real, imag, right, factor, outs, columns):
    dot = functools.partial(jnp.dot, preferred_element_type=jnp.float32)
    shots = right.shape[1] // 2
    first, second = dot(real, right), dot(imag, right)
    out_real = ((first[:, :shots] - second[:, shots:]).T * factor).astype(jnp.bfloat16)
    out_imag = ((first[:, shots:] + second[:, :shots]).T * factor).astype(jnp.bfloat16)
    for chunk, out in enumerate(outs):
        lo = chunk * part
        out[:part, columns] = out_real[lo : lo + part]
        out[part:, columns] = out_imag[lo : lo + part]


def first_kernel(part, level_ref, mine_ref, source_ref, weight_ref, factor_ref, upward_ref, *refs):
    *outs, joined_ref, later_ref, asked_ref, right, factor, sem, sems, asked_sems = refs
    width = joined_ref.shape[0]
    shots = later_ref.shape[1] // 2
    blocks = sems.shape[0]
    wide = width // blocks
    groups = asked_sems.shape[0]
    tall = asked_ref.shape[1] // groups
    _, place, _ = places(mine_ref)

    def copies(n):
        rows = pl.ds(n * wide, wide)
        return [
            pltpu.make_async_copy(
                weight_ref.at[0, 0, half, rows], joined_ref.at[rows, pl.ds(half * width, width)], sems.at[n, half]
            )
            for half in range(2)
        ]

    def columns_of(start, to_ref, first_sem):
        return [
            pltpu.make_async_copy(
                source_ref.at[0, half, :, pl.ds(start, shots)],
                to_ref.at[:, pl.ds(half * shots, shots)],
                sem.at[first_sem + half],
            )
            for half in range(2)
        ]

    begin = columns_of(0, right, 0) + [pltpu.make_async_copy(factor_ref.at[0], factor, sem.at[4])]
    rest = columns_of(shots, later_ref, 2)
    for k in range(groups):
        row = pl.multiple_of((2 * k + 1 - place) * tall, tall)
        rest.append(
            pltpu.make_async_copy(
                upward_ref.at[0, 0, :, pl.ds(row, tall)], asked_ref.at[:, pl.ds(k * tall, tall)], asked_sems.at[k]
            )
        )
    for copy in begin:
        copy.start()
    for n in range(blocks):
        for copy in copies(n):
            copy.start()
    for copy in rest:
        copy.start()
    for copy in begin:
        copy.wait()
    for n in range(blocks):
        for copy in copies(n):
            copy.wait()
        columns = slice(n * wide, (n + 1) * wide)
        real, imag = joined_ref[columns, :width], joined_ref[columns, width:]
        start_panels(part, real, imag, right[...], factor[:, columns], outs, columns)
    for copy in rest:
        copy.wait()


def first_advance(level, mine, source, propagator, transmission, upgoing, part, groups):
    width = propagator.shape[3]
    shots = source.shape[3]
    chunks = shots // 2 // part
    whole = pl.BlockSpec(memory_space=pltpu.VMEM)
    pinned = [pltpu.with_memory_space_constraint(x, pltpu.HBM) for x in (source, propagator, transmission, upgoing)]
    return pl.pallas_call(
        functools.partial(first_kernel, part),
        in_specs=[pl.BlockSpec(memory_space=pltpu.SMEM)] * 2 + [pl.BlockSpec(memory_space=pltpu.HBM)] * 4,
        out_specs=[whole] * (chunks + 3),
        out_shape=[jax.ShapeDtypeStruct((2 * part, width), jnp.bfloat16)] * chunks
        + [
            pltpu.VMEM((width, 2 * width), jnp.bfloat16),
            jax.ShapeDtypeStruct((width, shots), jnp.bfloat16),
            jax.ShapeDtypeStruct((2, width // 2, shots), jnp.bfloat16),
        ],
        scratch_shapes=[
            pltpu.VMEM((width, shots), jnp.bfloat16),
            pltpu.VMEM((1, width), jnp.float32),
            pltpu.SemaphoreType.DMA((5,)),
            pltpu.SemaphoreType.DMA((4, 2)),
            pltpu.SemaphoreType.DMA((groups,)),
        ],
        compiler_params=pltpu.CompilerParams(vmem_limit_bytes=LIMIT),
        cost_estimate=pl.CostEstimate(
            flops=4 * width * width * shots, bytes_accessed=4 * width * (width + 2 * shots), transcendentals=0
        ),
    )(level, mine, *pinned)


def second_kernel(part, joined_ref, right_ref, factor_ref, *outs):
    width = joined_ref.shape[0]
    wide = width // 4
    for n in range(4):
        columns = slice(n * wide, (n + 1) * wide)
        real, imag = joined_ref[columns, :width], joined_ref[columns, width:]
        start_panels(part, real, imag, right_ref[...], factor_ref[:, columns], outs, columns)


def second_advance(joined, right, factor, part):
    width, shots = right.shape
    outs = [jax.ShapeDtypeStruct((2 * part, width), jnp.bfloat16)] * (shots // 2 // part)
    joined = pltpu.with_memory_space_constraint(joined, pltpu.VMEM)
    return whole_call(functools.partial(second_kernel, part), (joined, right, factor), outs, 4 * width * width * shots)


def advance_kernel(level_ref, arrived_ref, ready_ref, joined_ref, factor_ref, out_ref, both):
    part = arrived_ref.shape[0] // 2
    width = arrived_ref.shape[1]
    wide = width // 4

    @pl.when(level_ref[0] == 0)
    def _():
        out_ref[...] = ready_ref[...]

    @pl.when(level_ref[0] != 0)
    def _():
        both[:, :width] = arrived_ref[...]
        both[:part, width:] = -arrived_ref[part:]
        both[part:, width:] = arrived_ref[:part]
        for n in range(4):
            columns = slice(n * wide, (n + 1) * wide)
            out = lax.dot_general(
                joined_ref[columns], both[...], (((1,), (1,)), ((), ())), preferred_element_type=jnp.float32
            )
            out_ref[:, columns] = (out.T * factor_ref[:, columns]).astype(jnp.bfloat16)


def advance(level, arrived, ready, joined, factor):
    rows, width = arrived.shape
    joined = pltpu.with_memory_space_constraint(joined, pltpu.VMEM)
    out = jax.ShapeDtypeStruct((rows, width), jnp.bfloat16)
    args = (arrived, ready, joined, factor)
    scratch = [pltpu.VMEM((rows, 2 * width), jnp.bfloat16)]
    return whole_call(advance_kernel, args, [out], 4 * rows * width * width, (level,), scratch)[0]


def stack_kernel(*refs):
    *panels, out_ref = refs
    rows = panels[0].shape[0]
    for at, panel in enumerate(panels):
        out_ref[at * rows : (at + 1) * rows] = panel[...]


def stacked(panels):
    rows, width = panels[0].shape
    out = jax.ShapeDtypeStruct((len(panels) * rows, width), panels[0].dtype)
    return whole_call(stack_kernel, panels, [out], 0)[0]


def operand_kernel(own_ref, got_ref, out_ref):
    rows, shots = own_ref.shape[1:]
    half = shots // STREAMS
    for which, ref in enumerate((own_ref, got_ref)):
        real, imag = ref[0], ref[1]
        minus = -real
        for stream in range(STREAMS):
            lanes = slice(stream * half, (stream + 1) * half)
            left = 2 * (which * shots + stream * half)
            out_ref[:rows, left : left + half] = real[:, lanes]
            out_ref[:rows, left + half : left + 2 * half] = imag[:, lanes]
            out_ref[rows:, left : left + half] = imag[:, lanes]
            out_ref[rows:, left + half : left + 2 * half] = minus[:, lanes]


def operand(mine, own, got, rows):
    shots = own.shape[2]
    blocks = got.shape[1] // rows
    groups = blocks // 2

    def spot(i, mine_ref, stride):
        group, place, core = places(mine_ref)
        other = lax.rem(lax.div(i, groups) + core, 2)
        block = stride * lax.rem(group + lax.rem(i, groups), groups) + other
        return block + 2 * place if stride == 4 else block

    return pl.pallas_call(
        lambda _, *refs: operand_kernel(*refs),
        grid_spec=pltpu.PrefetchScalarGridSpec(
            num_scalar_prefetch=1,
            grid=(blocks,),
            in_specs=[
                pl.BlockSpec((2, rows, shots), lambda i, mine_ref: (0, spot(i, mine_ref, 4), 0)),
                pl.BlockSpec((2, rows, shots), lambda i, mine_ref: (0, spot(i, mine_ref, 2), 0)),
            ],
            out_specs=pl.BlockSpec((2 * rows, 4 * shots), lambda i, mine_ref: (i, 0)),
        ),
        out_shape=jax.ShapeDtypeStruct((2 * rows * blocks, 4 * shots), jnp.bfloat16),
        compiler_params=pltpu.CompilerParams(vmem_limit_bytes=LIMIT),
        cost_estimate=pl.CostEstimate(flops=0, bytes_accessed=24 * rows * blocks * shots, transcendentals=0),
    )(mine, own, got)


def gather(levels, level_ref, panels, joined):
    part = joined.shape[0] // len(panels) // 2
    half = STEPS * part
    first = lax.rem(levels - 1 - level_ref[0], STEPS)
    for at, (ref, top) in enumerate(panels):
        base = at // STEPS * 2 * half
        row = pl.multiple_of(lax.rem(first + at, STEPS) * part, part)
        joined[pl.ds(base + row, part)] = ref[top : top + part]
        joined[pl.ds(base + half + row, part)] = ref[top + part : top + 2 * part]


def crossed(refs, counts, stream):
    rows = refs[0].shape[0] // counts[0]
    panels = [(ref, at * rows) for ref, count in zip(refs, counts) for at in range(count)]
    return panels[stream::STREAMS]


def early_kernel(levels, counts, level_ref, left_ref, *refs):
    *panels, out_ref, joined = refs
    own, other = panels[: STREAMS * STEPS], panels[STREAMS * STEPS :]
    gather(levels, level_ref, [(ref, 0) for ref in own] + crossed(other, counts, 0), joined)
    deep = joined.shape[0]
    wide = out_ref.shape[1] // 4
    for n in range(4):
        columns = slice(n * wide, (n + 1) * wide)
        out_ref[:, columns] = jnp.dot(left_ref[:, :deep], joined[:, columns], preferred_element_type=jnp.float32)


def late_kernel(levels, counts, level_ref, left_ref, early_ref, *refs):
    *panels, keep_ref, own_ref, send_ref, joined = refs
    gather(levels, level_ref, crossed(panels[:-1], counts[:-1], 1) + [(panels[-1], 0)], joined)
    start = left_ref.shape[1] - joined.shape[0]
    groups, _, rows, width = keep_ref.shape
    wide = width // 4
    for n in range(4):
        columns = slice(n * wide, (n + 1) * wide)
        out = early_ref[:, columns] + jnp.dot(
            left_ref[:, start:], joined[:, columns], preferred_element_type=jnp.float32
        )
        for k in range(groups):
            for part in range(2):
                lo = (2 * k + part) * rows
                keep_ref[k, part, :, columns] = out[lo : lo + rows]
                lo += 2 * groups * rows
                to_ref, at = (send_ref, k - 1) if k else (own_ref, 0)
                to_ref[at, part, :, columns] = out[lo : lo + rows].astype(jnp.bfloat16)


def whole_call(kernel, args, outs, flops, scalars=(), scratch=()):
    whole = pl.BlockSpec(memory_space=pltpu.VMEM)
    size = sum(math.prod(x.shape) * x.dtype.itemsize for x in (*args, *outs))
    return pl.pallas_call(
        kernel,
        in_specs=[pl.BlockSpec(memory_space=pltpu.SMEM)] * len(scalars) + [whole] * len(args),
        out_specs=[whole] * len(outs),
        out_shape=outs,
        scratch_shapes=scratch,
        compiler_params=pltpu.CompilerParams(vmem_limit_bytes=LIMIT),
        cost_estimate=pl.CostEstimate(flops=flops, bytes_accessed=size, transcendentals=0),
    )(*scalars, *args)


def early_terms(level, left, panels, levels, counts):
    width = panels[0].shape[1]
    deep = left.shape[1] - panels[-1].shape[0] * STEPS
    out = jax.ShapeDtypeStruct((left.shape[0], width), jnp.float32)
    kernel = functools.partial(early_kernel, levels, counts)
    scratch = [pltpu.VMEM((deep, width), jnp.bfloat16)]
    return whole_call(kernel, (left, *panels), [out], 2 * deep * left.shape[0] * width, (level,), scratch)[0]


def late_terms(level, left, early, panels, rows, levels, counts):
    width = early.shape[1]
    deep = panels[-1].shape[0] * STEPS
    groups = left.shape[0] // (4 * rows)
    outs = [jax.ShapeDtypeStruct((groups, 2, rows, width), jnp.float32)] + [
        jax.ShapeDtypeStruct((count, 2, rows, width), jnp.bfloat16) for count in (1, groups - 1)
    ]
    kernel = functools.partial(late_kernel, levels, counts)
    scratch = [pltpu.VMEM((deep, width), jnp.bfloat16)]
    return whole_call(kernel, (left, early, *panels), outs, 2 * deep * left.shape[0] * width, (level,), scratch)


def last_kernel(scale, *refs):
    *parts, out_ref = refs
    for part in range(2):
        total = parts[0][0, part]
        for ref in parts[1:]:
            total += ref[0, part].astype(jnp.float32)
        out_ref[0, :, part] = total * scale


def last_sum(parts, scale):
    rows, width = parts[0].shape[2:]
    out = jax.ShapeDtypeStruct((1, rows, 2, width), jnp.float32)
    return whole_call(functools.partial(last_kernel, scale), parts, [out], 2 * len(parts) * rows * width)[0]


def shards(source, propagator, transmission, upgoing):
    factor = transmission[0]
    upward = upgoing[0, 0]
    width = propagator.shape[3]
    shots = source.shape[3]
    levels = lax.axis_size("depth")
    freqs = lax.axis_size("freq")
    groups = freqs // 4
    rows = width // freqs
    part = shots // STREAMS // STEPS
    level, mine = (lax.axis_index(axis).astype(jnp.int32).reshape(1) for axis in ("depth", "freq"))
    *ready, joined, later, asked = first_advance(level, mine, source, propagator, transmission, upgoing, part, groups)
    ready = [ready, second_advance(joined, later, factor, part)]
    got = swapped(asked, "freq", 2)
    left = operand(mine, upward, got, rows)

    steps = STEPS + levels - 1
    flying = [None] * STREAMS
    own = [[] for _ in range(STREAMS)]
    waiting = []
    crossing = []
    for event in range(STREAMS * steps):
        step, stream = divmod(event, STREAMS)
        out = ready[stream][step % STEPS]
        if step >= 1:
            arrived = flying[stream]
            if event == steps:
                arrived, left = lax.optimization_barrier((arrived, left))
            for at, (sent, panel) in enumerate(crossing):
                if event == sent + BEHIND + (at == 0):
                    arrived, panel = lax.optimization_barrier((arrived, panel))
                    crossing[at] = (sent, panel)
            out = advance(level, arrived, out, joined, factor)
        if step + 1 < steps:
            flying[stream] = ring(out, "depth", 1)
        if step >= levels - 1:
            own[stream].append(out)
            if step == steps - 1:
                crossing.append((event, swapped(out, "freq", 2)))
            else:
                waiting.append(out)
                if len(waiting) == TOGETHER:
                    crossing.append((event, swapped(stacked(waiting), "freq", 2)))
                    waiting = []
    other = [panel for _, panel in crossing]
    counts = [panel.shape[0] // out.shape[0] for panel in other]
    early = early_terms(level, left, own[0] + own[1] + other[:-1], levels, counts[:-1])
    late = late_terms(level, left, early, other[:-2] + other[-1:], rows, levels, counts[:-2] + counts[-1:])
    keep, send_own, send = late
    near = swapped(send, "freq", 1)
    send_own, near = lax.optimization_barrier((send_own, near))
    parts = [keep, swapped(send_own, "freq", 1)]
    for k in range(1, groups):
        total = (keep[k : k + 1] + near[k - 1 : k].astype(jnp.float32)).astype(jnp.bfloat16)
        parts.append(ring(total, "freq", 4 * k))
    return last_sum(parts, (2.0 * shots * freqs) ** (-0.5))


def solution(mesh):
    return jax.shard_map(
        shards,
        mesh=mesh,
        in_specs=(
            P("freq", None, None, None),
            P("depth", "freq", None, None, None),
            P("depth", "freq", None),
            P("depth", "freq", None, None, None),
        ),
        out_specs=P("depth", "freq", None, None),
        check_vma=False,
    )
```

```python
import functools
import math

import jax
import jax.numpy as jnp
from jax import lax
from jax.experimental import pallas as pl
from jax.experimental.pallas import tpu as pltpu
from jax.sharding import PartitionSpec as P

STEPS = 4
STREAMS = 2
BEHIND = 3
TOGETHER = 2
LIMIT = 16 * 1024 * 1024


def ring(block, axis, distance):
    size = lax.axis_size(axis)
    return lax.ppermute(block, axis, [(i, (i + distance) % size) for i in range(size)])


def swapped(block, axis, bit):
    return lax.ppermute(block, axis, [(i, i ^ bit) for i in range(lax.axis_size(axis))])


def places(mine_ref):
    mine = mine_ref[0]
    return lax.div(mine, 4), lax.rem(lax.div(mine, 2), 2), lax.rem(mine, 2)


def start_panels(part, real, imag, right, factor, outs, columns):
    dot = functools.partial(jnp.dot, preferred_element_type=jnp.float32)
    shots = right.shape[1] // 2
    first, second = dot(real, right), dot(imag, right)
    out_real = ((first[:, :shots] - second[:, shots:]).T * factor).astype(jnp.bfloat16)
    out_imag = ((first[:, shots:] + second[:, :shots]).T * factor).astype(jnp.bfloat16)
    for chunk, out in enumerate(outs):
        lo = chunk * part
        out[:part, columns] = out_real[lo : lo + part]
        out[part:, columns] = out_imag[lo : lo + part]


def first_kernel(part, level_ref, mine_ref, source_ref, weight_ref, factor_ref, upward_ref, *refs):
    *outs, joined_ref, later_ref, asked_ref, right, factor, sem, sems, asked_sems = refs
    width = joined_ref.shape[0]
    shots = later_ref.shape[1] // 2
    blocks = sems.shape[0]
    wide = width // blocks
    groups = asked_sems.shape[0]
    tall = asked_ref.shape[1] // groups
    _, place, _ = places(mine_ref)

    def copies(n):
        rows = pl.ds(n * wide, wide)
        return [
            pltpu.make_async_copy(
                weight_ref.at[0, 0, half, rows], joined_ref.at[rows, pl.ds(half * width, width)], sems.at[n, half]
            )
            for half in range(2)
        ]

    def columns_of(start, to_ref, first_sem):
        return [
            pltpu.make_async_copy(
                source_ref.at[0, half, :, pl.ds(start, shots)],
                to_ref.at[:, pl.ds(half * shots, shots)],
                sem.at[first_sem + half],
            )
            for half in range(2)
        ]

    begin = columns_of(0, right, 0) + [pltpu.make_async_copy(factor_ref.at[0], factor, sem.at[4])]
    rest = columns_of(shots, later_ref, 2)
    for k in range(groups):
        row = pl.multiple_of((2 * k + 1 - place) * tall, tall)
        rest.append(
            pltpu.make_async_copy(
                upward_ref.at[0, 0, :, pl.ds(row, tall)], asked_ref.at[:, pl.ds(k * tall, tall)], asked_sems.at[k]
            )
        )
    for copy in begin:
        copy.start()
    for n in range(blocks):
        for copy in copies(n):
            copy.start()
    for copy in rest:
        copy.start()
    for copy in begin:
        copy.wait()
    for n in range(blocks):
        for copy in copies(n):
            copy.wait()
        columns = slice(n * wide, (n + 1) * wide)
        real, imag = joined_ref[columns, :width], joined_ref[columns, width:]
        start_panels(part, real, imag, right[...], factor[:, columns], outs, columns)
    for copy in rest:
        copy.wait()


def first_advance(level, mine, source, propagator, transmission, upgoing, part, groups):
    width = propagator.shape[3]
    shots = source.shape[3]
    chunks = shots // 2 // part
    whole = pl.BlockSpec(memory_space=pltpu.VMEM)
    pinned = [pltpu.with_memory_space_constraint(x, pltpu.HBM) for x in (source, propagator, transmission, upgoing)]
    return pl.pallas_call(
        functools.partial(first_kernel, part),
        in_specs=[pl.BlockSpec(memory_space=pltpu.SMEM)] * 2 + [pl.BlockSpec(memory_space=pltpu.HBM)] * 4,
        out_specs=[whole] * (chunks + 3),
        out_shape=[jax.ShapeDtypeStruct((2 * part, width), jnp.bfloat16)] * chunks
        + [
            pltpu.VMEM((width, 2 * width), jnp.bfloat16),
            jax.ShapeDtypeStruct((width, shots), jnp.bfloat16),
            jax.ShapeDtypeStruct((2, width // 2, shots), jnp.bfloat16),
        ],
        scratch_shapes=[
            pltpu.VMEM((width, shots), jnp.bfloat16),
            pltpu.VMEM((1, width), jnp.float32),
            pltpu.SemaphoreType.DMA((5,)),
            pltpu.SemaphoreType.DMA((4, 2)),
            pltpu.SemaphoreType.DMA((groups,)),
        ],
        compiler_params=pltpu.CompilerParams(vmem_limit_bytes=LIMIT),
        cost_estimate=pl.CostEstimate(
            flops=4 * width * width * shots, bytes_accessed=4 * width * (width + 2 * shots), transcendentals=0
        ),
    )(level, mine, *pinned)


def second_kernel(part, joined_ref, right_ref, factor_ref, *outs):
    width = joined_ref.shape[0]
    wide = width // 4
    for n in range(4):
        columns = slice(n * wide, (n + 1) * wide)
        real, imag = joined_ref[columns, :width], joined_ref[columns, width:]
        start_panels(part, real, imag, right_ref[...], factor_ref[:, columns], outs, columns)


def second_advance(joined, right, factor, part):
    width, shots = right.shape
    outs = [jax.ShapeDtypeStruct((2 * part, width), jnp.bfloat16)] * (shots // 2 // part)
    joined = pltpu.with_memory_space_constraint(joined, pltpu.VMEM)
    return whole_call(functools.partial(second_kernel, part), (joined, right, factor), outs, 4 * width * width * shots)


def advance_kernel(level_ref, arrived_ref, ready_ref, joined_ref, factor_ref, out_ref, both):
    part = arrived_ref.shape[0] // 2
    width = arrived_ref.shape[1]
    wide = width // 4

    @pl.when(level_ref[0] == 0)
    def _():
        out_ref[...] = ready_ref[...]

    @pl.when(level_ref[0] != 0)
    def _():
        both[:, :width] = arrived_ref[...]
        both[:part, width:] = -arrived_ref[part:]
        both[part:, width:] = arrived_ref[:part]
        for n in range(4):
            columns = slice(n * wide, (n + 1) * wide)
            out = lax.dot_general(
                joined_ref[columns], both[...], (((1,), (1,)), ((), ())), preferred_element_type=jnp.float32
            )
            out_ref[:, columns] = (out.T * factor_ref[:, columns]).astype(jnp.bfloat16)


def advance(level, arrived, ready, joined, factor):
    rows, width = arrived.shape
    joined = pltpu.with_memory_space_constraint(joined, pltpu.VMEM)
    out = jax.ShapeDtypeStruct((rows, width), jnp.bfloat16)
    args = (arrived, ready, joined, factor)
    scratch = [pltpu.VMEM((rows, 2 * width), jnp.bfloat16)]
    return whole_call(advance_kernel, args, [out], 4 * rows * width * width, (level,), scratch)[0]


def stack_kernel(*refs):
    *panels, out_ref = refs
    rows = panels[0].shape[0]
    for at, panel in enumerate(panels):
        out_ref[at * rows : (at + 1) * rows] = panel[...]


def stacked(panels):
    rows, width = panels[0].shape
    out = jax.ShapeDtypeStruct((len(panels) * rows, width), panels[0].dtype)
    return whole_call(stack_kernel, panels, [out], 0)[0]


def operand_kernel(own_ref, got_ref, out_ref):
    rows, shots = own_ref.shape[1:]
    half = shots // STREAMS
    for which, ref in enumerate((own_ref, got_ref)):
        real, imag = ref[0], ref[1]
        minus = -real
        for stream in range(STREAMS):
            lanes = slice(stream * half, (stream + 1) * half)
            left = 2 * (which * shots + stream * half)
            out_ref[:rows, left : left + half] = real[:, lanes]
            out_ref[:rows, left + half : left + 2 * half] = imag[:, lanes]
            out_ref[rows:, left : left + half] = imag[:, lanes]
            out_ref[rows:, left + half : left + 2 * half] = minus[:, lanes]


def operand(mine, own, got, rows):
    shots = own.shape[2]
    blocks = got.shape[1] // rows
    groups = blocks // 2

    def spot(i, mine_ref, stride):
        group, place, core = places(mine_ref)
        other = lax.rem(lax.div(i, groups) + core, 2)
        block = stride * lax.rem(group + lax.rem(i, groups), groups) + other
        return block + 2 * place if stride == 4 else block

    return pl.pallas_call(
        lambda _, *refs: operand_kernel(*refs),
        grid_spec=pltpu.PrefetchScalarGridSpec(
            num_scalar_prefetch=1,
            grid=(blocks,),
            in_specs=[
                pl.BlockSpec((2, rows, shots), lambda i, mine_ref: (0, spot(i, mine_ref, 4), 0)),
                pl.BlockSpec((2, rows, shots), lambda i, mine_ref: (0, spot(i, mine_ref, 2), 0)),
            ],
            out_specs=pl.BlockSpec((2 * rows, 4 * shots), lambda i, mine_ref: (i, 0)),
        ),
        out_shape=jax.ShapeDtypeStruct((2 * rows * blocks, 4 * shots), jnp.bfloat16),
        compiler_params=pltpu.CompilerParams(vmem_limit_bytes=LIMIT),
        cost_estimate=pl.CostEstimate(flops=0, bytes_accessed=24 * rows * blocks * shots, transcendentals=0),
    )(mine, own, got)


def gather(levels, level_ref, panels, joined):
    part = joined.shape[0] // len(panels) // 2
    half = STEPS * part
    first = lax.rem(levels - 1 - level_ref[0], STEPS)
    for at, (ref, top) in enumerate(panels):
        base = at // STEPS * 2 * half
        row = pl.multiple_of(lax.rem(first + at, STEPS) * part, part)
        joined[pl.ds(base + row, part)] = ref[top : top + part]
        joined[pl.ds(base + half + row, part)] = ref[top + part : top + 2 * part]


def crossed(refs, counts, stream):
    rows = refs[0].shape[0] // counts[0]
    panels = [(ref, at * rows) for ref, count in zip(refs, counts) for at in range(count)]
    return panels[stream::STREAMS]


def early_kernel(levels, counts, level_ref, left_ref, *refs):
    *panels, out_ref, joined = refs
    own, other = panels[: STREAMS * STEPS], panels[STREAMS * STEPS :]
    gather(levels, level_ref, [(ref, 0) for ref in own] + crossed(other, counts, 0), joined)
    deep = joined.shape[0]
    wide = out_ref.shape[1] // 4
    for n in range(4):
        columns = slice(n * wide, (n + 1) * wide)
        out_ref[:, columns] = jnp.dot(left_ref[:, :deep], joined[:, columns], preferred_element_type=jnp.float32)


def late_kernel(levels, counts, level_ref, left_ref, early_ref, *refs):
    *panels, keep_ref, own_ref, send_ref, joined = refs
    gather(levels, level_ref, crossed(panels[:-1], counts[:-1], 1) + [(panels[-1], 0)], joined)
    start = left_ref.shape[1] - joined.shape[0]
    groups, _, rows, width = keep_ref.shape
    wide = width // 4
    for n in range(4):
        columns = slice(n * wide, (n + 1) * wide)
        out = early_ref[:, columns] + jnp.dot(
            left_ref[:, start:], joined[:, columns], preferred_element_type=jnp.float32
        )
        for k in range(groups):
            for part in range(2):
                lo = (2 * k + part) * rows
                keep_ref[k, part, :, columns] = out[lo : lo + rows]
                lo += 2 * groups * rows
                to_ref, at = (send_ref, k - 1) if k else (own_ref, 0)
                to_ref[at, part, :, columns] = out[lo : lo + rows].astype(jnp.bfloat16)


def whole_call(kernel, args, outs, flops, scalars=(), scratch=()):
    whole = pl.BlockSpec(memory_space=pltpu.VMEM)
    size = sum(math.prod(x.shape) * x.dtype.itemsize for x in (*args, *outs))
    return pl.pallas_call(
        kernel,
        in_specs=[pl.BlockSpec(memory_space=pltpu.SMEM)] * len(scalars) + [whole] * len(args),
        out_specs=[whole] * len(outs),
        out_shape=outs,
        scratch_shapes=scratch,
        compiler_params=pltpu.CompilerParams(vmem_limit_bytes=LIMIT),
        cost_estimate=pl.CostEstimate(flops=flops, bytes_accessed=size, transcendentals=0),
    )(*scalars, *args)


def early_terms(level, left, panels, levels, counts):
    width = panels[0].shape[1]
    deep = left.shape[1] - panels[-1].shape[0] * STEPS
    out = jax.ShapeDtypeStruct((left.shape[0], width), jnp.float32)
    kernel = functools.partial(early_kernel, levels, counts)
    scratch = [pltpu.VMEM((deep, width), jnp.bfloat16)]
    return whole_call(kernel, (left, *panels), [out], 2 * deep * left.shape[0] * width, (level,), scratch)[0]


def late_terms(level, left, early, panels, rows, levels, counts):
    width = early.shape[1]
    deep = panels[-1].shape[0] * STEPS
    groups = left.shape[0] // (4 * rows)
    outs = [jax.ShapeDtypeStruct((groups, 2, rows, width), jnp.float32)] + [
        jax.ShapeDtypeStruct((count, 2, rows, width), jnp.bfloat16) for count in (1, groups - 1)
    ]
    kernel = functools.partial(late_kernel, levels, counts)
    scratch = [pltpu.VMEM((deep, width), jnp.bfloat16)]
    return whole_call(kernel, (left, early, *panels), outs, 2 * deep * left.shape[0] * width, (level,), scratch)


def last_kernel(scale, *refs):
    *parts, out_ref = refs
    for part in range(2):
        total = parts[0][0, part]
        for ref in parts[1:]:
            total += ref[0, part].astype(jnp.float32)
        out_ref[0, :, part] = total * scale


def last_sum(parts, scale):
    rows, width = parts[0].shape[2:]
    out = jax.ShapeDtypeStruct((1, rows, 2, width), jnp.float32)
    return whole_call(functools.partial(last_kernel, scale), parts, [out], 2 * len(parts) * rows * width)[0]


def shards(source, propagator, transmission, upgoing):
    factor = transmission[0]
    upward = upgoing[0, 0]
    width = propagator.shape[3]
    shots = source.shape[3]
    levels = lax.axis_size("depth")
    freqs = lax.axis_size("freq")
    groups = freqs // 4
    rows = width // freqs
    part = shots // STREAMS // STEPS
    level, mine = (lax.axis_index(axis).astype(jnp.int32).reshape(1) for axis in ("depth", "freq"))
    *ready, joined, later, asked = first_advance(level, mine, source, propagator, transmission, upgoing, part, groups)
    ready = [ready, second_advance(joined, later, factor, part)]
    got = swapped(asked, "freq", 2)
    left = operand(mine, upward, got, rows)

    steps = STEPS + levels - 1
    flying = [None] * STREAMS
    own = [[] for _ in range(STREAMS)]
    waiting = []
    crossing = []
    for event in range(STREAMS * steps):
        step, stream = divmod(event, STREAMS)
        out = ready[stream][step % STEPS]
        if step >= 1:
            arrived = flying[stream]
            if event == steps:
                arrived, left = lax.optimization_barrier((arrived, left))
            for at, (sent, panel) in enumerate(crossing):
                if event == sent + BEHIND + (at <= 1) - (at == 3):
                    arrived, panel = lax.optimization_barrier((arrived, panel))
                    crossing[at] = (sent, panel)
            out = advance(level, arrived, out, joined, factor)
        if step + 1 < steps:
            flying[stream] = ring(out, "depth", 1)
        if step >= levels - 1:
            own[stream].append(out)
            if step == steps - 1:
                crossing.append((event, swapped(out, "freq", 2)))
            else:
                waiting.append(out)
                if len(waiting) == TOGETHER or step >= steps - 2:
                    crossing.append((event, swapped(stacked(waiting) if len(waiting) > 1 else waiting[0], "freq", 2)))
                    waiting = []
    other = [panel for _, panel in crossing]
    counts = [panel.shape[0] // out.shape[0] for panel in other]
    early = early_terms(level, left, own[0] + own[1] + other[:-1], levels, counts[:-1])
    late = late_terms(level, left, early, other[:-2] + other[-1:], rows, levels, counts[:-2] + counts[-1:])
    keep, send_own, send = late
    near = swapped(send, "freq", 1)
    send_own, near = lax.optimization_barrier((send_own, near))
    parts = [keep, swapped(send_own, "freq", 1)]
    for k in range(1, groups):
        total = (keep[k : k + 1] + near[k - 1 : k].astype(jnp.float32)).astype(jnp.bfloat16)
        parts.append(ring(total, "freq", 4 * k))
    return last_sum(parts, (2.0 * shots * freqs) ** (-0.5))


def solution(mesh):
    return jax.shard_map(
        shards,
        mesh=mesh,
        in_specs=(
            P("freq", None, None, None),
            P("depth", "freq", None, None, None),
            P("depth", "freq", None),
            P("depth", "freq", None, None, None),
        ),
        out_specs=P("depth", "freq", None, None),
        check_vma=False,
    )
```

```python
import functools
import math

import jax
import jax.numpy as jnp
from jax import lax
from jax.experimental import pallas as pl
from jax.experimental.pallas import tpu as pltpu
from jax.sharding import PartitionSpec as P

STEPS = 4
STREAMS = 2
BEHIND = 3
TOGETHER = 2
LIMIT = 16 * 1024 * 1024


def ring(block, axis, distance):
    size = lax.axis_size(axis)
    return lax.ppermute(block, axis, [(i, (i + distance) % size) for i in range(size)])


def swapped(block, axis, bit):
    return lax.ppermute(block, axis, [(i, i ^ bit) for i in range(lax.axis_size(axis))])


def places(mine_ref):
    mine = mine_ref[0]
    return lax.div(mine, 4), lax.rem(lax.div(mine, 2), 2), lax.rem(mine, 2)


def start_panels(part, real, imag, right, factor, outs, columns):
    dot = functools.partial(jnp.dot, preferred_element_type=jnp.float32)
    shots = right.shape[1] // 2
    first, second = dot(real, right), dot(imag, right)
    out_real = ((first[:, :shots] - second[:, shots:]).T * factor).astype(jnp.bfloat16)
    out_imag = ((first[:, shots:] + second[:, :shots]).T * factor).astype(jnp.bfloat16)
    for chunk, out in enumerate(outs):
        lo = chunk * part
        out[:part, columns] = out_real[lo : lo + part]
        out[part:, columns] = out_imag[lo : lo + part]


def first_kernel(part, level_ref, mine_ref, source_ref, weight_ref, factor_ref, upward_ref, *refs):
    *outs, joined_ref, later_ref, asked_ref, right, factor, sem, sems, asked_sems = refs
    width = joined_ref.shape[0]
    shots = later_ref.shape[1] // 2
    blocks = sems.shape[0]
    wide = width // blocks
    groups = asked_sems.shape[0]
    tall = asked_ref.shape[1] // groups
    _, place, _ = places(mine_ref)

    def copies(n):
        rows = pl.ds(n * wide, wide)
        return [
            pltpu.make_async_copy(
                weight_ref.at[0, 0, half, rows], joined_ref.at[rows, pl.ds(half * width, width)], sems.at[n, half]
            )
            for half in range(2)
        ]

    def columns_of(start, to_ref, first_sem):
        return [
            pltpu.make_async_copy(
                source_ref.at[0, half, :, pl.ds(start, shots)],
                to_ref.at[:, pl.ds(half * shots, shots)],
                sem.at[first_sem + half],
            )
            for half in range(2)
        ]

    begin = columns_of(0, right, 0) + [pltpu.make_async_copy(factor_ref.at[0], factor, sem.at[4])]
    rest = columns_of(shots, later_ref, 2)
    for k in range(groups):
        row = pl.multiple_of((2 * k + 1 - place) * tall, tall)
        rest.append(
            pltpu.make_async_copy(
                upward_ref.at[0, 0, :, pl.ds(row, tall)], asked_ref.at[:, pl.ds(k * tall, tall)], asked_sems.at[k]
            )
        )
    for copy in begin:
        copy.start()
    for n in range(blocks):
        for copy in copies(n):
            copy.start()
    for copy in rest:
        copy.start()
    for copy in begin:
        copy.wait()
    for n in range(blocks):
        for copy in copies(n):
            copy.wait()
        columns = slice(n * wide, (n + 1) * wide)
        real, imag = joined_ref[columns, :width], joined_ref[columns, width:]
        start_panels(part, real, imag, right[...], factor[:, columns], outs, columns)
    for copy in rest:
        copy.wait()


def first_advance(level, mine, source, propagator, transmission, upgoing, part, groups):
    width = propagator.shape[3]
    shots = source.shape[3]
    chunks = shots // 2 // part
    whole = pl.BlockSpec(memory_space=pltpu.VMEM)
    pinned = [pltpu.with_memory_space_constraint(x, pltpu.HBM) for x in (source, propagator, transmission, upgoing)]
    return pl.pallas_call(
        functools.partial(first_kernel, part),
        in_specs=[pl.BlockSpec(memory_space=pltpu.SMEM)] * 2 + [pl.BlockSpec(memory_space=pltpu.HBM)] * 4,
        out_specs=[whole] * (chunks + 3),
        out_shape=[jax.ShapeDtypeStruct((2 * part, width), jnp.bfloat16)] * chunks
        + [
            pltpu.VMEM((width, 2 * width), jnp.bfloat16),
            jax.ShapeDtypeStruct((width, shots), jnp.bfloat16),
            jax.ShapeDtypeStruct((2, width // 2, shots), jnp.bfloat16),
        ],
        scratch_shapes=[
            pltpu.VMEM((width, shots), jnp.bfloat16),
            pltpu.VMEM((1, width), jnp.float32),
            pltpu.SemaphoreType.DMA((5,)),
            pltpu.SemaphoreType.DMA((4, 2)),
            pltpu.SemaphoreType.DMA((groups,)),
        ],
        compiler_params=pltpu.CompilerParams(vmem_limit_bytes=LIMIT),
        cost_estimate=pl.CostEstimate(
            flops=4 * width * width * shots, bytes_accessed=4 * width * (width + 2 * shots), transcendentals=0
        ),
    )(level, mine, *pinned)


def second_kernel(part, joined_ref, right_ref, factor_ref, *outs):
    width = joined_ref.shape[0]
    wide = width // 4
    for n in range(4):
        columns = slice(n * wide, (n + 1) * wide)
        real, imag = joined_ref[columns, :width], joined_ref[columns, width:]
        start_panels(part, real, imag, right_ref[...], factor_ref[:, columns], outs, columns)


def second_advance(joined, right, factor, part):
    width, shots = right.shape
    outs = [jax.ShapeDtypeStruct((2 * part, width), jnp.bfloat16)] * (shots // 2 // part)
    joined = pltpu.with_memory_space_constraint(joined, pltpu.VMEM)
    return whole_call(functools.partial(second_kernel, part), (joined, right, factor), outs, 4 * width * width * shots)


def advance_kernel(level_ref, arrived_ref, ready_ref, joined_ref, factor_ref, out_ref, both):
    part = arrived_ref.shape[0] // 2
    width = arrived_ref.shape[1]
    wide = width // 4

    @pl.when(level_ref[0] == 0)
    def _():
        out_ref[...] = ready_ref[...]

    @pl.when(level_ref[0] != 0)
    def _():
        both[:, :width] = arrived_ref[...]
        both[:part, width:] = -arrived_ref[part:]
        both[part:, width:] = arrived_ref[:part]
        for n in range(4):
            columns = slice(n * wide, (n + 1) * wide)
            out = lax.dot_general(
                joined_ref[columns], both[...], (((1,), (1,)), ((), ())), preferred_element_type=jnp.float32
            )
            out_ref[:, columns] = (out.T * factor_ref[:, columns]).astype(jnp.bfloat16)


def advance(level, arrived, ready, joined, factor):
    rows, width = arrived.shape
    joined = pltpu.with_memory_space_constraint(joined, pltpu.VMEM)
    out = jax.ShapeDtypeStruct((rows, width), jnp.bfloat16)
    args = (arrived, ready, joined, factor)
    scratch = [pltpu.VMEM((rows, 2 * width), jnp.bfloat16)]
    return whole_call(advance_kernel, args, [out], 4 * rows * width * width, (level,), scratch)[0]


def stack_kernel(*refs):
    *panels, out_ref = refs
    rows = panels[0].shape[0]
    for at, panel in enumerate(panels):
        out_ref[at * rows : (at + 1) * rows] = panel[...]


def stacked(panels):
    rows, width = panels[0].shape
    out = jax.ShapeDtypeStruct((len(panels) * rows, width), panels[0].dtype)
    return whole_call(stack_kernel, panels, [out], 0)[0]


def operand_kernel(own_ref, got_ref, out_ref):
    rows, shots = own_ref.shape[1:]
    half = shots // STREAMS
    for which, ref in enumerate((own_ref, got_ref)):
        real, imag = ref[0], ref[1]
        minus = -real
        for stream in range(STREAMS):
            lanes = slice(stream * half, (stream + 1) * half)
            left = 2 * (which * shots + stream * half)
            out_ref[:rows, left : left + half] = real[:, lanes]
            out_ref[:rows, left + half : left + 2 * half] = imag[:, lanes]
            out_ref[rows:, left : left + half] = imag[:, lanes]
            out_ref[rows:, left + half : left + 2 * half] = minus[:, lanes]


def operand(mine, own, got, rows):
    shots = own.shape[2]
    blocks = got.shape[1] // rows
    groups = blocks // 2

    def spot(i, mine_ref, stride):
        group, place, core = places(mine_ref)
        other = lax.rem(lax.div(i, groups) + core, 2)
        block = stride * lax.rem(group + lax.rem(i, groups), groups) + other
        return block + 2 * place if stride == 4 else block

    return pl.pallas_call(
        lambda _, *refs: operand_kernel(*refs),
        grid_spec=pltpu.PrefetchScalarGridSpec(
            num_scalar_prefetch=1,
            grid=(blocks,),
            in_specs=[
                pl.BlockSpec((2, rows, shots), lambda i, mine_ref: (0, spot(i, mine_ref, 4), 0)),
                pl.BlockSpec((2, rows, shots), lambda i, mine_ref: (0, spot(i, mine_ref, 2), 0)),
            ],
            out_specs=pl.BlockSpec((2 * rows, 4 * shots), lambda i, mine_ref: (i, 0)),
        ),
        out_shape=jax.ShapeDtypeStruct((2 * rows * blocks, 4 * shots), jnp.bfloat16),
        compiler_params=pltpu.CompilerParams(vmem_limit_bytes=LIMIT),
        cost_estimate=pl.CostEstimate(flops=0, bytes_accessed=24 * rows * blocks * shots, transcendentals=0),
    )(mine, own, got)


def gather(levels, level_ref, panels, joined):
    part = joined.shape[0] // len(panels) // 2
    half = STEPS * part
    first = lax.rem(levels - 1 - level_ref[0], STEPS)
    for at, (ref, top) in enumerate(panels):
        base = at // STEPS * 2 * half
        row = pl.multiple_of(lax.rem(first + at, STEPS) * part, part)
        joined[pl.ds(base + row, part)] = ref[top : top + part]
        joined[pl.ds(base + half + row, part)] = ref[top + part : top + 2 * part]


def crossed(refs, counts, stream):
    rows = refs[0].shape[0] // counts[0]
    panels = [(ref, at * rows) for ref, count in zip(refs, counts) for at in range(count)]
    return panels[stream::STREAMS]


def early_kernel(levels, counts, level_ref, left_ref, *refs):
    *panels, out_ref, joined = refs
    own, other = panels[: STREAMS * STEPS], panels[STREAMS * STEPS :]
    gather(levels, level_ref, [(ref, 0) for ref in own] + crossed(other, counts, 0), joined)
    deep = joined.shape[0]
    wide = out_ref.shape[1] // 4
    for n in range(4):
        columns = slice(n * wide, (n + 1) * wide)
        out_ref[:, columns] = jnp.dot(left_ref[:, :deep], joined[:, columns], preferred_element_type=jnp.float32)


def late_kernel(levels, counts, level_ref, left_ref, early_ref, *refs):
    *panels, keep_ref, own_ref, send_ref, joined = refs
    gather(levels, level_ref, crossed(panels[:-1], counts[:-1], 1) + [(panels[-1], 0)], joined)
    start = left_ref.shape[1] - joined.shape[0]
    groups, _, rows, width = keep_ref.shape
    wide = width // 4
    for n in range(4):
        columns = slice(n * wide, (n + 1) * wide)
        out = early_ref[:, columns] + jnp.dot(
            left_ref[:, start:], joined[:, columns], preferred_element_type=jnp.float32
        )
        for k in range(groups):
            for part in range(2):
                lo = (2 * k + part) * rows
                keep_ref[k, part, :, columns] = out[lo : lo + rows]
                lo += 2 * groups * rows
                to_ref, at = (send_ref, k - 1) if k else (own_ref, 0)
                to_ref[at, part, :, columns] = out[lo : lo + rows].astype(jnp.bfloat16)


def whole_call(kernel, args, outs, flops, scalars=(), scratch=()):
    whole = pl.BlockSpec(memory_space=pltpu.VMEM)
    size = sum(math.prod(x.shape) * x.dtype.itemsize for x in (*args, *outs))
    return pl.pallas_call(
        kernel,
        in_specs=[pl.BlockSpec(memory_space=pltpu.SMEM)] * len(scalars) + [whole] * len(args),
        out_specs=[whole] * len(outs),
        out_shape=outs,
        scratch_shapes=scratch,
        compiler_params=pltpu.CompilerParams(vmem_limit_bytes=LIMIT),
        cost_estimate=pl.CostEstimate(flops=flops, bytes_accessed=size, transcendentals=0),
    )(*scalars, *args)


def early_terms(level, left, panels, levels, counts):
    width = panels[0].shape[1]
    deep = left.shape[1] - panels[-1].shape[0] * STEPS
    out = jax.ShapeDtypeStruct((left.shape[0], width), jnp.float32)
    kernel = functools.partial(early_kernel, levels, counts)
    scratch = [pltpu.VMEM((deep, width), jnp.bfloat16)]
    return whole_call(kernel, (left, *panels), [out], 2 * deep * left.shape[0] * width, (level,), scratch)[0]


def late_terms(level, left, early, panels, rows, levels, counts):
    width = early.shape[1]
    deep = panels[-1].shape[0] * STEPS
    groups = left.shape[0] // (4 * rows)
    outs = [jax.ShapeDtypeStruct((groups, 2, rows, width), jnp.float32)] + [
        jax.ShapeDtypeStruct((count, 2, rows, width), jnp.bfloat16) for count in (1, groups - 1)
    ]
    kernel = functools.partial(late_kernel, levels, counts)
    scratch = [pltpu.VMEM((deep, width), jnp.bfloat16)]
    return whole_call(kernel, (left, early, *panels), outs, 2 * deep * left.shape[0] * width, (level,), scratch)


def last_kernel(scale, *refs):
    *parts, out_ref, total, sems = refs
    pieces = sems.shape[0]
    tall = total.shape[0] // pieces
    copies = []
    for piece in range(pieces):
        rows = slice(piece * tall, (piece + 1) * tall)
        for part in range(2):
            out = parts[0][0, part, rows]
            for ref in parts[1:]:
                out += ref[0, part, rows].astype(jnp.float32)
            total[rows, part] = out * scale
        span = pl.ds(piece * tall, tall)
        copies.append(pltpu.make_async_copy(total.at[span], out_ref.at[0, span], sems.at[piece]))
        copies[-1].start()
    for copy in copies:
        copy.wait()


def last_sum(parts, scale):
    rows, width = parts[0].shape[2:]
    return pl.pallas_call(
        functools.partial(last_kernel, scale),
        in_specs=[pl.BlockSpec(memory_space=pltpu.VMEM)] * len(parts),
        out_specs=pl.BlockSpec(memory_space=pltpu.HBM),
        out_shape=jax.ShapeDtypeStruct((1, rows, 2, width), jnp.float32),
        scratch_shapes=[pltpu.VMEM((rows, 2, width), jnp.float32), pltpu.SemaphoreType.DMA((4,))],
        compiler_params=pltpu.CompilerParams(vmem_limit_bytes=LIMIT),
        cost_estimate=pl.CostEstimate(
            flops=2 * len(parts) * rows * width, bytes_accessed=16 * rows * width, transcendentals=0
        ),
    )(*parts)


def shards(source, propagator, transmission, upgoing):
    factor = transmission[0]
    upward = upgoing[0, 0]
    width = propagator.shape[3]
    shots = source.shape[3]
    levels = lax.axis_size("depth")
    freqs = lax.axis_size("freq")
    groups = freqs // 4
    rows = width // freqs
    part = shots // STREAMS // STEPS
    level, mine = (lax.axis_index(axis).astype(jnp.int32).reshape(1) for axis in ("depth", "freq"))
    *ready, joined, later, asked = first_advance(level, mine, source, propagator, transmission, upgoing, part, groups)
    ready = [ready, second_advance(joined, later, factor, part)]
    got = swapped(asked, "freq", 2)
    left = operand(mine, upward, got, rows)

    steps = STEPS + levels - 1
    flying = [None] * STREAMS
    own = [[] for _ in range(STREAMS)]
    waiting = []
    crossing = []
    for event in range(STREAMS * steps):
        step, stream = divmod(event, STREAMS)
        out = ready[stream][step % STEPS]
        if step >= 1:
            arrived = flying[stream]
            if event == steps:
                arrived, left = lax.optimization_barrier((arrived, left))
            for at, (sent, panel) in enumerate(crossing):
                if event == sent + BEHIND + (at == 0):
                    arrived, panel = lax.optimization_barrier((arrived, panel))
                    crossing[at] = (sent, panel)
            out = advance(level, arrived, out, joined, factor)
        if step + 1 < steps:
            flying[stream] = ring(out, "depth", 1)
        if step >= levels - 1:
            own[stream].append(out)
            if step == steps - 1:
                crossing.append((event, swapped(out, "freq", 2)))
            else:
                waiting.append(out)
                if len(waiting) == TOGETHER:
                    crossing.append((event, swapped(stacked(waiting), "freq", 2)))
                    waiting = []
    other = [panel for _, panel in crossing]
    counts = [panel.shape[0] // out.shape[0] for panel in other]
    early = early_terms(level, left, own[0] + own[1] + other[:-1], levels, counts[:-1])
    late = late_terms(level, left, early, other[:-2] + other[-1:], rows, levels, counts[:-2] + counts[-1:])
    keep, send_own, send = late
    near = swapped(send, "freq", 1)
    send_own, near = lax.optimization_barrier((send_own, near))
    parts = [keep, swapped(send_own, "freq", 1)]
    for k in range(1, groups):
        total = (keep[k : k + 1] + near[k - 1 : k].astype(jnp.float32)).astype(jnp.bfloat16)
        parts.append(ring(total, "freq", 4 * k))
    return last_sum(parts, (2.0 * shots * freqs) ** (-0.5))


def solution(mesh):
    return jax.shard_map(
        shards,
        mesh=mesh,
        in_specs=(
            P("freq", None, None, None),
            P("depth", "freq", None, None, None),
            P("depth", "freq", None),
            P("depth", "freq", None, None, None),
        ),
        out_specs=P("depth", "freq", None, None),
        check_vma=False,
    )
```

```python
import functools
import math

import jax
import jax.numpy as jnp
from jax import lax
from jax.experimental import pallas as pl
from jax.experimental.pallas import tpu as pltpu
from jax.sharding import PartitionSpec as P

STEPS = 4
STREAMS = 2
BEHIND = 3
TOGETHER = 2
LIMIT = 16 * 1024 * 1024


def ring(block, axis, distance):
    size = lax.axis_size(axis)
    return lax.ppermute(block, axis, [(i, (i + distance) % size) for i in range(size)])


def swapped(block, axis, bit):
    return lax.ppermute(block, axis, [(i, i ^ bit) for i in range(lax.axis_size(axis))])


def places(mine_ref):
    mine = mine_ref[0]
    return lax.div(mine, 4), lax.rem(lax.div(mine, 2), 2), lax.rem(mine, 2)


def start_panels(part, real, imag, right, factor, outs, columns):
    dot = functools.partial(jnp.dot, preferred_element_type=jnp.float32)
    shots = right.shape[1] // 2
    first, second = dot(real, right), dot(imag, right)
    out_real = ((first[:, :shots] - second[:, shots:]).T * factor).astype(jnp.bfloat16)
    out_imag = ((first[:, shots:] + second[:, :shots]).T * factor).astype(jnp.bfloat16)
    for chunk, out in enumerate(outs):
        lo = chunk * part
        out[:part, columns] = out_real[lo : lo + part]
        out[part:, columns] = out_imag[lo : lo + part]


def first_kernel(part, level_ref, mine_ref, source_ref, weight_ref, factor_ref, upward_ref, *refs):
    *outs, joined_ref, later_ref, asked_ref, right, factor, sem, sems, asked_sems = refs
    width = joined_ref.shape[0]
    shots = later_ref.shape[1] // 2
    blocks = sems.shape[0]
    wide = width // blocks
    groups = asked_sems.shape[0]
    tall = asked_ref.shape[1] // groups
    _, place, _ = places(mine_ref)

    def copies(n):
        rows = pl.ds(n * wide, wide)
        return [
            pltpu.make_async_copy(
                weight_ref.at[0, 0, half, rows], joined_ref.at[rows, pl.ds(half * width, width)], sems.at[n, half]
            )
            for half in range(2)
        ]

    def columns_of(start, to_ref, first_sem):
        return [
            pltpu.make_async_copy(
                source_ref.at[0, half, :, pl.ds(start, shots)],
                to_ref.at[:, pl.ds(half * shots, shots)],
                sem.at[first_sem + half],
            )
            for half in range(2)
        ]

    begin = columns_of(0, right, 0) + [pltpu.make_async_copy(factor_ref.at[0], factor, sem.at[4])]
    rest = columns_of(shots, later_ref, 2)
    for k in range(groups):
        row = pl.multiple_of((2 * k + 1 - place) * tall, tall)
        rest.append(
            pltpu.make_async_copy(
                upward_ref.at[0, 0, :, pl.ds(row, tall)], asked_ref.at[:, pl.ds(k * tall, tall)], asked_sems.at[k]
            )
        )
    for copy in begin:
        copy.start()
    for n in range(blocks):
        for copy in copies(n):
            copy.start()
    for copy in rest:
        copy.start()
    for copy in begin:
        copy.wait()
    for n in range(blocks):
        for copy in copies(n):
            copy.wait()
        columns = slice(n * wide, (n + 1) * wide)
        real, imag = joined_ref[columns, :width], joined_ref[columns, width:]
        start_panels(part, real, imag, right[...], factor[:, columns], outs, columns)
    for copy in rest:
        copy.wait()


def first_advance(level, mine, source, propagator, transmission, upgoing, part, groups):
    width = propagator.shape[3]
    shots = source.shape[3]
    chunks = shots // 2 // part
    whole = pl.BlockSpec(memory_space=pltpu.VMEM)
    pinned = [pltpu.with_memory_space_constraint(x, pltpu.HBM) for x in (source, propagator, transmission, upgoing)]
    return pl.pallas_call(
        functools.partial(first_kernel, part),
        in_specs=[pl.BlockSpec(memory_space=pltpu.SMEM)] * 2 + [pl.BlockSpec(memory_space=pltpu.HBM)] * 4,
        out_specs=[whole] * (chunks + 3),
        out_shape=[jax.ShapeDtypeStruct((2 * part, width), jnp.bfloat16)] * chunks
        + [
            pltpu.VMEM((width, 2 * width), jnp.bfloat16),
            jax.ShapeDtypeStruct((width, shots), jnp.bfloat16),
            jax.ShapeDtypeStruct((2, width // 2, shots), jnp.bfloat16),
        ],
        scratch_shapes=[
            pltpu.VMEM((width, shots), jnp.bfloat16),
            pltpu.VMEM((1, width), jnp.float32),
            pltpu.SemaphoreType.DMA((5,)),
            pltpu.SemaphoreType.DMA((4, 2)),
            pltpu.SemaphoreType.DMA((groups,)),
        ],
        compiler_params=pltpu.CompilerParams(vmem_limit_bytes=LIMIT),
        cost_estimate=pl.CostEstimate(
            flops=4 * width * width * shots, bytes_accessed=4 * width * (width + 2 * shots), transcendentals=0
        ),
    )(level, mine, *pinned)


def second_kernel(part, joined_ref, right_ref, factor_ref, *outs):
    width = joined_ref.shape[0]
    wide = width // 4
    for n in range(4):
        columns = slice(n * wide, (n + 1) * wide)
        real, imag = joined_ref[columns, :width], joined_ref[columns, width:]
        start_panels(part, real, imag, right_ref[...], factor_ref[:, columns], outs, columns)


def second_advance(joined, right, factor, part):
    width, shots = right.shape
    outs = [jax.ShapeDtypeStruct((2 * part, width), jnp.bfloat16)] * (shots // 2 // part)
    joined = pltpu.with_memory_space_constraint(joined, pltpu.VMEM)
    return whole_call(functools.partial(second_kernel, part), (joined, right, factor), outs, 4 * width * width * shots)


def advance_kernel(level_ref, arrived_ref, ready_ref, joined_ref, factor_ref, out_ref, both):
    part = arrived_ref.shape[0] // 2
    width = arrived_ref.shape[1]

    @pl.when(level_ref[0] == 0)
    def _():
        out_ref[...] = ready_ref[...]

    @pl.when(level_ref[0] != 0)
    def _():
        both[:, :width] = arrived_ref[...]
        both[:part, width:] = -arrived_ref[part:]
        both[part:, width:] = arrived_ref[:part]
        out = lax.dot_general(
            joined_ref[...], both[...], (((1,), (1,)), ((), ())), preferred_element_type=jnp.float32
        )
        out_ref[...] = (out.T * factor_ref[...]).astype(jnp.bfloat16)


def advance(level, arrived, ready, joined, factor):
    rows, width = arrived.shape
    joined = pltpu.with_memory_space_constraint(joined, pltpu.VMEM)
    out = jax.ShapeDtypeStruct((rows, width), jnp.bfloat16)
    args = (arrived, ready, joined, factor)
    scratch = [pltpu.VMEM((rows, 2 * width), jnp.bfloat16)]
    return whole_call(advance_kernel, args, [out], 4 * rows * width * width, (level,), scratch)[0]


def stack_kernel(*refs):
    *panels, out_ref = refs
    rows = panels[0].shape[0]
    for at, panel in enumerate(panels):
        out_ref[at * rows : (at + 1) * rows] = panel[...]


def stacked(panels):
    rows, width = panels[0].shape
    out = jax.ShapeDtypeStruct((len(panels) * rows, width), panels[0].dtype)
    return whole_call(stack_kernel, panels, [out], 0)[0]


def operand_kernel(own_ref, got_ref, out_ref):
    rows, shots = own_ref.shape[1:]
    half = shots // STREAMS
    for which, ref in enumerate((own_ref, got_ref)):
        real, imag = ref[0], ref[1]
        minus = -real
        for stream in range(STREAMS):
            lanes = slice(stream * half, (stream + 1) * half)
            left = 2 * (which * shots + stream * half)
            out_ref[:rows, left : left + half] = real[:, lanes]
            out_ref[:rows, left + half : left + 2 * half] = imag[:, lanes]
            out_ref[rows:, left : left + half] = imag[:, lanes]
            out_ref[rows:, left + half : left + 2 * half] = minus[:, lanes]


def operand(mine, own, got, rows):
    shots = own.shape[2]
    blocks = got.shape[1] // rows
    groups = blocks // 2

    def spot(i, mine_ref, stride):
        group, place, core = places(mine_ref)
        other = lax.rem(lax.div(i, groups) + core, 2)
        block = stride * lax.rem(group + lax.rem(i, groups), groups) + other
        return block + 2 * place if stride == 4 else block

    return pl.pallas_call(
        lambda _, *refs: operand_kernel(*refs),
        grid_spec=pltpu.PrefetchScalarGridSpec(
            num_scalar_prefetch=1,
            grid=(blocks,),
            in_specs=[
                pl.BlockSpec((2, rows, shots), lambda i, mine_ref: (0, spot(i, mine_ref, 4), 0)),
                pl.BlockSpec((2, rows, shots), lambda i, mine_ref: (0, spot(i, mine_ref, 2), 0)),
            ],
            out_specs=pl.BlockSpec((2 * rows, 4 * shots), lambda i, mine_ref: (i, 0)),
        ),
        out_shape=jax.ShapeDtypeStruct((2 * rows * blocks, 4 * shots), jnp.bfloat16),
        compiler_params=pltpu.CompilerParams(vmem_limit_bytes=LIMIT),
        cost_estimate=pl.CostEstimate(flops=0, bytes_accessed=24 * rows * blocks * shots, transcendentals=0),
    )(mine, own, got)


def gather(levels, level_ref, panels, joined):
    part = joined.shape[0] // len(panels) // 2
    half = STEPS * part
    first = lax.rem(levels - 1 - level_ref[0], STEPS)
    for at, (ref, top) in enumerate(panels):
        base = at // STEPS * 2 * half
        row = pl.multiple_of(lax.rem(first + at, STEPS) * part, part)
        joined[pl.ds(base + row, part)] = ref[top : top + part]
        joined[pl.ds(base + half + row, part)] = ref[top + part : top + 2 * part]


def crossed(refs, counts, stream):
    rows = refs[0].shape[0] // counts[0]
    panels = [(ref, at * rows) for ref, count in zip(refs, counts) for at in range(count)]
    return panels[stream::STREAMS]


def early_kernel(levels, counts, level_ref, left_ref, *refs):
    *panels, out_ref, joined = refs
    own, other = panels[: STREAMS * STEPS], panels[STREAMS * STEPS :]
    gather(levels, level_ref, [(ref, 0) for ref in own] + crossed(other, counts, 0), joined)
    deep = joined.shape[0]
    wide = out_ref.shape[1] // 4
    for n in range(4):
        columns = slice(n * wide, (n + 1) * wide)
        out_ref[:, columns] = jnp.dot(left_ref[:, :deep], joined[:, columns], preferred_element_type=jnp.float32)


def late_kernel(levels, counts, level_ref, left_ref, early_ref, *refs):
    *panels, keep_ref, own_ref, send_ref, joined = refs
    gather(levels, level_ref, crossed(panels[:-1], counts[:-1], 1) + [(panels[-1], 0)], joined)
    start = left_ref.shape[1] - joined.shape[0]
    groups, _, rows, width = keep_ref.shape
    wide = width // 4
    for n in range(4):
        columns = slice(n * wide, (n + 1) * wide)
        out = early_ref[:, columns] + jnp.dot(
            left_ref[:, start:], joined[:, columns], preferred_element_type=jnp.float32
        )
        for k in range(groups):
            for part in range(2):
                lo = (2 * k + part) * rows
                keep_ref[k, part, :, columns] = out[lo : lo + rows]
                lo += 2 * groups * rows
                to_ref, at = (send_ref, k - 1) if k else (own_ref, 0)
                to_ref[at, part, :, columns] = out[lo : lo + rows].astype(jnp.bfloat16)


def whole_call(kernel, args, outs, flops, scalars=(), scratch=()):
    whole = pl.BlockSpec(memory_space=pltpu.VMEM)
    size = sum(math.prod(x.shape) * x.dtype.itemsize for x in (*args, *outs))
    return pl.pallas_call(
        kernel,
        in_specs=[pl.BlockSpec(memory_space=pltpu.SMEM)] * len(scalars) + [whole] * len(args),
        out_specs=[whole] * len(outs),
        out_shape=outs,
        scratch_shapes=scratch,
        compiler_params=pltpu.CompilerParams(vmem_limit_bytes=LIMIT),
        cost_estimate=pl.CostEstimate(flops=flops, bytes_accessed=size, transcendentals=0),
    )(*scalars, *args)


def early_terms(level, left, panels, levels, counts):
    width = panels[0].shape[1]
    deep = left.shape[1] - panels[-1].shape[0] * STEPS
    out = jax.ShapeDtypeStruct((left.shape[0], width), jnp.float32)
    kernel = functools.partial(early_kernel, levels, counts)
    scratch = [pltpu.VMEM((deep, width), jnp.bfloat16)]
    return whole_call(kernel, (left, *panels), [out], 2 * deep * left.shape[0] * width, (level,), scratch)[0]


def late_terms(level, left, early, panels, rows, levels, counts):
    width = early.shape[1]
    deep = panels[-1].shape[0] * STEPS
    groups = left.shape[0] // (4 * rows)
    outs = [jax.ShapeDtypeStruct((groups, 2, rows, width), jnp.float32)] + [
        jax.ShapeDtypeStruct((count, 2, rows, width), jnp.bfloat16) for count in (1, groups - 1)
    ]
    kernel = functools.partial(late_kernel, levels, counts)
    scratch = [pltpu.VMEM((deep, width), jnp.bfloat16)]
    return whole_call(kernel, (left, early, *panels), outs, 2 * deep * left.shape[0] * width, (level,), scratch)


def last_kernel(scale, *refs):
    *parts, out_ref, total, sems = refs
    pieces = sems.shape[0]
    tall = total.shape[0] // pieces
    copies = []
    for piece in range(pieces):
        rows = slice(piece * tall, (piece + 1) * tall)
        for part in range(2):
            out = parts[0][0, part, rows]
            for ref in parts[1:]:
                out += ref[0, part, rows].astype(jnp.float32)
            total[rows, part] = out * scale
        span = pl.ds(piece * tall, tall)
        copies.append(pltpu.make_async_copy(total.at[span], out_ref.at[0, span], sems.at[piece]))
        copies[-1].start()
    for copy in copies:
        copy.wait()


def last_sum(parts, scale):
    rows, width = parts[0].shape[2:]
    return pl.pallas_call(
        functools.partial(last_kernel, scale),
        in_specs=[pl.BlockSpec(memory_space=pltpu.VMEM)] * len(parts),
        out_specs=pl.BlockSpec(memory_space=pltpu.HBM),
        out_shape=jax.ShapeDtypeStruct((1, rows, 2, width), jnp.float32),
        scratch_shapes=[pltpu.VMEM((rows, 2, width), jnp.float32), pltpu.SemaphoreType.DMA((4,))],
        compiler_params=pltpu.CompilerParams(vmem_limit_bytes=LIMIT),
        cost_estimate=pl.CostEstimate(
            flops=2 * len(parts) * rows * width, bytes_accessed=16 * rows * width, transcendentals=0
        ),
    )(*parts)


def shards(source, propagator, transmission, upgoing):
    factor = transmission[0]
    upward = upgoing[0, 0]
    width = propagator.shape[3]
    shots = source.shape[3]
    levels = lax.axis_size("depth")
    freqs = lax.axis_size("freq")
    groups = freqs // 4
    rows = width // freqs
    part = shots // STREAMS // STEPS
    level, mine = (lax.axis_index(axis).astype(jnp.int32).reshape(1) for axis in ("depth", "freq"))
    *ready, joined, later, asked = first_advance(level, mine, source, propagator, transmission, upgoing, part, groups)
    ready = [ready, second_advance(joined, later, factor, part)]
    got = swapped(asked, "freq", 2)
    left = operand(mine, upward, got, rows)

    steps = STEPS + levels - 1
    flying = [None] * STREAMS
    own = [[] for _ in range(STREAMS)]
    waiting = []
    crossing = []
    for event in range(STREAMS * steps):
        step, stream = divmod(event, STREAMS)
        out = ready[stream][step % STEPS]
        if step >= 1:
            arrived = flying[stream]
            if event == steps:
                arrived, left = lax.optimization_barrier((arrived, left))
            for at, (sent, panel) in enumerate(crossing):
                if event == sent + BEHIND + (at == 0):
                    arrived, panel = lax.optimization_barrier((arrived, panel))
                    crossing[at] = (sent, panel)
            out = advance(level, arrived, out, joined, factor)
        if step + 1 < steps:
            flying[stream] = ring(out, "depth", 1)
        if step >= levels - 1:
            own[stream].append(out)
            if step == steps - 1:
                crossing.append((event, swapped(out, "freq", 2)))
            else:
                waiting.append(out)
                if len(waiting) == TOGETHER:
                    crossing.append((event, swapped(stacked(waiting), "freq", 2)))
                    waiting = []
    other = [panel for _, panel in crossing]
    counts = [panel.shape[0] // out.shape[0] for panel in other]
    early = early_terms(level, left, own[0] + own[1] + other[:-1], levels, counts[:-1])
    late = late_terms(level, left, early, other[:-2] + other[-1:], rows, levels, counts[:-2] + counts[-1:])
    keep, send_own, send = late
    near = swapped(send, "freq", 1)
    send_own, near = lax.optimization_barrier((send_own, near))
    parts = [keep, swapped(send_own, "freq", 1)]
    for k in range(1, groups):
        total = (keep[k : k + 1] + near[k - 1 : k].astype(jnp.float32)).astype(jnp.bfloat16)
        parts.append(ring(total, "freq", 4 * k))
    return last_sum(parts, (2.0 * shots * freqs) ** (-0.5))


def solution(mesh):
    return jax.shard_map(
        shards,
        mesh=mesh,
        in_specs=(
            P("freq", None, None, None),
            P("depth", "freq", None, None, None),
            P("depth", "freq", None),
            P("depth", "freq", None, None, None),
        ),
        out_specs=P("depth", "freq", None, None),
        check_vma=False,
    )
```

```python
import functools
import math

import jax
import jax.numpy as jnp
from jax import lax
from jax.experimental import pallas as pl
from jax.experimental.pallas import tpu as pltpu
from jax.sharding import PartitionSpec as P

STEPS = 4
STREAMS = 2
BEHIND = 3
TOGETHER = 2
LIMIT = 16 * 1024 * 1024


def ring(block, axis, distance):
    size = lax.axis_size(axis)
    return lax.ppermute(block, axis, [(i, (i + distance) % size) for i in range(size)])


def swapped(block, axis, bit):
    return lax.ppermute(block, axis, [(i, i ^ bit) for i in range(lax.axis_size(axis))])


def places(mine_ref):
    mine = mine_ref[0]
    return lax.div(mine, 4), lax.rem(lax.div(mine, 2), 2), lax.rem(mine, 2)


def start_panels(part, real, imag, right, factor, outs, columns):
    dot = functools.partial(jnp.dot, preferred_element_type=jnp.float32)
    shots = right.shape[1] // 2
    first, second = dot(real, right), dot(imag, right)
    out_real = ((first[:, :shots] - second[:, shots:]).T * factor).astype(jnp.bfloat16)
    out_imag = ((first[:, shots:] + second[:, :shots]).T * factor).astype(jnp.bfloat16)
    for chunk, out in enumerate(outs):
        lo = chunk * part
        out[:part, columns] = out_real[lo : lo + part]
        out[part:, columns] = out_imag[lo : lo + part]


def first_kernel(part, level_ref, mine_ref, source_ref, weight_ref, factor_ref, upward_ref, *refs):
    *outs, joined_ref, later_ref, asked_ref, right, factor, sem, sems, asked_sems = refs
    width = joined_ref.shape[0]
    shots = later_ref.shape[1] // 2
    blocks = sems.shape[0]
    wide = width // blocks
    groups = asked_sems.shape[0]
    tall = asked_ref.shape[1] // groups
    _, place, _ = places(mine_ref)

    def copies(n):
        rows = pl.ds(n * wide, wide)
        return [
            pltpu.make_async_copy(
                weight_ref.at[0, 0, half, rows], joined_ref.at[rows, pl.ds(half * width, width)], sems.at[n, half]
            )
            for half in range(2)
        ]

    def columns_of(start, to_ref, first_sem):
        return [
            pltpu.make_async_copy(
                source_ref.at[0, half, :, pl.ds(start, shots)],
                to_ref.at[:, pl.ds(half * shots, shots)],
                sem.at[first_sem + half],
            )
            for half in range(2)
        ]

    begin = columns_of(0, right, 0) + [pltpu.make_async_copy(factor_ref.at[0], factor, sem.at[4])]
    rest = columns_of(shots, later_ref, 2)
    for k in range(groups):
        row = pl.multiple_of((2 * k + 1 - place) * tall, tall)
        rest.append(
            pltpu.make_async_copy(
                upward_ref.at[0, 0, :, pl.ds(row, tall)], asked_ref.at[:, pl.ds(k * tall, tall)], asked_sems.at[k]
            )
        )
    for copy in begin + copies(0) + copies(1):
        copy.start()
    for copy in begin:
        copy.wait()
    for n in range(blocks):
        for copy in copies(n):
            copy.wait()
        for copy in copies(n + 2) if n + 2 < blocks else rest if n + 2 == blocks else []:
            copy.start()
        columns = slice(n * wide, (n + 1) * wide)
        real, imag = joined_ref[columns, :width], joined_ref[columns, width:]
        start_panels(part, real, imag, right[...], factor[:, columns], outs, columns)
    for copy in rest:
        copy.wait()


def first_advance(level, mine, source, propagator, transmission, upgoing, part, groups):
    width = propagator.shape[3]
    shots = source.shape[3]
    chunks = shots // 2 // part
    whole = pl.BlockSpec(memory_space=pltpu.VMEM)
    pinned = [pltpu.with_memory_space_constraint(x, pltpu.HBM) for x in (source, propagator, transmission, upgoing)]
    return pl.pallas_call(
        functools.partial(first_kernel, part),
        in_specs=[pl.BlockSpec(memory_space=pltpu.SMEM)] * 2 + [pl.BlockSpec(memory_space=pltpu.HBM)] * 4,
        out_specs=[whole] * (chunks + 3),
        out_shape=[jax.ShapeDtypeStruct((2 * part, width), jnp.bfloat16)] * chunks
        + [
            pltpu.VMEM((width, 2 * width), jnp.bfloat16),
            jax.ShapeDtypeStruct((width, shots), jnp.bfloat16),
            jax.ShapeDtypeStruct((2, width // 2, shots), jnp.bfloat16),
        ],
        scratch_shapes=[
            pltpu.VMEM((width, shots), jnp.bfloat16),
            pltpu.VMEM((1, width), jnp.float32),
            pltpu.SemaphoreType.DMA((5,)),
            pltpu.SemaphoreType.DMA((4, 2)),
            pltpu.SemaphoreType.DMA((groups,)),
        ],
        compiler_params=pltpu.CompilerParams(vmem_limit_bytes=LIMIT),
        cost_estimate=pl.CostEstimate(
            flops=4 * width * width * shots, bytes_accessed=4 * width * (width + 2 * shots), transcendentals=0
        ),
    )(level, mine, *pinned)


def second_kernel(part, joined_ref, right_ref, factor_ref, *outs):
    width = joined_ref.shape[0]
    wide = width // 4
    for n in range(4):
        columns = slice(n * wide, (n + 1) * wide)
        real, imag = joined_ref[columns, :width], joined_ref[columns, width:]
        start_panels(part, real, imag, right_ref[...], factor_ref[:, columns], outs, columns)


def second_advance(joined, right, factor, part):
    width, shots = right.shape
    outs = [jax.ShapeDtypeStruct((2 * part, width), jnp.bfloat16)] * (shots // 2 // part)
    joined = pltpu.with_memory_space_constraint(joined, pltpu.VMEM)
    return whole_call(functools.partial(second_kernel, part), (joined, right, factor), outs, 4 * width * width * shots)


def advance_kernel(level_ref, arrived_ref, ready_ref, joined_ref, factor_ref, out_ref, both):
    part = arrived_ref.shape[0] // 2
    width = arrived_ref.shape[1]

    @pl.when(level_ref[0] == 0)
    def _():
        out_ref[...] = ready_ref[...]

    @pl.when(level_ref[0] != 0)
    def _():
        both[:, :width] = arrived_ref[...]
        both[:part, width:] = -arrived_ref[part:]
        both[part:, width:] = arrived_ref[:part]
        out = lax.dot_general(
            joined_ref[...], both[...], (((1,), (1,)), ((), ())), preferred_element_type=jnp.float32
        )
        out_ref[...] = (out.T * factor_ref[...]).astype(jnp.bfloat16)


def advance(level, arrived, ready, joined, factor):
    rows, width = arrived.shape
    joined = pltpu.with_memory_space_constraint(joined, pltpu.VMEM)
    out = jax.ShapeDtypeStruct((rows, width), jnp.bfloat16)
    args = (arrived, ready, joined, factor)
    scratch = [pltpu.VMEM((rows, 2 * width), jnp.bfloat16)]
    return whole_call(advance_kernel, args, [out], 4 * rows * width * width, (level,), scratch)[0]


def stack_kernel(*refs):
    *panels, out_ref = refs
    rows = panels[0].shape[0]
    for at, panel in enumerate(panels):
        out_ref[at * rows : (at + 1) * rows] = panel[...]


def stacked(panels):
    rows, width = panels[0].shape
    out = jax.ShapeDtypeStruct((len(panels) * rows, width), panels[0].dtype)
    return whole_call(stack_kernel, panels, [out], 0)[0]


def operand_kernel(own_ref, got_ref, out_ref):
    rows, shots = own_ref.shape[1:]
    half = shots // STREAMS
    for which, ref in enumerate((own_ref, got_ref)):
        real, imag = ref[0], ref[1]
        minus = -real
        for stream in range(STREAMS):
            lanes = slice(stream * half, (stream + 1) * half)
            left = 2 * (which * shots + stream * half)
            out_ref[:rows, left : left + half] = real[:, lanes]
            out_ref[:rows, left + half : left + 2 * half] = imag[:, lanes]
            out_ref[rows:, left : left + half] = imag[:, lanes]
            out_ref[rows:, left + half : left + 2 * half] = minus[:, lanes]


def operand(mine, own, got, rows):
    shots = own.shape[2]
    blocks = got.shape[1] // rows
    groups = blocks // 2

    def spot(i, mine_ref, stride):
        group, place, core = places(mine_ref)
        other = lax.rem(lax.div(i, groups) + core, 2)
        block = stride * lax.rem(group + lax.rem(i, groups), groups) + other
        return block + 2 * place if stride == 4 else block

    return pl.pallas_call(
        lambda _, *refs: operand_kernel(*refs),
        grid_spec=pltpu.PrefetchScalarGridSpec(
            num_scalar_prefetch=1,
            grid=(blocks,),
            in_specs=[
                pl.BlockSpec((2, rows, shots), lambda i, mine_ref: (0, spot(i, mine_ref, 4), 0)),
                pl.BlockSpec((2, rows, shots), lambda i, mine_ref: (0, spot(i, mine_ref, 2), 0)),
            ],
            out_specs=pl.BlockSpec((2 * rows, 4 * shots), lambda i, mine_ref: (i, 0)),
        ),
        out_shape=jax.ShapeDtypeStruct((2 * rows * blocks, 4 * shots), jnp.bfloat16),
        compiler_params=pltpu.CompilerParams(vmem_limit_bytes=LIMIT),
        cost_estimate=pl.CostEstimate(flops=0, bytes_accessed=24 * rows * blocks * shots, transcendentals=0),
    )(mine, own, got)


def gather(levels, level_ref, panels, joined):
    part = joined.shape[0] // len(panels) // 2
    half = STEPS * part
    first = lax.rem(levels - 1 - level_ref[0], STEPS)
    for at, (ref, top) in enumerate(panels):
        base = at // STEPS * 2 * half
        row = pl.multiple_of(lax.rem(first + at, STEPS) * part, part)
        joined[pl.ds(base + row, part)] = ref[top : top + part]
        joined[pl.ds(base + half + row, part)] = ref[top + part : top + 2 * part]


def crossed(refs, counts, stream):
    rows = refs[0].shape[0] // counts[0]
    panels = [(ref, at * rows) for ref, count in zip(refs, counts) for at in range(count)]
    return panels[stream::STREAMS]


def early_kernel(levels, counts, level_ref, left_ref, *refs):
    *panels, out_ref, joined = refs
    own, other = panels[: STREAMS * STEPS], panels[STREAMS * STEPS :]
    gather(levels, level_ref, [(ref, 0) for ref in own] + crossed(other, counts, 0), joined)
    deep = joined.shape[0]
    wide = out_ref.shape[1] // 4
    for n in range(4):
        columns = slice(n * wide, (n + 1) * wide)
        out_ref[:, columns] = jnp.dot(left_ref[:, :deep], joined[:, columns], preferred_element_type=jnp.float32)


def late_kernel(levels, counts, level_ref, left_ref, early_ref, *refs):
    *panels, keep_ref, own_ref, send_ref, joined = refs
    gather(levels, level_ref, crossed(panels[:-1], counts[:-1], 1) + [(panels[-1], 0)], joined)
    start = left_ref.shape[1] - joined.shape[0]
    groups, _, rows, width = keep_ref.shape
    wide = width // 4
    for n in range(4):
        columns = slice(n * wide, (n + 1) * wide)
        out = early_ref[:, columns] + jnp.dot(
            left_ref[:, start:], joined[:, columns], preferred_element_type=jnp.float32
        )
        for k in range(groups):
            for part in range(2):
                lo = (2 * k + part) * rows
                keep_ref[k, part, :, columns] = out[lo : lo + rows]
                lo += 2 * groups * rows
                to_ref, at = (send_ref, k - 1) if k else (own_ref, 0)
                to_ref[at, part, :, columns] = out[lo : lo + rows].astype(jnp.bfloat16)


def whole_call(kernel, args, outs, flops, scalars=(), scratch=()):
    whole = pl.BlockSpec(memory_space=pltpu.VMEM)
    size = sum(math.prod(x.shape) * x.dtype.itemsize for x in (*args, *outs))
    return pl.pallas_call(
        kernel,
        in_specs=[pl.BlockSpec(memory_space=pltpu.SMEM)] * len(scalars) + [whole] * len(args),
        out_specs=[whole] * len(outs),
        out_shape=outs,
        scratch_shapes=scratch,
        compiler_params=pltpu.CompilerParams(vmem_limit_bytes=LIMIT),
        cost_estimate=pl.CostEstimate(flops=flops, bytes_accessed=size, transcendentals=0),
    )(*scalars, *args)


def early_terms(level, left, panels, levels, counts):
    width = panels[0].shape[1]
    deep = left.shape[1] - panels[-1].shape[0] * STEPS
    out = jax.ShapeDtypeStruct((left.shape[0], width), jnp.float32)
    kernel = functools.partial(early_kernel, levels, counts)
    scratch = [pltpu.VMEM((deep, width), jnp.bfloat16)]
    return whole_call(kernel, (left, *panels), [out], 2 * deep * left.shape[0] * width, (level,), scratch)[0]


def late_terms(level, left, early, panels, rows, levels, counts):
    width = early.shape[1]
    deep = panels[-1].shape[0] * STEPS
    groups = left.shape[0] // (4 * rows)
    outs = [jax.ShapeDtypeStruct((groups, 2, rows, width), jnp.float32)] + [
        jax.ShapeDtypeStruct((count, 2, rows, width), jnp.bfloat16) for count in (1, groups - 1)
    ]
    kernel = functools.partial(late_kernel, levels, counts)
    scratch = [pltpu.VMEM((deep, width), jnp.bfloat16)]
    return whole_call(kernel, (left, early, *panels), outs, 2 * deep * left.shape[0] * width, (level,), scratch)


def last_kernel(scale, *refs):
    *parts, out_ref, total, sems = refs
    pieces = sems.shape[0]
    tall = total.shape[0] // pieces
    copies = []
    for piece in range(pieces):
        rows = slice(piece * tall, (piece + 1) * tall)
        for part in range(2):
            out = parts[0][0, part, rows]
            for ref in parts[1:]:
                out += ref[0, part, rows].astype(jnp.float32)
            total[rows, part] = out * scale
        span = pl.ds(piece * tall, tall)
        copies.append(pltpu.make_async_copy(total.at[span], out_ref.at[0, span], sems.at[piece]))
        copies[-1].start()
    for copy in copies:
        copy.wait()


def last_sum(parts, scale):
    rows, width = parts[0].shape[2:]
    return pl.pallas_call(
        functools.partial(last_kernel, scale),
        in_specs=[pl.BlockSpec(memory_space=pltpu.VMEM)] * len(parts),
        out_specs=pl.BlockSpec(memory_space=pltpu.HBM),
        out_shape=jax.ShapeDtypeStruct((1, rows, 2, width), jnp.float32),
        scratch_shapes=[pltpu.VMEM((rows, 2, width), jnp.float32), pltpu.SemaphoreType.DMA((4,))],
        compiler_params=pltpu.CompilerParams(vmem_limit_bytes=LIMIT),
        cost_estimate=pl.CostEstimate(
            flops=2 * len(parts) * rows * width, bytes_accessed=16 * rows * width, transcendentals=0
        ),
    )(*parts)


def shards(source, propagator, transmission, upgoing):
    factor = transmission[0]
    upward = upgoing[0, 0]
    width = propagator.shape[3]
    shots = source.shape[3]
    levels = lax.axis_size("depth")
    freqs = lax.axis_size("freq")
    groups = freqs // 4
    rows = width // freqs
    part = shots // STREAMS // STEPS
    level, mine = (lax.axis_index(axis).astype(jnp.int32).reshape(1) for axis in ("depth", "freq"))
    *ready, joined, later, asked = first_advance(level, mine, source, propagator, transmission, upgoing, part, groups)
    ready = [ready, second_advance(joined, later, factor, part)]
    got = swapped(asked, "freq", 2)
    left = operand(mine, upward, got, rows)

    steps = STEPS + levels - 1
    flying = [None] * STREAMS
    own = [[] for _ in range(STREAMS)]
    waiting = []
    crossing = []
    for event in range(STREAMS * steps):
        step, stream = divmod(event, STREAMS)
        out = ready[stream][step % STEPS]
        if step >= 1:
            arrived = flying[stream]
            if event == steps:
                arrived, left = lax.optimization_barrier((arrived, left))
            for at, (sent, panel) in enumerate(crossing):
                if event == sent + BEHIND + (at == 0):
                    arrived, panel = lax.optimization_barrier((arrived, panel))
                    crossing[at] = (sent, panel)
            out = advance(level, arrived, out, joined, factor)
        if step + 1 < steps:
            flying[stream] = ring(out, "depth", 1)
        if step >= levels - 1:
            own[stream].append(out)
            if step == steps - 1:
                crossing.append((event, swapped(out, "freq", 2)))
            else:
                waiting.append(out)
                if len(waiting) == TOGETHER:
                    crossing.append((event, swapped(stacked(waiting), "freq", 2)))
                    waiting = []
    other = [panel for _, panel in crossing]
    counts = [panel.shape[0] // out.shape[0] for panel in other]
    early = early_terms(level, left, own[0] + own[1] + other[:-1], levels, counts[:-1])
    late = late_terms(level, left, early, other[:-2] + other[-1:], rows, levels, counts[:-2] + counts[-1:])
    keep, send_own, send = late
    near = swapped(send, "freq", 1)
    send_own, near = lax.optimization_barrier((send_own, near))
    parts = [keep, swapped(send_own, "freq", 1)]
    for k in range(1, groups):
        total = (keep[k : k + 1] + near[k - 1 : k].astype(jnp.float32)).astype(jnp.bfloat16)
        parts.append(ring(total, "freq", 4 * k))
    return last_sum(parts, (2.0 * shots * freqs) ** (-0.5))


def solution(mesh):
    return jax.shard_map(
        shards,
        mesh=mesh,
        in_specs=(
            P("freq", None, None, None),
            P("depth", "freq", None, None, None),
            P("depth", "freq", None),
            P("depth", "freq", None, None, None),
        ),
        out_specs=P("depth", "freq", None, None),
        check_vma=False,
    )
```

```python
import functools
import math

import jax
import jax.numpy as jnp
from jax import lax
from jax.experimental import pallas as pl
from jax.experimental.pallas import tpu as pltpu
from jax.sharding import PartitionSpec as P

STEPS = 4
STREAMS = 2
BEHIND = 3
TOGETHER = 2
LIMIT = 16 * 1024 * 1024


def ring(block, axis, distance):
    size = lax.axis_size(axis)
    return lax.ppermute(block, axis, [(i, (i + distance) % size) for i in range(size)])


def swapped(block, axis, bit):
    return lax.ppermute(block, axis, [(i, i ^ bit) for i in range(lax.axis_size(axis))])


def places(mine_ref):
    mine = mine_ref[0]
    return lax.div(mine, 4), lax.rem(lax.div(mine, 2), 2), lax.rem(mine, 2)


def start_panels(part, real, imag, right, factor, outs, columns):
    dot = functools.partial(jnp.dot, preferred_element_type=jnp.float32)
    shots = right.shape[1] // 2
    first, second = dot(real, right), dot(imag, right)
    out_real = ((first[:, :shots] - second[:, shots:]).T * factor).astype(jnp.bfloat16)
    out_imag = ((first[:, shots:] + second[:, :shots]).T * factor).astype(jnp.bfloat16)
    for chunk, out in enumerate(outs):
        lo = chunk * part
        out[:part, columns] = out_real[lo : lo + part]
        out[part:, columns] = out_imag[lo : lo + part]


def first_kernel(part, level_ref, mine_ref, source_ref, weight_ref, factor_ref, upward_ref, *refs):
    *outs, joined_ref, later_ref, asked_ref, right, factor, sem, sems, asked_sems = refs
    width = joined_ref.shape[0]
    shots = later_ref.shape[1] // 2
    blocks = sems.shape[0]
    wide = width // blocks
    groups = asked_sems.shape[0]
    tall = asked_ref.shape[1] // groups
    _, place, _ = places(mine_ref)

    def copies(n):
        rows = pl.ds(n * wide, wide)
        return [
            pltpu.make_async_copy(
                weight_ref.at[0, 0, half, rows], joined_ref.at[rows, pl.ds(half * width, width)], sems.at[n, half]
            )
            for half in range(2)
        ]

    def columns_of(start, to_ref, first_sem):
        return [
            pltpu.make_async_copy(
                source_ref.at[0, half, :, pl.ds(start, shots)],
                to_ref.at[:, pl.ds(half * shots, shots)],
                sem.at[first_sem + half],
            )
            for half in range(2)
        ]

    begin = columns_of(0, right, 0) + [pltpu.make_async_copy(factor_ref.at[0], factor, sem.at[4])]
    rest = columns_of(shots, later_ref, 2)
    for k in range(groups):
        row = pl.multiple_of((2 * k + 1 - place) * tall, tall)
        rest.append(
            pltpu.make_async_copy(
                upward_ref.at[0, 0, :, pl.ds(row, tall)], asked_ref.at[:, pl.ds(k * tall, tall)], asked_sems.at[k]
            )
        )
    for copy in begin + copies(0) + copies(1):
        copy.start()
    for copy in begin:
        copy.wait()
    for n in range(blocks):
        for copy in copies(n):
            copy.wait()
        for copy in copies(n + 2) if n + 2 < blocks else rest if n + 2 == blocks else []:
            copy.start()
        columns = slice(n * wide, (n + 1) * wide)
        real, imag = joined_ref[columns, :width], joined_ref[columns, width:]
        start_panels(part, real, imag, right[...], factor[:, columns], outs, columns)
    for copy in rest:
        copy.wait()


def first_advance(level, mine, source, propagator, transmission, upgoing, part, groups):
    width = propagator.shape[3]
    shots = source.shape[3]
    chunks = shots // 2 // part
    whole = pl.BlockSpec(memory_space=pltpu.VMEM)
    pinned = [pltpu.with_memory_space_constraint(x, pltpu.HBM) for x in (source, propagator, transmission, upgoing)]
    return pl.pallas_call(
        functools.partial(first_kernel, part),
        in_specs=[pl.BlockSpec(memory_space=pltpu.SMEM)] * 2 + [pl.BlockSpec(memory_space=pltpu.HBM)] * 4,
        out_specs=[whole] * (chunks + 3),
        out_shape=[jax.ShapeDtypeStruct((2 * part, width), jnp.bfloat16)] * chunks
        + [
            pltpu.VMEM((width, 2 * width), jnp.bfloat16),
            jax.ShapeDtypeStruct((width, shots), jnp.bfloat16),
            jax.ShapeDtypeStruct((2, width // 2, shots), jnp.bfloat16),
        ],
        scratch_shapes=[
            pltpu.VMEM((width, shots), jnp.bfloat16),
            pltpu.VMEM((1, width), jnp.float32),
            pltpu.SemaphoreType.DMA((5,)),
            pltpu.SemaphoreType.DMA((4, 2)),
            pltpu.SemaphoreType.DMA((groups,)),
        ],
        compiler_params=pltpu.CompilerParams(vmem_limit_bytes=LIMIT),
        cost_estimate=pl.CostEstimate(
            flops=4 * width * width * shots, bytes_accessed=4 * width * (width + 2 * shots), transcendentals=0
        ),
    )(level, mine, *pinned)


def second_kernel(part, joined_ref, right_ref, factor_ref, *outs):
    width = joined_ref.shape[0]
    wide = width // 2
    for n in range(2):
        columns = slice(n * wide, (n + 1) * wide)
        real, imag = joined_ref[columns, :width], joined_ref[columns, width:]
        start_panels(part, real, imag, right_ref[...], factor_ref[:, columns], outs, columns)


def second_advance(joined, right, factor, part):
    width, shots = right.shape
    outs = [jax.ShapeDtypeStruct((2 * part, width), jnp.bfloat16)] * (shots // 2 // part)
    joined = pltpu.with_memory_space_constraint(joined, pltpu.VMEM)
    return whole_call(functools.partial(second_kernel, part), (joined, right, factor), outs, 4 * width * width * shots)


def advance_kernel(level_ref, arrived_ref, ready_ref, joined_ref, factor_ref, out_ref, both):
    part = arrived_ref.shape[0] // 2
    width = arrived_ref.shape[1]

    @pl.when(level_ref[0] == 0)
    def _():
        out_ref[...] = ready_ref[...]

    @pl.when(level_ref[0] != 0)
    def _():
        both[:, :width] = arrived_ref[...]
        both[:part, width:] = -arrived_ref[part:]
        both[part:, width:] = arrived_ref[:part]
        out = lax.dot_general(
            joined_ref[...], both[...], (((1,), (1,)), ((), ())), preferred_element_type=jnp.float32
        )
        out_ref[...] = (out.T * factor_ref[...]).astype(jnp.bfloat16)


def advance(level, arrived, ready, joined, factor):
    rows, width = arrived.shape
    joined = pltpu.with_memory_space_constraint(joined, pltpu.VMEM)
    out = jax.ShapeDtypeStruct((rows, width), jnp.bfloat16)
    args = (arrived, ready, joined, factor)
    scratch = [pltpu.VMEM((rows, 2 * width), jnp.bfloat16)]
    return whole_call(advance_kernel, args, [out], 4 * rows * width * width, (level,), scratch)[0]


def stack_kernel(*refs):
    *panels, out_ref = refs
    rows = panels[0].shape[0]
    for at, panel in enumerate(panels):
        out_ref[at * rows : (at + 1) * rows] = panel[...]


def stacked(panels):
    rows, width = panels[0].shape
    out = jax.ShapeDtypeStruct((len(panels) * rows, width), panels[0].dtype)
    return whole_call(stack_kernel, panels, [out], 0)[0]


def operand_kernel(own_ref, got_ref, out_ref):
    rows, shots = own_ref.shape[1:]
    half = shots // STREAMS
    for which, ref in enumerate((own_ref, got_ref)):
        real, imag = ref[0], ref[1]
        minus = -real
        for stream in range(STREAMS):
            lanes = slice(stream * half, (stream + 1) * half)
            left = 2 * (which * shots + stream * half)
            out_ref[:rows, left : left + half] = real[:, lanes]
            out_ref[:rows, left + half : left + 2 * half] = imag[:, lanes]
            out_ref[rows:, left : left + half] = imag[:, lanes]
            out_ref[rows:, left + half : left + 2 * half] = minus[:, lanes]


def operand(mine, own, got, rows):
    shots = own.shape[2]
    blocks = got.shape[1] // rows
    groups = blocks // 2

    def spot(i, mine_ref, stride):
        group, place, core = places(mine_ref)
        other = lax.rem(lax.div(i, groups) + core, 2)
        block = stride * lax.rem(group + lax.rem(i, groups), groups) + other
        return block + 2 * place if stride == 4 else block

    return pl.pallas_call(
        lambda _, *refs: operand_kernel(*refs),
        grid_spec=pltpu.PrefetchScalarGridSpec(
            num_scalar_prefetch=1,
            grid=(blocks,),
            in_specs=[
                pl.BlockSpec((2, rows, shots), lambda i, mine_ref: (0, spot(i, mine_ref, 4), 0)),
                pl.BlockSpec((2, rows, shots), lambda i, mine_ref: (0, spot(i, mine_ref, 2), 0)),
            ],
            out_specs=pl.BlockSpec((2 * rows, 4 * shots), lambda i, mine_ref: (i, 0)),
        ),
        out_shape=jax.ShapeDtypeStruct((2 * rows * blocks, 4 * shots), jnp.bfloat16),
        compiler_params=pltpu.CompilerParams(vmem_limit_bytes=LIMIT),
        cost_estimate=pl.CostEstimate(flops=0, bytes_accessed=24 * rows * blocks * shots, transcendentals=0),
    )(mine, own, got)


def gather(levels, level_ref, panels, joined):
    part = joined.shape[0] // len(panels) // 2
    half = STEPS * part
    first = lax.rem(levels - 1 - level_ref[0], STEPS)
    for at, (ref, top) in enumerate(panels):
        base = at // STEPS * 2 * half
        row = pl.multiple_of(lax.rem(first + at, STEPS) * part, part)
        joined[pl.ds(base + row, part)] = ref[top : top + part]
        joined[pl.ds(base + half + row, part)] = ref[top + part : top + 2 * part]


def crossed(refs, counts, stream):
    rows = refs[0].shape[0] // counts[0]
    panels = [(ref, at * rows) for ref, count in zip(refs, counts) for at in range(count)]
    return panels[stream::STREAMS]


def early_kernel(levels, counts, level_ref, left_ref, *refs):
    *panels, out_ref, joined = refs
    own, other = panels[: STREAMS * STEPS], panels[STREAMS * STEPS :]
    gather(levels, level_ref, [(ref, 0) for ref in own] + crossed(other, counts, 0), joined)
    deep = joined.shape[0]
    wide = out_ref.shape[1] // 4
    for n in range(4):
        columns = slice(n * wide, (n + 1) * wide)
        out_ref[:, columns] = jnp.dot(left_ref[:, :deep], joined[:, columns], preferred_element_type=jnp.float32)


def late_kernel(levels, counts, level_ref, left_ref, early_ref, *refs):
    *panels, keep_ref, own_ref, send_ref, joined = refs
    gather(levels, level_ref, crossed(panels[:-1], counts[:-1], 1) + [(panels[-1], 0)], joined)
    start = left_ref.shape[1] - joined.shape[0]
    groups, _, rows, width = keep_ref.shape
    wide = width // 4
    for n in range(4):
        columns = slice(n * wide, (n + 1) * wide)
        out = early_ref[:, columns] + jnp.dot(
            left_ref[:, start:], joined[:, columns], preferred_element_type=jnp.float32
        )
        for k in range(groups):
            for part in range(2):
                lo = (2 * k + part) * rows
                keep_ref[k, part, :, columns] = out[lo : lo + rows]
                lo += 2 * groups * rows
                to_ref, at = (send_ref, k - 1) if k else (own_ref, 0)
                to_ref[at, part, :, columns] = out[lo : lo + rows].astype(jnp.bfloat16)


def whole_call(kernel, args, outs, flops, scalars=(), scratch=()):
    whole = pl.BlockSpec(memory_space=pltpu.VMEM)
    size = sum(math.prod(x.shape) * x.dtype.itemsize for x in (*args, *outs))
    return pl.pallas_call(
        kernel,
        in_specs=[pl.BlockSpec(memory_space=pltpu.SMEM)] * len(scalars) + [whole] * len(args),
        out_specs=[whole] * len(outs),
        out_shape=outs,
        scratch_shapes=scratch,
        compiler_params=pltpu.CompilerParams(vmem_limit_bytes=LIMIT),
        cost_estimate=pl.CostEstimate(flops=flops, bytes_accessed=size, transcendentals=0),
    )(*scalars, *args)


def early_terms(level, left, panels, levels, counts):
    width = panels[0].shape[1]
    deep = left.shape[1] - panels[-1].shape[0] * STEPS
    out = jax.ShapeDtypeStruct((left.shape[0], width), jnp.float32)
    kernel = functools.partial(early_kernel, levels, counts)
    scratch = [pltpu.VMEM((deep, width), jnp.bfloat16)]
    return whole_call(kernel, (left, *panels), [out], 2 * deep * left.shape[0] * width, (level,), scratch)[0]


def late_terms(level, left, early, panels, rows, levels, counts):
    width = early.shape[1]
    deep = panels[-1].shape[0] * STEPS
    groups = left.shape[0] // (4 * rows)
    outs = [jax.ShapeDtypeStruct((groups, 2, rows, width), jnp.float32)] + [
        jax.ShapeDtypeStruct((count, 2, rows, width), jnp.bfloat16) for count in (1, groups - 1)
    ]
    kernel = functools.partial(late_kernel, levels, counts)
    scratch = [pltpu.VMEM((deep, width), jnp.bfloat16)]
    return whole_call(kernel, (left, early, *panels), outs, 2 * deep * left.shape[0] * width, (level,), scratch)


def last_kernel(scale, *refs):
    *parts, out_ref, total, sems = refs
    pieces = sems.shape[0]
    tall = total.shape[0] // pieces
    copies = []
    for piece in range(pieces):
        rows = slice(piece * tall, (piece + 1) * tall)
        for part in range(2):
            out = parts[0][0, part, rows]
            for ref in parts[1:]:
                out += ref[0, part, rows].astype(jnp.float32)
            total[rows, part] = out * scale
        span = pl.ds(piece * tall, tall)
        copies.append(pltpu.make_async_copy(total.at[span], out_ref.at[0, span], sems.at[piece]))
        copies[-1].start()
    for copy in copies:
        copy.wait()


def last_sum(parts, scale):
    rows, width = parts[0].shape[2:]
    return pl.pallas_call(
        functools.partial(last_kernel, scale),
        in_specs=[pl.BlockSpec(memory_space=pltpu.VMEM)] * len(parts),
        out_specs=pl.BlockSpec(memory_space=pltpu.HBM),
        out_shape=jax.ShapeDtypeStruct((1, rows, 2, width), jnp.float32),
        scratch_shapes=[pltpu.VMEM((rows, 2, width), jnp.float32), pltpu.SemaphoreType.DMA((4,))],
        compiler_params=pltpu.CompilerParams(vmem_limit_bytes=LIMIT),
        cost_estimate=pl.CostEstimate(
            flops=2 * len(parts) * rows * width, bytes_accessed=16 * rows * width, transcendentals=0
        ),
    )(*parts)


def shards(source, propagator, transmission, upgoing):
    factor = transmission[0]
    upward = upgoing[0, 0]
    width = propagator.shape[3]
    shots = source.shape[3]
    levels = lax.axis_size("depth")
    freqs = lax.axis_size("freq")
    groups = freqs // 4
    rows = width // freqs
    part = shots // STREAMS // STEPS
    level, mine = (lax.axis_index(axis).astype(jnp.int32).reshape(1) for axis in ("depth", "freq"))
    *ready, joined, later, asked = first_advance(level, mine, source, propagator, transmission, upgoing, part, groups)
    ready = [ready, second_advance(joined, later, factor, part)]
    got = swapped(asked, "freq", 2)
    left = operand(mine, upward, got, rows)

    steps = STEPS + levels - 1
    flying = [None] * STREAMS
    own = [[] for _ in range(STREAMS)]
    waiting = []
    crossing = []
    for event in range(STREAMS * steps):
        step, stream = divmod(event, STREAMS)
        out = ready[stream][step % STEPS]
        if step >= 1:
            arrived = flying[stream]
            if event == steps:
                arrived, left = lax.optimization_barrier((arrived, left))
            for at, (sent, panel) in enumerate(crossing):
                if event == sent + BEHIND + (at == 0):
                    arrived, panel = lax.optimization_barrier((arrived, panel))
                    crossing[at] = (sent, panel)
            out = advance(level, arrived, out, joined, factor)
        if step + 1 < steps:
            flying[stream] = ring(out, "depth", 1)
        if step >= levels - 1:
            own[stream].append(out)
            if step == steps - 1:
                crossing.append((event, swapped(out, "freq", 2)))
            else:
                waiting.append(out)
                if len(waiting) == TOGETHER:
                    crossing.append((event, swapped(stacked(waiting), "freq", 2)))
                    waiting = []
    other = [panel for _, panel in crossing]
    counts = [panel.shape[0] // out.shape[0] for panel in other]
    early = early_terms(level, left, own[0] + own[1] + other[:-1], levels, counts[:-1])
    late = late_terms(level, left, early, other[:-2] + other[-1:], rows, levels, counts[:-2] + counts[-1:])
    keep, send_own, send = late
    near = swapped(send, "freq", 1)
    send_own, near = lax.optimization_barrier((send_own, near))
    parts = [keep, swapped(send_own, "freq", 1)]
    for k in range(1, groups):
        total = (keep[k : k + 1] + near[k - 1 : k].astype(jnp.float32)).astype(jnp.bfloat16)
        parts.append(ring(total, "freq", 4 * k))
    return last_sum(parts, (2.0 * shots * freqs) ** (-0.5))


def solution(mesh):
    return jax.shard_map(
        shards,
        mesh=mesh,
        in_specs=(
            P("freq", None, None, None),
            P("depth", "freq", None, None, None),
            P("depth", "freq", None),
            P("depth", "freq", None, None, None),
        ),
        out_specs=P("depth", "freq", None, None),
        check_vma=False,
    )
```
